32 devices in a mesh: blk: 8 (over z, y), dp: 2 (over core), head: 2 (over x).
Axes of the slice: x: 2, y: 2, z: 4, core: 2. Of those that a mesh axis runs over, the one named last changes fastest.
Arguments:
- tokens: bfloat16 [4, 4096, 1024], P('dp', 'blk'), may hold values from -6 to 6
- doc_ids: int32 [4, 4096], P('dp'), may hold values from 0 to 6, as said below
- w_qkv: bfloat16 [3, 1024, 1024], P(None, None, 'head'), may hold values from -0.1875 to 0.1875
- w_out: bfloat16 [1024, 1024], P('head'), may hold values from -0.75 to 0.75
- slopes: float32 [8], P('head'), may hold values from 0.02 to 1
- w_up: bfloat16 [1024, 4096], P(None, 'head'), may hold values from -0.1875 to 0.1875
- w_down: bfloat16 [4096, 1024], P('head'), may hold values from -0.09375 to 0.09375
- w_comp: bfloat16 [3, 1024, 1024], replicated, may hold values from -0.109375 to 0.109375
- comp_bias: float32 [1024], replicated, may hold values from -1.5 to 1.5
- norm1_gain: float32 [1024], replicated, may hold values from 0.5 to 1.5
- norm1_bias: float32 [1024], replicated, may hold values from -1 to 1
- norm2_gain: float32 [1024], replicated, may hold values from 0.5 to 1.5
- norm2_bias: float32 [1024], replicated, may hold values from -1 to 1
- out_cot: bfloat16 [4, 4096, 1024], P('dp', 'blk'), may hold values from -6 to 6
- recon_cot: float32 [4, 8, 4096], P('dp', 'head', 'blk'), may hold values from -6 to 6
Outputs:
- layer_out: bfloat16 [4, 4096, 1024], P('dp', 'blk')
- recon: float32 [4, 8, 4096], P('dp', 'head', 'blk')
- grad_tokens: bfloat16 [4, 4096, 1024], P('dp', 'blk')
- grad_qkv: float32 [3, 1024, 1024], P(None, ('blk', 'dp'), 'head')
- grad_out: float32 [1024, 1024], P('head', ('blk', 'dp'))
- grad_slopes: float32 [8], P('head')
- grad_up: float32 [1024, 4096], P(('blk', 'dp'), 'head')
- grad_down: float32 [4096, 1024], P('head', ('blk', 'dp'))
- grad_comp: float32 [3, 1024, 1024], P(None, ('blk', 'dp'))
- grad_comp_bias: float32 [1024], replicated
- grad_norm1_gain: float32 [1024], replicated
- grad_norm1_bias: float32 [1024], replicated
- grad_norm2_gain: float32 [1024], replicated
- grad_norm2_bias: float32 [1024], replicated
The draws below stay inside these ranges and needn't reach their ends.
Inputs may be any that keep to these rules, and one draw needn't show every extreme that they name: `doc_ids`: ids never fall along a sequence and start at 0. In every draw, among the 2 sequences of each index of dp, one chosen by the seed is a single document; each of the others holds exactly 7 documents.
All inputs are finite; a program needn't handle non-finite values.
Results may differ from the reference program's by a relative error of at most 0.015.
Values may be sent and summed in bfloat16 or wider, within the bound.
No kernel may reach another device: no remote copies, remote signals or barrier semaphores. Data moves between devices by JAX's collectives and lax.ppermute only.
A program may use at most 256 MiB of HBM per device.

```python
import math
import jax
import jax.numpy as jnp
from jax import lax

D = 1024
HEADS = 8
HD = 128
FF = 4096
SEG = 512
CSEGS = 3
SEQ_DEV = 2
LEN = 4096
SEQS = 4


def draw_doc_ids(key, part):
    key = jax.random.fold_in(key, 7)
    pick_key, flag_key = jax.random.split(key)
    single = jax.random.randint(pick_key, (SEQS // SEQ_DEV,), 0, SEQ_DEV)
    row_ids = jnp.arange(SEQS, dtype=jnp.int32)
    whole_row = row_ids % SEQ_DEV == single[row_ids // SEQ_DEV]
    row_keys = jax.random.split(flag_key, SEQS)
    orders = jax.vmap(lambda row_key: jax.random.permutation(row_key, LEN - 1))(row_keys).astype(jnp.int32) + 1
    chosen = orders[:, :6]
    columns = jnp.arange(LEN, dtype=jnp.int32)
    flags = jnp.any(columns[None, None, :] == chosen[:, :, None], axis=1)
    flags = flags & jnp.logical_not(whole_row[:, None])
    return jnp.cumsum(flags.astype(jnp.int32), axis=1).astype(jnp.int32)


def shard_levels(stream_key, dims, cuts, smallest, largest):
    factor_of = 1.0
    for position, parts in cuts:
        heights = jax.random.uniform(jax.random.fold_in(jax.random.fold_in(stream_key, 6), position), (parts,), jnp.float32, smallest / len(cuts), largest / len(cuts))
        factor_of = factor_of * jnp.repeat(jnp.exp(heights), dims[position] // parts).reshape((-1,) + (1,) * (len(dims) - 1 - position))
    return factor_of


def noise(rng, dims, scale, reach, cuts=(), kind=jnp.bfloat16):
    values = jax.random.normal(rng, dims, jnp.float32) * scale
    if len(cuts) > 0:
        values = shard_levels(rng, dims, cuts, -0.22, 0.18) * values
    return jnp.clip(values, min=-reach, max=reach).astype(kind)


def setup_inputs(seed: int = 0) -> dict:
    keys = jax.random.split(jax.random.key(seed), 16)
    tokens = noise(keys[0], (SEQS, LEN, D), 1.0, 6.0, ((0, 2), (1, 8)))
    doc_ids = draw_doc_ids(jax.random.fold_in(keys[15], 71), 0)
    w_qkv = noise(keys[2], (3, D, D), D ** -0.5, 0.1875, ((2, 2),))
    w_out = noise(keys[3], (D, D), (D // 16) ** -0.5, 0.75, ((0, 2),))
    slopes = jnp.clip(jnp.exp(math.log(1.0) - 3.912023 * jax.random.uniform(keys[4], (HEADS,), jnp.float32) ** shard_levels(keys[4], (HEADS,), ((0, 2),), -0.2, 0.2)), 0.02, 1.0)
    w_up = noise(keys[5], (D, FF), D ** -0.5, 0.1875, ((1, 2),))
    w_down = noise(keys[6], (FF, D), FF ** -0.5, 0.09375, ((0, 2),))
    w_comp = noise(keys[7], (3, D, D), (3 * D) ** -0.5, 0.109375)
    comp_bias = noise(keys[8], (D,), 0.3, 1.5, (), jnp.float32)
    norm1_gain = jnp.clip(1.0 + 0.1 * jax.random.normal(keys[9], (D,), jnp.float32), 0.5, 1.5)
    norm1_bias = noise(keys[10], (D,), 0.2, 1.0, (), jnp.float32)
    norm2_gain = jnp.clip(1.0 + 0.1 * jax.random.normal(keys[11], (D,), jnp.float32), 0.5, 1.5)
    norm2_bias = noise(keys[12], (D,), 0.2, 1.0, (), jnp.float32)
    out_cot = noise(keys[13], (SEQS, LEN, D), 1.0, 6.0, ((0, 2), (1, 8)))
    recon_cot = noise(keys[14], (SEQS, HEADS, LEN), 1.0, 6.0, ((0, 2), (1, 2), (2, 8)), jnp.float32)
    return dict(tokens=tokens, doc_ids=doc_ids, w_qkv=w_qkv, w_out=w_out, slopes=slopes, w_up=w_up, w_down=w_down, w_comp=w_comp, comp_bias=comp_bias, norm1_gain=norm1_gain, norm1_bias=norm1_bias, norm2_gain=norm2_gain, norm2_bias=norm2_bias, out_cot=out_cot, recon_cot=recon_cot)


NEG = -1e+30
EPS = 1e-05
HIGH = lax.Precision.HIGHEST

@jax.custom_vjp
def low(v):
    return lax.optimization_barrier(v.astype(jnp.bfloat16)).astype(jnp.float32)

@jax.custom_vjp
def low_back(v):
    return v

def low_keep(v):
    return (low(v), None)

def low_pass(kept, grad):
    return (grad,)

def back_keep(v):
    return (v, None)

def back_low(kept, grad):
    return (low(grad),)
low.defvjp(low_keep, low_pass)
low_back.defvjp(back_keep, back_low)

def low_both(value):
    return low_back(low(value))

def norm_rows(inputs, gain, bias):
    center = inputs - lax.optimization_barrier(jnp.mean(inputs, axis=-1, keepdims=True))
    inverse = lax.rsqrt(lax.optimization_barrier(jnp.mean(center * center, axis=-1, keepdims=True)) + EPS)
    return center * inverse * gain + bias

def high_dot(left, right):
    return jnp.dot(left, right, precision=HIGH, preferred_element_type=jnp.float32)

def self_attend(queries, key_part, value_part, scaling):
    scores = low_back(jnp.einsum('qhe,khe->hqk', queries, key_part, precision=HIGH) * scaling)
    weights = jax.nn.softmax(scores, axis=-1)
    return low_back(jnp.einsum('hqk,khe->hqe', low(weights), value_part, precision=HIGH))

def block_layer(inputs, w_qkv, w_out, slopes, w_up, w_down, w_comp, comp_bias, gain_one, bias_one, gain_two, bias_two, doc_row):
    length = inputs.shape[0]
    seg_count = length // SEG
    per_segment = SEG // 3
    slot_count = seg_count * per_segment
    memory_slots = CSEGS * per_segment
    pad_slots = (CSEGS + 1) * per_segment
    scaling = HD ** (-0.5)
    normed = low(norm_rows(inputs, gain_one, bias_one))
    queries = low_both(high_dot(normed, w_qkv[0])).reshape(length, HEADS, HD)
    keys_all = low_both(high_dot(normed, w_qkv[1])).reshape(length, HEADS, HD)
    values_all = low_both(high_dot(normed, w_qkv[2])).reshape(length, HEADS, HD)
    triples = normed.reshape(seg_count, SEG, D)[:, :3 * per_segment].reshape(slot_count, 3, D)
    packed = low_both(jnp.einsum('srd,rde->se', triples, w_comp, precision=HIGH) + comp_bias)
    slot_keys = low_both(high_dot(packed, w_qkv[1])).reshape(slot_count, HEADS, HD)
    slot_values = low_both(high_dot(packed, w_qkv[2])).reshape(slot_count, HEADS, HD)
    zero_rows = jnp.zeros((SEG, HEADS, HD), jnp.float32)
    key_pad = jnp.concatenate([zero_rows, keys_all], 0)
    value_pad = jnp.concatenate([zero_rows, values_all], 0)
    doc_pad = jnp.concatenate([jnp.full((SEG,), -1, jnp.int32), doc_row], 0)
    zero_slots = jnp.zeros((pad_slots, HEADS, HD), jnp.float32)
    slot_key_pad = jnp.concatenate([zero_slots, slot_keys], 0)
    slot_value_pad = jnp.concatenate([zero_slots, slot_values], 0)
    slot_doc = doc_row.reshape(seg_count, SEG)[:, 0:3 * per_segment:3].reshape(slot_count)
    slot_doc_pad = jnp.concatenate([jnp.full((pad_slots,), -1, jnp.int32), slot_doc], 0)
    slot_local = jnp.arange(memory_slots, dtype=jnp.int32)

    def segment_pass(segment_id):
        first_row = segment_id * SEG
        seg_queries = lax.dynamic_slice_in_dim(queries, first_row, SEG, 0)
        near_keys = lax.dynamic_slice_in_dim(key_pad, first_row, 2 * SEG, 0)
        near_values = lax.dynamic_slice_in_dim(value_pad, first_row, 2 * SEG, 0)
        query_doc = lax.dynamic_slice_in_dim(doc_row, first_row, SEG, 0)
        near_doc = lax.dynamic_slice_in_dim(doc_pad, first_row, 2 * SEG, 0)
        query_pos = first_row + jnp.arange(SEG, dtype=jnp.int32)
        near_pos = first_row - SEG + jnp.arange(2 * SEG, dtype=jnp.int32)
        near_mask = (near_pos[None, :] >= 0) & (near_pos[None, :] <= query_pos[:, None]) & (near_doc[None, :] == query_doc[:, None])
        near_dist = jnp.log1p(jnp.maximum(query_pos[:, None] - near_pos[None, :], 0).astype(jnp.float32))
        slot_start = segment_id * per_segment
        mem_keys = lax.dynamic_slice_in_dim(slot_key_pad, slot_start, memory_slots, 0)
        mem_values = lax.dynamic_slice_in_dim(slot_value_pad, slot_start, memory_slots, 0)
        mem_doc = lax.dynamic_slice_in_dim(slot_doc_pad, slot_start, memory_slots, 0)
        mem_seg = segment_id - 1 - CSEGS + slot_local // per_segment
        mem_pos = mem_seg * SEG + 3 * (slot_local % per_segment) + 1
        slot_mask = (mem_seg[None, :] >= 0) & (mem_doc[None, :] == query_doc[:, None])
        slot_dist = jnp.log1p(jnp.maximum(query_pos[:, None] - mem_pos[None, :], 0).astype(jnp.float32))
        near_score = low_back(jnp.einsum('qhe,khe->hqk', seg_queries, near_keys, precision=HIGH) * scaling) - slopes[:, None, None] * near_dist[None]
        slot_score = low_back(jnp.einsum('qhe,khe->hqk', seg_queries, mem_keys, precision=HIGH) * scaling) - slopes[:, None, None] * slot_dist[None]
        near_score = jnp.where(near_mask[None], near_score, NEG)
        slot_score = jnp.where(slot_mask[None], slot_score, NEG)
        highest = jnp.maximum(lax.optimization_barrier(jnp.max(near_score, axis=-1)), lax.optimization_barrier(jnp.max(slot_score, axis=-1)))
        near_w = jnp.where(near_mask[None], jnp.exp(near_score - highest[..., None]), 0.0)
        slot_w = jnp.where(slot_mask[None], jnp.exp(slot_score - highest[..., None]), 0.0)
        row_total = lax.optimization_barrier(jnp.sum(near_w, axis=-1)) + lax.optimization_barrier(jnp.sum(slot_w, axis=-1))
        near_p = low(near_w / row_total[..., None])
        slot_p = low(slot_w / row_total[..., None])
        mixed = jnp.einsum('hqk,khe->qhe', near_p, near_values, precision=HIGH) + jnp.einsum('hqk,khe->qhe', slot_p, mem_values, precision=HIGH)
        own_keys = lax.dynamic_slice_in_dim(keys_all, first_row, SEG, 0)
        own_values = lax.dynamic_slice_in_dim(values_all, first_row, SEG, 0)
        own_slot_keys = lax.dynamic_slice_in_dim(slot_keys, slot_start, per_segment, 0)
        own_slot_values = lax.dynamic_slice_in_dim(slot_values, slot_start, per_segment, 0)
        full = self_attend(seg_queries, own_keys, own_values, scaling)
        comp = self_attend(seg_queries, own_slot_keys, own_slot_values, scaling)
        spread = full - comp
        errors = lax.optimization_barrier(jnp.sum(spread * spread, axis=-1)) / jnp.sqrt(jnp.float32(HD))
        return (mixed, errors)
    mixed_all, error_blocks = lax.map(jax.checkpoint(segment_pass), jnp.arange(seg_count, dtype=jnp.int32))
    errors_all = jnp.transpose(error_blocks, (1, 0, 2)).reshape(HEADS, length)
    attended = low_both(mixed_all.reshape(length, D))
    branch = low_back(high_dot(attended, w_out))
    middle = inputs + branch
    normed_two = low(norm_rows(middle, gain_two, bias_two))
    inner = low_back(high_dot(normed_two, w_up))
    hidden = low(jax.nn.gelu(inner))
    branch_two = low_back(high_dot(hidden, w_down))
    return (middle + branch_two, errors_all)

def reference(tokens, doc_ids, w_qkv, w_out, slopes, w_up, w_down, w_comp, comp_bias, norm1_gain, norm1_bias, norm2_gain, norm2_bias, out_cot, recon_cot):
    weights = tuple((element.astype(jnp.float32) for element in (w_qkv, w_out, slopes, w_up, w_down, w_comp, comp_bias, norm1_gain, norm1_bias, norm2_gain, norm2_bias)))

    def per_sequence(totals, sequence):
        seq_tokens, seq_doc, seq_cot, seq_recon = sequence

        def forward_fn(inputs, *params):
            return block_layer(inputs, *params, seq_doc)
        results, pullback = jax.vjp(forward_fn, seq_tokens.astype(jnp.float32), *weights)
        gradients = pullback((seq_cot.astype(jnp.float32), seq_recon.astype(jnp.float32)))
        totals = tuple((running_sum + gradient for running_sum, gradient in zip(totals, gradients[1:])))
        return (totals, (results[0].astype(jnp.bfloat16), results[1], gradients[0].astype(jnp.bfloat16)))
    start_totals = tuple((jnp.zeros_like(element) for element in weights))
    totals, (layer_out, recon, grad_tokens) = lax.scan(per_sequence, start_totals, (tokens, doc_ids, out_cot, recon_cot))
    return (layer_out, recon, grad_tokens, totals[0], totals[1], totals[2], totals[3], totals[4], totals[5], totals[6], totals[7], totals[8], totals[9], totals[10])
```

```python
import functools
import math

import jax
import jax.numpy as jnp
from jax import lax
from jax.experimental import pallas as pl
from jax.experimental.pallas import tpu as pltpu
from jax.sharding import PartitionSpec as P

CSEGS = 3
EPS = 1e-05
FAR = 1e30
LOG2E = math.log2(math.e)
BF = jnp.bfloat16
F32 = jnp.float32
TILE = 256
NT = (((1,), (1,)), ((), ()))
GELU_A = math.sqrt(2.0 / math.pi)
GELU_B = 0.044715


def dot(a, b):
    return jnp.dot(a, b, preferred_element_type=F32)


def dot_nt(a, b):
    return lax.dot_general(a, b, NT, preferred_element_type=F32)


def dot_tn(a, b):
    return lax.dot_general(a, b, (((0,), (0,)), ((), ())), preferred_element_type=F32)


def shift(x, axis, by):
    devices = lax.axis_size(axis)
    pairs = [(i, i + by) for i in range(devices) if 0 <= i + by < devices]
    return lax.ppermute(x, axis, pairs)


def swap(x, axis, step=1):
    devices = lax.axis_size(axis)
    return lax.ppermute(x, axis, [(i, i ^ step) for i in range(devices)])


def row_stats(x):
    center = x - jnp.mean(x, axis=-1, keepdims=True)
    inverse = lax.rsqrt(jnp.mean(center * center, axis=-1, keepdims=True) + EPS)
    return center * inverse, inverse


def norm_back(grad, unit, inverse, gain):
    scaled = grad * gain
    mean_one = jnp.mean(scaled, axis=-1, keepdims=True)
    mean_two = jnp.mean(scaled * unit, axis=-1, keepdims=True)
    return inverse * (scaled - mean_one - unit * mean_two)


def forward_kernel(slopes, q, kp, ko, km, vp, vo, vm, far, out, lse, *, rows, scaling):
    head = pl.program_id(0)
    c1 = scaling * LOG2E
    c2 = slopes[head] * LOG2E
    tiles = rows // TILE
    sources = ((kp, vp, 0), (ko, vo, rows), (km, vm, 2 * rows))
    for qi in range(tiles):
        qs = slice(qi * TILE, (qi + 1) * TILE)
        qb = q[0, qs, :]
        scores = []
        for which, (k, v, base) in enumerate(sources):
            for ki in range(tiles):
                if which == 1 and ki > qi:
                    continue
                ks = slice(ki * TILE, (ki + 1) * TILE)
                s = dot_nt(k[0, 0, ks, :], qb) * c1
                s = s - c2 * far[0, base + ki * TILE : base + (ki + 1) * TILE, qs]
                scores.append((s, v, ks))
        top = functools.reduce(
            jnp.maximum, [jnp.max(s, axis=0, keepdims=True) for s, _, _ in scores]
        )
        total = jnp.zeros((1, TILE), F32)
        mixed = jnp.zeros((q.shape[2], TILE), F32)
        for s, v, ks in scores:
            p = jnp.exp2(s - top)
            total = total + jnp.sum(p, axis=0, keepdims=True)
            mixed = mixed + dot(v[0, 0, ks, :].T, p.astype(BF))
        out[0, qs, :] = (mixed / total).T.astype(BF)
        lse[0, :, qs] = top + jnp.log2(total)


def attend_forward(s, slopes, q, kv_prev, kv_own, kv_mem, far, scaling):
    rows, width = q.shape[1], q.shape[2]
    heads = slopes.shape[0]
    hd = width // heads
    part = lambda i: pl.BlockSpec((1, 1, rows, hd), lambda h: (i, s, 0, h))
    return pl.pallas_call(
        functools.partial(forward_kernel, rows=rows, scaling=scaling),
        grid=(heads,),
        in_specs=[
            pl.BlockSpec(memory_space=pltpu.SMEM),
            pl.BlockSpec((1, rows, hd), lambda h: (s, 0, h)),
            part(0), part(0), part(0), part(1), part(1), part(1),
            pl.BlockSpec((1, 3 * rows, rows), lambda h: (s, 0, 0)),
        ],
        out_specs=[
            pl.BlockSpec((1, rows, hd), lambda h: (0, 0, h)),
            pl.BlockSpec((1, 1, rows), lambda h: (h, 0, 0)),
        ],
        out_shape=[
            jax.ShapeDtypeStruct((1, rows, width), BF),
            jax.ShapeDtypeStruct((heads, 1, rows), F32),
        ],
        compiler_params=pltpu.CompilerParams(vmem_limit_bytes=40 << 20),
        cost_estimate=pl.CostEstimate(
            flops=4 * heads * rows * rows * 3 * hd, bytes_accessed=8 << 20,
            transcendentals=3 * heads * rows * rows),
        name="attend_forward",
    )(slopes, q, kv_prev, kv_own, kv_mem, kv_prev, kv_own, kv_mem, far)


def backward_kernel(
    slopes, q, do, lse, dot_row, far, *refs, rows, scaling, parts, own, extra
):
    head = pl.program_id(0)
    c1 = scaling * LOG2E
    c2 = slopes[head] * LOG2E
    tiles = rows // TILE
    kv = refs[: 2 * parts]
    extras = refs[2 * parts : 2 * parts + extra]
    dq, dkv, dslope = refs[2 * parts + extra], refs[2 * parts + extra + 1 : -1], refs[-1]
    hd = q.shape[2]
    dqs = [jnp.zeros((hd, TILE), F32) for _ in range(tiles)]
    zero = jnp.zeros((8, TILE), F32)
    sums = [[zero, zero, zero] for _ in range(tiles)]
    for part in range(parts):
        k, v = kv[2 * part], kv[2 * part + 1]
        for ki in range(tiles):
            ks = slice(ki * TILE, (ki + 1) * TILE)
            kb, vb = k[0, 0, ks, :], v[0, 0, ks, :]
            kt = kb.T
            dk = jnp.zeros((TILE, hd), F32)
            dv = jnp.zeros((TILE, hd), F32)
            for qi in range(tiles):
                if own and ki > qi:
                    continue
                qs = slice(qi * TILE, (qi + 1) * TILE)
                qb, db = q[0, qs, :], do[0, qs, :]
                base = part * rows + ki * TILE
                dist = far[0, base : base + TILE, qs]
                s = dot_nt(kb, qb) * c1 - c2 * dist
                p = jnp.exp2(s - lse[0, :, qs])
                dp = dot_nt(vb, db)
                weighted = p * dp
                away = p * dist
                ds = weighted - p * dot_row[0, :, qs]
                for index, value in enumerate((weighted, away, away * dp)):
                    value = jnp.sum(value.reshape(TILE // 8, 8, TILE), axis=0)
                    sums[qi][index] = sums[qi][index] + value
                p = p.astype(BF)
                ds = ds.astype(BF)
                dv = dv + dot(p, db)
                dk = dk + dot(ds, qb)
                dqs[qi] = dqs[qi] + dot(kt, ds)
            dk = dk * scaling
            if own:
                dk = dk + extras[2][0, ks, :]
                dv = dv + extras[3][0, ks, :]
            dkv[part][0, ks, :] = dk.astype(dkv[part].dtype)
            dkv[part][1, ks, :] = dv.astype(dkv[part].dtype)
    for qi in range(tiles):
        qs = slice(qi * TILE, (qi + 1) * TILE)
        value = dqs[qi].T * scaling
        if own:
            value = value + extras[0][0, qs, :] + extras[1][0, qs, :]
        dq[0, qs, :] = value.astype(dq.dtype)
        for index in range(3):
            rows_sum = jnp.sum(sums[qi][index], axis=0, keepdims=True)
            dslope[0, index : index + 1, qs] = rows_sum


def attend_backward(s, slopes, q, do, lse, dot_row, far, kvs, own, extras, scaling):
    rows, width = q.shape[1], q.shape[2]
    heads = slopes.shape[0]
    hd = width // heads
    parts = len(kvs)
    part = lambda i: pl.BlockSpec((1, 1, rows, hd), lambda h: (i, s, 0, h))
    plain = pl.BlockSpec((1, rows, hd), lambda h: (0, 0, h))
    lane = pl.BlockSpec((1, 1, rows), lambda h: (h, 0, 0))
    dtype = F32 if own else BF
    operands = [slopes, q, do, lse, dot_row, far]
    specs = [
        pl.BlockSpec(memory_space=pltpu.SMEM),
        pl.BlockSpec((1, rows, hd), lambda h: (s, 0, h)),
        plain, lane, lane,
        pl.BlockSpec((1, parts * rows, rows), lambda h: (s, 0, 0)),
    ]
    for kv in kvs:
        operands += [kv, kv]
        specs += [part(0), part(1)]
    operands += extras
    specs += [plain] * len(extras)
    pair = pl.BlockSpec((2, rows, hd), lambda h: (0, 0, h))
    return pl.pallas_call(
        functools.partial(
            backward_kernel, rows=rows, scaling=scaling, parts=parts, own=own, extra=len(extras)
        ),
        grid=(heads,),
        in_specs=specs,
        out_specs=[plain] + [pair] * parts + [pl.BlockSpec((1, 8, rows), lambda h: (h, 0, 0))],
        out_shape=[jax.ShapeDtypeStruct((1, rows, width), BF if own else F32)]
        + [jax.ShapeDtypeStruct((2, rows, width), dtype)] * parts
        + [jax.ShapeDtypeStruct((heads, 8, rows), F32)],
        compiler_params=pltpu.CompilerParams(vmem_limit_bytes=48 << 20),
        cost_estimate=pl.CostEstimate(
            flops=10 * heads * rows * rows * parts * hd, bytes_accessed=8 << 20,
            transcendentals=parts * heads * rows * rows),
        name="attend_backward_own" if own else "attend_backward_far",
    )(*operands)


def recon_kernel(
    q, ko, vo, kc, vc, cot, recon, dq, dk, dv, dkc, dvc, *, rows, slots, scaling
):
    hd = q.shape[2]
    c1 = scaling * LOG2E
    tiles = rows // TILE
    comp_rows = kc.shape[2]
    dkt = [jnp.zeros((TILE, hd), F32) for _ in range(tiles)]
    dvt = [jnp.zeros((TILE, hd), F32) for _ in range(tiles)]
    dkct = jnp.zeros((comp_rows, hd), F32)
    dvct = jnp.zeros((comp_rows, hd), F32)
    live = lax.broadcasted_iota(jnp.int32, (comp_rows, TILE), 0) < slots
    kct, vct = kc[0, 0].T, vc[0, 0].T
    for qi in range(tiles):
        qs = slice(qi * TILE, (qi + 1) * TILE)
        qb = q[0, qs, :]
        full_s = [dot_nt(ko[0, 0, ki * TILE : (ki + 1) * TILE, :], qb) * c1 for ki in range(tiles)]
        top = functools.reduce(
            jnp.maximum, [jnp.max(s, axis=0, keepdims=True) for s in full_s]
        )
        full_p = [jnp.exp2(s - top) for s in full_s]
        total = functools.reduce(jnp.add, [jnp.sum(p, axis=0, keepdims=True) for p in full_p])
        inverse = 1.0 / total
        full_p = [p * inverse for p in full_p]
        full_low = [p.astype(BF) for p in full_p]
        full = functools.reduce(
            jnp.add,
            [dot(vo[0, 0, ki * TILE : (ki + 1) * TILE, :].T, full_low[ki]) for ki in range(tiles)],
        )
        comp_s = jnp.where(live, dot_nt(kc[0, 0], qb) * c1, -FAR)
        comp_p = jnp.exp2(comp_s - jnp.max(comp_s, axis=0, keepdims=True))
        comp_p = comp_p * (1.0 / jnp.sum(comp_p, axis=0, keepdims=True))
        comp_low = comp_p.astype(BF)
        comp = dot(vct, comp_low)
        spread = full - comp
        recon[0, :, qs] = jnp.sum(spread * spread, axis=0, keepdims=True) / hd**0.5
        dfull = spread * (cot[0, :, qs] * (2.0 / hd**0.5))
        dfull_low = dfull.astype(BF)
        dcomp_low = (-dfull).astype(BF)
        dqt = jnp.zeros((hd, TILE), F32)
        dws = [dot(vo[0, 0, ki * TILE : (ki + 1) * TILE, :], dfull_low) for ki in range(tiles)]
        row = functools.reduce(
            jnp.add, [jnp.sum(p * d, axis=0, keepdims=True) for p, d in zip(full_p, dws)]
        )
        for ki in range(tiles):
            ds = (full_p[ki] * (dws[ki] - row)).astype(BF)
            dkt[ki] = dkt[ki] + dot(ds, qb)
            dvt[ki] = dvt[ki] + dot_nt(full_low[ki], dfull_low)
            dqt = dqt + dot(ko[0, 0, ki * TILE : (ki + 1) * TILE, :].T, ds)
        dw = dot(vc[0, 0], dcomp_low)
        row = jnp.sum(comp_p * dw, axis=0, keepdims=True)
        ds = (comp_p * (dw - row)).astype(BF)
        dkct = dkct + dot(ds, qb)
        dvct = dvct + dot_nt(comp_low, dcomp_low)
        dqt = dqt + dot(kct, ds)
        dq[0, qs, :] = dqt.T * scaling
    for ki in range(tiles):
        dk[0, ki * TILE : (ki + 1) * TILE, :] = dkt[ki] * scaling
        dv[0, ki * TILE : (ki + 1) * TILE, :] = dvt[ki]
    dkc[0] = dkct * scaling
    dvc[0] = dvct


def recon_both(s, q, kv_own, kv_slot, cot, slots, heads, scaling):
    rows, width = q.shape[1], q.shape[2]
    hd = width // heads
    comp_rows = kv_slot.shape[2]
    part = lambda i: pl.BlockSpec((1, 1, rows, hd), lambda h: (i, s, 0, h))
    slot = lambda i: pl.BlockSpec((1, 1, comp_rows, hd), lambda h: (i, s, 0, h))
    plain = pl.BlockSpec((1, rows, hd), lambda h: (0, 0, h))
    small = pl.BlockSpec((1, comp_rows, hd), lambda h: (0, 0, h))
    lane = pl.BlockSpec((1, 1, rows), lambda h: (h, 0, 0))
    big = jax.ShapeDtypeStruct((1, rows, width), F32)
    little = jax.ShapeDtypeStruct((1, comp_rows, width), F32)
    return pl.pallas_call(
        functools.partial(recon_kernel, rows=rows, slots=slots, scaling=scaling),
        grid=(heads,),
        in_specs=[
            pl.BlockSpec((1, rows, hd), lambda h: (s, 0, h)),
            part(0), part(1), slot(0), slot(1),
            pl.BlockSpec((1, 1, rows), lambda h: (s * heads + h, 0, 0)),
        ],
        out_specs=[lane, plain, plain, plain, small, small],
        out_shape=[jax.ShapeDtypeStruct((heads, 1, rows), F32), big, big, big, little, little],
        compiler_params=pltpu.CompilerParams(vmem_limit_bytes=40 << 20),
        cost_estimate=pl.CostEstimate(
            flops=12 * heads * rows * (rows + comp_rows) * hd, bytes_accessed=8 << 20,
            transcendentals=heads * rows * (rows + comp_rows)),
        name="recon_both",
    )(q, kv_own, kv_own, kv_slot, kv_slot, cot)


def reduce_rows(part, dp_index):
    blocks, cores = lax.axis_size("blk"), lax.axis_size("dp")
    rows = part.shape[0] // (blocks * cores)
    split = part.astype(BF).reshape(blocks, cores, rows, part.shape[1])
    away = lax.dynamic_index_in_dim(split, 1 - dp_index, 1, keepdims=False)
    here = lax.dynamic_index_in_dim(split, dp_index, 1, keepdims=False)
    total = here + swap(away, "dp")
    total = total.reshape(blocks * rows, part.shape[1])
    return lax.psum_scatter(total, "blk", scatter_dimension=0, tiled=True).astype(F32)


def butterfly(x):
    x = x + swap(x, "dp")
    step = 1
    while step < lax.axis_size("blk"):
        x = x + swap(x, "blk", step)
        step *= 2
    return x


def shards(
    tokens, doc_ids, w_qkv, w_out, slopes, w_up, w_down, w_comp, comp_bias,
    norm1_gain, norm1_bias, norm2_gain, norm2_bias, out_cot, recon_cot,
):
    seqs, rows, model = tokens.shape
    heads = slopes.shape[0]
    width = w_qkv.shape[2]
    hd = width // heads
    slots = rows // 3
    used = 3 * slots
    slot_pad = -(-slots // 16) * 16
    position = lax.axis_index("blk")
    dp_index = lax.axis_index("dp")
    head_index = lax.axis_index("head")
    scaling = hd ** (-0.5)
    memory = CSEGS * slots
    half = model // lax.axis_size("head")

    w_out_other = swap(w_out, "head")

    inputs = tokens.astype(F32)
    unit1, inverse1 = row_stats(inputs)
    normed = (unit1 * norm1_gain + norm1_bias).astype(BF)
    kv_own = jnp.einsum("sgd,tde->tsge", normed, w_qkv[1:], preferred_element_type=F32).astype(BF)
    kv_prev = shift(kv_own, "blk", 1)
    triples = normed[:, :used].reshape(seqs, slots, 3, model)
    packed = jnp.einsum("scrd,rde->sce", triples, w_comp, preferred_element_type=F32) + comp_bias
    packed = packed.astype(BF)
    kv_slot = jnp.einsum("scd,tde->tsce", packed, w_qkv[1:], preferred_element_type=F32).astype(BF)
    kv_mem = jnp.concatenate(
        [shift(kv_slot, "blk", lag) for lag in range(CSEGS + 1, 1, -1)]
        + [jnp.zeros((2, seqs, rows - memory, width), BF)],
        2,
    )
    kv_slot_pad = jnp.pad(kv_slot, ((0, 0), (0, 0), (0, slot_pad - slots), (0, 0)))
    q = jnp.einsum("sgd,de->sge", normed, w_qkv[0], preferred_element_type=F32).astype(BF)

    local = jnp.arange(rows, dtype=jnp.int32)
    query_pos = position * rows + local
    mem_seg = position - 1 - CSEGS + local // slots
    mem_pos = mem_seg * rows + 3 * (local % slots) + 1
    key_pos = jnp.concatenate([query_pos - rows, query_pos, mem_pos])
    key_live = jnp.concatenate(
        [query_pos - rows >= 0, query_pos >= 0, (mem_seg >= 0) & (local < memory)]
    )
    query_doc = lax.dynamic_slice_in_dim(doc_ids, position * rows, rows, 1)
    lead = jnp.full((seqs, (CSEGS + 1) * rows), -1, jnp.int32)
    padded_doc = jnp.concatenate([lead, doc_ids], 1)
    window = lax.dynamic_slice_in_dim(padded_doc, position * rows, (CSEGS + 2) * rows, 1)
    window = window.reshape(seqs, CSEGS + 2, rows)
    mem_doc = window[:, :CSEGS, 0:used:3].reshape(seqs, memory)
    mem_doc = jnp.pad(mem_doc, ((0, 0), (0, rows - memory)), constant_values=-1)
    key_doc = jnp.concatenate([window[:, CSEGS], window[:, CSEGS + 1], mem_doc], 1)
    apart = query_pos[None, :] - key_pos[:, None]
    seen = (
        key_live[None, :, None]
        & (apart >= 0)[None]
        & (key_doc[:, :, None] == query_doc[:, None, :])
    )
    far = jnp.where(seen, jnp.log((1 + jnp.maximum(apart, 0)).astype(F32))[None], FAR)

    cot_rows = recon_cot.reshape(seqs * heads, 1, rows)
    recon_parts = [
        recon_both(s, q, kv_own, kv_slot_pad, cot_rows, slots, heads, scaling)
        for s in range(seqs)
    ]
    recon = jnp.stack([part[0].reshape(heads, rows) for part in recon_parts])

    dhidden = jnp.einsum("sge,fe->sgf", out_cot, w_down, preferred_element_type=F32).astype(BF)

    attended, lses, others = [], [], []
    for s in range(seqs):
        out, lse = attend_forward(s, slopes, q, kv_prev, kv_own, kv_mem, far, scaling)
        attended.append(out)
        lses.append(lse)
        others.append(swap(out, "head"))

    middles, units2, inverses2, normed2s, hiddens, dinners, dn2s = [], [], [], [], [], [], []
    ffn_parts = []
    for s in range(seqs):
        branch = dot(attended[s][0], w_out) + dot(others[s][0], w_out_other)
        middle = inputs[s] + branch
        unit2, inverse2 = row_stats(middle)
        normed2 = (unit2 * norm2_gain + norm2_bias).astype(BF)
        inner = dot(normed2, w_up)
        inside = jnp.tanh(GELU_A * (inner + GELU_B * inner * inner * inner))
        hidden = (0.5 * inner * (1.0 + inside)).astype(BF)
        slope = 0.5 * (1.0 + inside) + 0.5 * inner * (1.0 - inside * inside) * GELU_A * (
            1.0 + 3.0 * GELU_B * inner * inner
        )
        dinner = (dhidden[s].astype(F32) * slope).astype(BF)
        dn2 = dot_nt(dinner, w_up).astype(BF)
        middles.append(middle)
        units2.append(unit2)
        inverses2.append(inverse2)
        normed2s.append(normed2)
        hiddens.append(hidden)
        dinners.append(dinner)
        dn2s.append((dn2, swap(dn2, "head")))
        ffn_parts.append(dot(hidden, w_down).astype(BF))
    normed2 = jnp.concatenate(normed2s, 0)
    hidden = jnp.concatenate(hiddens, 0)
    dinner = jnp.concatenate(dinners, 0)
    flat_cot = out_cot.reshape(seqs * rows, model)
    grad_up = dot_tn(normed2, dinner)
    grad_down = dot_tn(flat_cot, hidden)
    up_down = reduce_rows(jnp.concatenate([grad_up, grad_down], 1), dp_index)
    ffn_part = jnp.stack(ffn_parts)
    ffn_other = swap(ffn_part, "head")
    layer_out = jnp.stack(middles) + (ffn_part.astype(F32) + ffn_other.astype(F32))
    layer_out = layer_out.astype(BF)

    dmiddles, dbranches, dmixeds, dot_rows = [], [], [], []
    dgain2 = jnp.zeros((model,), F32)
    dbias2 = jnp.zeros((model,), F32)
    far_parts = []
    for s in range(seqs):
        dn2 = dn2s[s][0].astype(F32) + dn2s[s][1].astype(F32)
        dgain2 = dgain2 + jnp.sum(dn2 * units2[s], axis=0)
        dbias2 = dbias2 + jnp.sum(dn2, axis=0)
        dmiddle = out_cot[s].astype(F32) + norm_back(dn2, units2[s], inverses2[s], norm2_gain)
        dbranch = dmiddle.astype(BF)
        dmixed = dot_nt(dbranch, w_out).astype(BF)
        product = dmixed.astype(F32) * attended[s][0].astype(F32)
        dot_row = jnp.sum(product.reshape(rows, heads, hd), axis=-1).T.reshape(heads, 1, rows)
        dmiddles.append(dmiddle)
        dbranches.append(dbranch)
        dmixeds.append(dmixed[None])
        dot_rows.append(dot_row)
        far_parts.append(
            attend_backward(
                s, slopes, q, dmixed[None], lses[s], dot_row,
                jnp.concatenate([far[:, :rows], far[:, 2 * rows :]], 1),
                [kv_prev, kv_mem], False, [], scaling,
            )
        )
    back_kv = [shift(part[1], "blk", -1) for part in far_parts]
    dmem = jnp.stack([part[2] for part in far_parts], 1)
    dslot = jnp.stack(
        [
            jnp.stack([part[4][0, :slots], part[5][0, :slots]]) for part in recon_parts
        ],
        1,
    )
    for index, lag in enumerate(range(CSEGS + 1, 1, -1)):
        got = shift(dmem[:, :, index * slots : (index + 1) * slots], "blk", -lag)
        dslot = dslot + got.astype(F32)
    dslot = dslot.astype(BF)
    dpacked_part = jnp.einsum("tsce,tde->scd", dslot, w_qkv[1:], preferred_element_type=F32)
    dpacked_part = dpacked_part.astype(BF)
    away = lax.dynamic_slice_in_dim(dpacked_part, (1 - head_index) * half, half, 2)
    here = lax.dynamic_slice_in_dim(dpacked_part, head_index * half, half, 2)
    dpacked = (here.astype(F32) + swap(away, "head").astype(F32)).astype(BF)
    w_comp_half = lax.dynamic_slice_in_dim(w_comp, head_index * half, half, 2)
    grad_comp = jnp.einsum("scrd,sce->dre", triples, dpacked, preferred_element_type=F32)
    dcomp_bias = jnp.sum(dpacked.astype(F32), axis=(0, 1))
    dtriples = jnp.einsum("sce,rde->scrd", dpacked, w_comp_half, preferred_element_type=F32)
    dtriples = dtriples.reshape(seqs, used, model)
    dtriples = jnp.pad(dtriples, ((0, 0), (0, rows - used), (0, 0)))

    grad_out = dot_tn(
        jnp.concatenate(dbranches, 0), jnp.concatenate([a[0] for a in attended], 0)
    )

    own_parts = []
    for s in range(seqs):
        own_parts.append(
            attend_backward(
                s, slopes, q, dmixeds[s], lses[s], dot_rows[s], far[:, rows : 2 * rows],
                [kv_own], True,
                [far_parts[s][0], recon_parts[s][1], recon_parts[s][2], recon_parts[s][3]],
                scaling,
            )
        )
    dn1s, dqs, dkvs = [], [], []
    for s in range(seqs):
        dq = own_parts[s][0][0]
        dkv = (own_parts[s][1] + back_kv[s].astype(F32)).astype(BF)
        dn1 = dot_nt(dq, w_qkv[0]) + dot_nt(dkv[0], w_qkv[1]) + dot_nt(dkv[1], w_qkv[2])
        dn1 = (dn1 + dtriples[s]).astype(BF)
        dn1s.append((dn1, swap(dn1, "head")))
        dqs.append(dq)
        dkvs.append(dkv)
    flat_normed = normed.reshape(seqs * rows, model)
    flat_packed = packed.reshape(seqs * slots, model)
    dq_all = jnp.concatenate(dqs, 0)
    dkv_all = jnp.concatenate(dkvs, 1)
    flat_slot = dslot.reshape(2, seqs * slots, width)
    grad_q = dot_tn(flat_normed, dq_all)
    grad_k = dot_tn(flat_normed, dkv_all[0]) + dot_tn(flat_packed, flat_slot[0])
    grad_v = dot_tn(flat_normed, dkv_all[1]) + dot_tn(flat_packed, flat_slot[1])
    late = reduce_rows(
        jnp.concatenate([grad_q, grad_k, grad_v, grad_out, grad_comp.reshape(model, 3 * half)], 1),
        dp_index,
    )
    share = late.shape[0]
    comp_mine = late[:, 4 * width :].reshape(share, 3, half)
    comp_all = lax.all_gather(comp_mine, "head", axis=2, tiled=True)

    grad_tokens = []
    dgain1 = jnp.zeros((model,), F32)
    dbias1 = jnp.zeros((model,), F32)
    for s in range(seqs):
        dn1 = dn1s[s][0].astype(F32) + dn1s[s][1].astype(F32)
        dgain1 = dgain1 + jnp.sum(dn1 * unit1[s], axis=0)
        dbias1 = dbias1 + jnp.sum(dn1, axis=0)
        grad = dmiddles[s] + norm_back(dn1, unit1[s], inverse1[s], norm1_gain)
        grad_tokens.append(grad.astype(BF))
    dslopes = jnp.zeros((heads,), F32)
    for s in range(seqs):
        sums = far_parts[s][-1] + own_parts[s][-1]
        dslopes = dslopes - jnp.sum(sums[:, 2] - sums[:, 0] * sums[:, 1], axis=1)
    comp_bias_all = jnp.zeros((model,), F32)
    comp_bias_all = lax.dynamic_update_slice_in_dim(comp_bias_all, dcomp_bias, head_index * half, 0)
    small = jnp.concatenate([dgain1, dbias1, dgain2, dbias2, comp_bias_all, jnp.pad(dslopes, (0, 128 - heads))])
    small = butterfly(small.reshape(-1, 128)).reshape(-1)
    comp_bias_sum = small[4 * model : 5 * model]
    comp_bias_sum = comp_bias_sum + swap(comp_bias_sum, "head")
    return (
        layer_out,
        recon,
        jnp.stack(grad_tokens),
        jnp.transpose(late[:, : 3 * width].reshape(share, 3, width), (1, 0, 2)),
        late[:, 3 * width : 4 * width].T,
        small[5 * model : 5 * model + heads],
        up_down[:, : w_up.shape[1]],
        up_down[:, w_up.shape[1] :].T,
        jnp.transpose(comp_all, (1, 0, 2)),
        comp_bias_sum,
        small[:model],
        small[model : 2 * model],
        small[2 * model : 3 * model],
        small[3 * model : 4 * model],
    )


def solution(mesh):
    in_specs = (
        P("dp", "blk", None),
        P("dp", None),
        P(None, None, "head"),
        P("head", None),
        P("head"),
        P(None, "head"),
        P("head", None),
        P(),
        P(),
        P(),
        P(),
        P(),
        P(),
        P("dp", "blk", None),
        P("dp", "head", "blk"),
    )
    out_specs = (
        P("dp", "blk", None),
        P("dp", "head", "blk"),
        P("dp", "blk", None),
        P(None, ("blk", "dp"), "head"),
        P("head", ("blk", "dp")),
        P("head"),
        P(("blk", "dp"), "head"),
        P("head", ("blk", "dp")),
        P(None, ("blk", "dp"), None),
        P(),
        P(),
        P(),
        P(),
        P(),
    )
    return jax.shard_map(shards, mesh=mesh, in_specs=in_specs, out_specs=out_specs, check_vma=False)
```

```python
import functools
import math

import jax
import jax.numpy as jnp
from jax import lax
from jax.experimental import pallas as pl
from jax.experimental.pallas import tpu as pltpu
from jax.sharding import PartitionSpec as P

CSEGS = 3
EPS = 1e-05
FAR = 1e30
LOG2E = math.log2(math.e)
BF = jnp.bfloat16
F32 = jnp.float32
TILE = 256
NT = (((1,), (1,)), ((), ()))
GELU_A = math.sqrt(2.0 / math.pi)
GELU_B = 0.044715


def dot(a, b):
    return jnp.dot(a, b, preferred_element_type=F32)


def dot_nt(a, b):
    return lax.dot_general(a, b, NT, preferred_element_type=F32)


def dot_tn(a, b):
    return lax.dot_general(a, b, (((0,), (0,)), ((), ())), preferred_element_type=F32)


def shift(x, axis, by):
    devices = lax.axis_size(axis)
    pairs = [(i, i + by) for i in range(devices) if 0 <= i + by < devices]
    return lax.ppermute(x, axis, pairs)


def swap(x, axis, step=1):
    devices = lax.axis_size(axis)
    return lax.ppermute(x, axis, [(i, i ^ step) for i in range(devices)])


def row_stats(x):
    center = x - jnp.mean(x, axis=-1, keepdims=True)
    inverse = lax.rsqrt(jnp.mean(center * center, axis=-1, keepdims=True) + EPS)
    return center * inverse, inverse


def norm_back(grad, unit, inverse, gain):
    scaled = grad * gain
    mean_one = jnp.mean(scaled, axis=-1, keepdims=True)
    mean_two = jnp.mean(scaled * unit, axis=-1, keepdims=True)
    return inverse * (scaled - mean_one - unit * mean_two)


def front_kernel(me, own, other, gain, bias, normed, tri_own, tri_other, unit, *, slots):
    rows, model = own.shape
    padded = tri_own.shape[0]
    for source, tri in ((own, tri_own), (other, tri_other)):
        for start in range(0, rows, 128):
            part = slice(start, start + 128)
            x, _ = row_stats(source[part, :].astype(F32))
            x = x * gain[...] + bias[...]
            for lane in range(model // 128):
                unit[lane, part, :] = x[:, lane * 128 : (lane + 1) * 128]
            if source is own:
                normed[part, :] = x.astype(BF)
        live = lax.broadcasted_iota(jnp.int32, (padded, 128), 0) < slots
        for lane in range(model // 128):
            unit[lane, rows:, :] = jnp.zeros((unit.shape[1] - rows, 128), F32)
            for tap in range(3):
                at = tap * model + lane * 128
                rows_of = unit[lane, pl.ds(tap, padded, stride=3), :]
                tri[:, at : at + 128] = jnp.where(live, rows_of, 0.0).astype(BF)


def front(me, tokens, gain, bias, slots, padded):
    _, rows, model = tokens.shape
    tri = jax.ShapeDtypeStruct((padded, 3 * model), BF)
    fixed = lambda shape: pl.BlockSpec(shape, lambda i, m: (0, 0))
    pick = lambda turn: pl.BlockSpec((None, rows, model), lambda i, m: ((m[0] + turn) % 2, 0, 0))
    return pl.pallas_call(
        functools.partial(front_kernel, slots=slots),
        grid_spec=pltpu.PrefetchScalarGridSpec(
            num_scalar_prefetch=1,
            grid=(1,),
            in_specs=[pick(0), pick(1), fixed((1, model)), fixed((1, model))],
            out_specs=[fixed((rows, model)), fixed((padded, 3 * model)), fixed((padded, 3 * model))],
            scratch_shapes=[pltpu.VMEM((model // 128, 3 * padded + 8, 128), F32)],
        ),
        out_shape=[jax.ShapeDtypeStruct((rows, model), BF), tri, tri],
        compiler_params=pltpu.CompilerParams(vmem_limit_bytes=20 << 20),
        cost_estimate=pl.CostEstimate(
            flops=40 * rows * model, bytes_accessed=6 << 20, transcendentals=0),
        name="front",
    )(me, tokens, tokens, gain.reshape(1, model), bias.reshape(1, model))


def distant_kernel(halo, mem, w, kf, vf):
    rows = halo.shape[0]
    for index, out in ((1, kf), (2, vf)):
        out[:rows, :] = dot(halo[...], w[index]).astype(BF)
        out[rows:, :] = dot(mem[...], w[index]).astype(BF)


def project_distant(halo, mem, w):
    rows, model = halo.shape
    width = w.shape[2]
    shape = jax.ShapeDtypeStruct((2 * rows, width), BF)
    return pl.pallas_call(
        distant_kernel,
        out_shape=[shape, shape],
        compiler_params=pltpu.CompilerParams(vmem_limit_bytes=20 << 20),
        cost_estimate=pl.CostEstimate(
            flops=8 * model * width * rows, bytes_accessed=6 << 20, transcendentals=0),
        name="project_distant",
    )(halo, mem, w)


def far_kernel(place, docs, query, out, mem, *, slots, rows):
    position = place[0]
    for seg in range(CSEGS):
        mem[seg * slots : (seg + 1) * slots, :] = docs[pl.ds(seg * rows, slots, stride=3), :]
    mem[CSEGS * slots :, :] = jnp.full((rows - CSEGS * slots, 128), -1, jnp.int32)
    column = lax.broadcasted_iota(jnp.int32, (1, rows), 1)
    step = 64
    for start in range(0, 3 * rows, step):
        local = lax.broadcasted_iota(jnp.int32, (step, 1), 0) + start % rows
        if start < rows:
            doc = docs[CSEGS * rows + start : CSEGS * rows + start + step, :1]
            where, live = local - rows, position > 0
        elif start < 2 * rows:
            doc = mem[start - rows : start - rows + step, :1]
            lead = sum((local >= seg * slots).astype(jnp.int32) for seg in range(1, CSEGS + 1))
            where = (lead - 1 - CSEGS) * rows + 3 * (local - lead * slots) + 1
            live = position - 1 - CSEGS + lead >= 0
        else:
            at = (CSEGS + 1) * rows + start - 2 * rows
            doc = docs[at : at + step, :1]
            where, live = local, position >= 0
        doc = jnp.where(live, doc, -2)
        apart = column - where
        seen = (apart >= 0) & (doc == query[...])
        value = jnp.log((1 + jnp.maximum(apart, 0)).astype(F32))
        out[start : start + step, :] = jnp.where(seen, value, FAR)


def far_log(place, docs, query, slots):
    rows = query.shape[1]
    return pl.pallas_call(
        functools.partial(far_kernel, slots=slots, rows=rows),
        in_specs=[
            pl.BlockSpec(memory_space=pltpu.SMEM),
            pl.BlockSpec(memory_space=pltpu.VMEM),
            pl.BlockSpec(memory_space=pltpu.VMEM),
        ],
        out_shape=jax.ShapeDtypeStruct((3 * rows, rows), F32),
        scratch_shapes=[pltpu.VMEM((rows, 128), jnp.int32)],
        compiler_params=pltpu.CompilerParams(vmem_limit_bytes=20 << 20),
        cost_estimate=pl.CostEstimate(
            flops=60 * rows * rows, bytes_accessed=5 << 20, transcendentals=3 * rows * rows),
        name="far_log",
    )(place, docs, query)


def project_kernel(normed, packed, w, q, k, v, kc, vc):
    for index, out in enumerate((q, k, v)):
        out[...] = dot(normed[...], w[index]).astype(BF)
    kc[...] = dot(packed[...], w[1]).astype(BF)
    vc[...] = dot(packed[...], w[2]).astype(BF)


def project(normed, packed, w):
    rows, model = normed.shape
    padded, width = packed.shape[0], w.shape[2]
    near = jax.ShapeDtypeStruct((rows, width), BF)
    little = jax.ShapeDtypeStruct((padded, width), BF)
    return pl.pallas_call(
        project_kernel,
        out_shape=[near, near, near, little, little],
        compiler_params=pltpu.CompilerParams(vmem_limit_bytes=20 << 20),
        cost_estimate=pl.CostEstimate(
            flops=2 * model * width * (3 * rows + 2 * padded), bytes_accessed=6 << 20,
            transcendentals=0),
        name="project",
    )(normed, packed, w)


def forward_kernel(slopes, q, kf, vf, ko, vo, far, out, lse, *, scaling):
    head = pl.program_id(0)
    c1 = scaling * LOG2E
    c2 = slopes[head] * LOG2E
    rows, reach = q.shape[0], kf.shape[0]
    vft, vot = vf[...].T, vo[...].T
    for qi in range(rows // TILE):
        qs = slice(qi * TILE, (qi + 1) * TILE)
        until = (qi + 1) * TILE
        qb = q[qs, :]
        near = dot_nt(ko[:until, :], qb) * c1 - c2 * far[reach : reach + until, qs]
        away = dot_nt(kf[...], qb) * c1 - c2 * far[:reach, qs]
        top = jnp.maximum(
            jnp.max(near, axis=0, keepdims=True), jnp.max(away, axis=0, keepdims=True)
        )
        near = jnp.exp2(near - top)
        away = jnp.exp2(away - top)
        total = jnp.sum(near, axis=0, keepdims=True) + jnp.sum(away, axis=0, keepdims=True)
        mixed = dot(vot[:, :until], near.astype(BF)) + dot(vft, away.astype(BF))
        out[qs, :] = (mixed / total).T.astype(BF)
        lse[0, :, qs] = top + jnp.log2(total)


def attend_forward(slopes, q, kf, vf, ko, vo, far, scaling):
    rows, width = q.shape
    reach = kf.shape[0]
    heads = slopes.shape[0]
    hd = width // heads
    near = pl.BlockSpec((rows, hd), lambda h: (0, h))
    wide = pl.BlockSpec((reach, hd), lambda h: (0, h))
    return pl.pallas_call(
        functools.partial(forward_kernel, scaling=scaling),
        grid=(heads,),
        in_specs=[
            pl.BlockSpec(memory_space=pltpu.SMEM), near, wide, wide, near, near,
            pl.BlockSpec((reach + rows, rows), lambda h: (0, 0)),
        ],
        out_specs=[near, pl.BlockSpec((1, 1, rows), lambda h: (h, 0, 0))],
        out_shape=[
            jax.ShapeDtypeStruct((rows, width), BF),
            jax.ShapeDtypeStruct((heads, 1, rows), F32),
        ],
        compiler_params=pltpu.CompilerParams(vmem_limit_bytes=20 << 20),
        cost_estimate=pl.CostEstimate(
            flops=8 * heads * rows * (reach + rows) * hd, bytes_accessed=8 << 20,
            transcendentals=heads * rows * (reach + rows)),
        name="attend_forward",
    )(slopes, q, kf, vf, ko, vo, far)


def backward_kernel(slopes, q, do, lse, dot_row, far, k, v, *refs, scaling, own):
    head = pl.program_id(0)
    c1 = scaling * LOG2E
    c2 = slopes[head] * LOG2E
    extras = refs[:-4]
    dq, dk_out, dv_out, sums_out = refs[-4:]
    rows, hd = q.shape
    keys = k.shape[0]
    tall = rows
    for ki in range(keys // tall):
        base = ki * tall
        kt = k[base : base + tall, :].T
        dks, dvs = [], []
        for qi in range(rows // TILE):
            qs = slice(qi * TILE, (qi + 1) * TILE)
            until = (qi + 1) * TILE if own else tall
            ks = slice(base, base + until)
            qb, db = q[qs, :], do[qs, :]
            dist = far[ks, qs]
            s = dot_nt(k[ks, :], qb) * c1 - c2 * dist
            p = jnp.exp2(s - lse[0, :, qs])
            dp = dot_nt(v[ks, :], db)
            ds = p * (dp - dot_row[0, :, qs])
            for index, value in enumerate((ds, p * dist, ds * dist)):
                value = jnp.sum(value, axis=0, keepdims=True)
                if ki > 0:
                    value = value + sums_out[0, index : index + 1, qs]
                sums_out[0, index : index + 1, qs] = value
            p = p.astype(BF)
            ds = ds.astype(BF)
            dvs.append(dot(p, db))
            dks.append(dot(ds, qb))
            value = dot(kt[:, :until], ds).T * scaling
            if own:
                value = value + extras[0][qs, :] + extras[1][qs, :]
            if ki > 0:
                value = value + dq[qs, :]
            dq[qs, :] = value.astype(dq.dtype)
        for start in range(0, tall, TILE):
            ks = slice(base + start, base + start + TILE)
            dk = sum(d[start : start + TILE, :] for d in dks if d.shape[0] > start) * scaling
            dv = sum(d[start : start + TILE, :] for d in dvs if d.shape[0] > start)
            if own:
                dk = dk + extras[2][ks, :]
                dv = dv + extras[3][ks, :]
            dk_out[ks, :] = dk.astype(BF)
            dv_out[ks, :] = dv.astype(BF)


def attend_backward(slopes, q, do, lse, dot_row, far, k, v, own, extras, scaling):
    rows, width = q.shape
    keys = k.shape[0]
    heads = slopes.shape[0]
    hd = width // heads
    near = pl.BlockSpec((rows, hd), lambda h: (0, h))
    wide = pl.BlockSpec((keys, hd), lambda h: (0, h))
    lane = pl.BlockSpec((1, 1, rows), lambda h: (h, 0, 0))
    place = far.shape[0] // keys - 1 if own else 0
    return pl.pallas_call(
        functools.partial(backward_kernel, scaling=scaling, own=own),
        grid=(heads,),
        in_specs=[
            pl.BlockSpec(memory_space=pltpu.SMEM), near, near, lane, lane,
            pl.BlockSpec((keys, rows), lambda h: (place, 0)), wide, wide,
        ]
        + [near] * len(extras),
        out_specs=[near, wide, wide, pl.BlockSpec((1, 8, rows), lambda h: (h, 0, 0))],
        out_shape=[
            jax.ShapeDtypeStruct((rows, width), BF if own else F32),
            jax.ShapeDtypeStruct((keys, width), BF),
            jax.ShapeDtypeStruct((keys, width), BF),
            jax.ShapeDtypeStruct((heads, 8, rows), F32),
        ],
        compiler_params=pltpu.CompilerParams(vmem_limit_bytes=30 << 20),
        cost_estimate=pl.CostEstimate(
            flops=12 * heads * rows * keys * hd, bytes_accessed=8 << 20,
            transcendentals=heads * rows * keys),
        name="attend_backward_own" if own else "attend_backward_far",
    )(slopes, q, do, lse, dot_row, far, k, v, *extras)


def recon_kernel(q, ko, vo, kc, vc, cot, recon, dq, dk, dv, dkc, dvc, *, slots, scaling):
    rows, hd = q.shape
    c1 = scaling * LOG2E
    comp_rows = kc.shape[0]
    live = lax.broadcasted_iota(jnp.int32, (comp_rows, TILE), 0) < slots
    kct, vct, kot, vot = kc[...].T, vc[...].T, ko[...].T, vo[...].T
    for qi in range(rows // TILE):
        qs = slice(qi * TILE, (qi + 1) * TILE)
        qb = q[qs, :]
        full_s = dot_nt(ko[...], qb) * c1
        full_p = jnp.exp2(full_s - jnp.max(full_s, axis=0, keepdims=True))
        full_p = full_p * (1.0 / jnp.sum(full_p, axis=0, keepdims=True))
        full_low = full_p.astype(BF)
        comp_s = jnp.where(live, dot_nt(kc[...], qb) * c1, -FAR)
        comp_p = jnp.exp2(comp_s - jnp.max(comp_s, axis=0, keepdims=True))
        comp_p = comp_p * (1.0 / jnp.sum(comp_p, axis=0, keepdims=True))
        comp_low = comp_p.astype(BF)
        full, comp = dot(vot, full_low), dot(vct, comp_low)
        spread = full - comp
        recon[0, :, qs] = jnp.sum(spread * spread, axis=0, keepdims=True) / hd**0.5
        dfull = spread * (cot[0, :, qs] * (2.0 / hd**0.5))
        dfull_low = dfull.astype(BF)
        dfull_rows = dfull_low.T
        full_dw = dot(vo[...], dfull_low)
        comp_dw = dot(vc[...], dfull_low)
        row = jnp.sum(full_p * full_dw, axis=0, keepdims=True)
        full_ds = (full_p * (full_dw - row)).astype(BF)
        row = jnp.sum(comp_p * comp_dw, axis=0, keepdims=True)
        comp_ds = (comp_p * (row - comp_dw)).astype(BF)
        dq[qs, :] = (dot(kot, full_ds) + dot(kct, comp_ds)).T * scaling
        values = (
            (dk, dot(full_ds, qb) * scaling),
            (dv, dot(full_low, dfull_rows)),
            (dkc, dot(comp_ds, qb) * scaling),
            (dvc, -dot(comp_low, dfull_rows)),
        )
        for ref, value in values:
            if qi > 0:
                value = value + ref[...]
            ref[...] = value


def recon_both(q, ko, vo, kc, vc, cot, slots, scaling):
    rows, width = q.shape
    heads = cot.shape[0]
    hd = width // heads
    comp_rows = kc.shape[0]
    near = pl.BlockSpec((rows, hd), lambda h: (0, h))
    small = pl.BlockSpec((comp_rows, hd), lambda h: (0, h))
    lane = pl.BlockSpec((1, 1, rows), lambda h: (h, 0, 0))
    big = jax.ShapeDtypeStruct((rows, width), F32)
    little = jax.ShapeDtypeStruct((comp_rows, width), F32)
    return pl.pallas_call(
        functools.partial(recon_kernel, slots=slots, scaling=scaling),
        grid=(heads,),
        in_specs=[near, near, near, small, small, lane],
        out_specs=[lane, near, near, near, small, small],
        out_shape=[jax.ShapeDtypeStruct((heads, 1, rows), F32), big, big, big, little, little],
        compiler_params=pltpu.CompilerParams(vmem_limit_bytes=20 << 20),
        cost_estimate=pl.CostEstimate(
            flops=24 * heads * rows * (rows + comp_rows) * hd, bytes_accessed=8 << 20,
            transcendentals=heads * rows * (rows + comp_rows)),
        name="recon_both",
    )(q, ko, vo, kc, vc, cot)


def middle_kernel(me, tokens, a_one, a_two, w_one, w_two, gain, bias, middle, normed):
    value = tokens[...].astype(F32) + (dot(a_one[...], w_one[...]) + dot(a_two[...], w_two[...]))
    middle[...] = value
    unit, _ = row_stats(value)
    normed[...] = (unit * gain[...] + bias[...]).astype(BF)


def middle_norm(me, tokens, a_one, a_two, w_one, w_two, gain, bias):
    _, rows, model = tokens.shape
    width = a_one.shape[1]
    tall = pl.BlockSpec((TILE, model), lambda i, m: (i, 0))
    part = pl.BlockSpec((TILE, width), lambda i, m: (i, 0))
    fixed = lambda shape: pl.BlockSpec(shape, lambda i, m: (0, 0))
    return pl.pallas_call(
        middle_kernel,
        grid_spec=pltpu.PrefetchScalarGridSpec(
            num_scalar_prefetch=1,
            grid=(rows // TILE,),
            in_specs=[pl.BlockSpec((None, TILE, model), lambda i, m: (m[0], i, 0)), part, part,
                      fixed((width, model)), fixed((width, model)), fixed((1, model)),
                      fixed((1, model))],
            out_specs=[tall, tall],
        ),
        out_shape=[jax.ShapeDtypeStruct((rows, model), F32), jax.ShapeDtypeStruct((rows, model), BF)],
        compiler_params=pltpu.CompilerParams(vmem_limit_bytes=20 << 20),
        cost_estimate=pl.CostEstimate(
            flops=4 * rows * width * model, bytes_accessed=8 << 20, transcendentals=0),
        name="middle_norm",
    )(me, tokens, a_one, a_two, w_one, w_two, gain.reshape(1, model), bias.reshape(1, model))


def mlp_kernel(which, normed, cot, w_up, w_down, hidden, dinner, dnormed, branch, dn_sum, br_sum):
    step = pl.program_id(0)
    rows = normed.shape[0]
    for start in range(0, rows, rows):
        part = slice(start, start + rows)
        inner = dot(normed[part, :], w_up[...])
        dhidden = dot_nt(cot[part, :], w_down[...])
        square = inner * inner
        inside = jnp.tanh(inner * (GELU_A + (GELU_A * GELU_B) * square))
        bent = 0.5 * (1.0 + inside)
        low = (inner * bent).astype(BF)
        slope = bent + inner * (0.5 - 0.5 * inside * inside) * (
            GELU_A + (3.0 * GELU_A * GELU_B) * square
        )
        dlow = (dhidden * slope).astype(BF)
        hidden[part, :] = low
        dinner[part, :] = dlow
        dn = dot_nt(dlow, w_up[...])
        br = dot(low, w_down[...])

        @pl.when(step == 0)
        def _():
            dn_sum[part, :] = dn
            br_sum[part, :] = br

        @pl.when(step > 0)
        def _():
            dn_sum[part, :] += dn
            br_sum[part, :] += br

    @pl.when(step == pl.num_programs(0) - 1)
    def _():
        dnormed[...] = dn_sum[...].astype(dnormed.dtype)
        branch[...] = br_sum[...].astype(branch.dtype)


def mlp(which, normed, cot, w_up, w_down, dtype):
    rows, model = normed.shape
    units = w_up.shape[1]
    step = 512
    tall = pl.BlockSpec((rows, model), lambda f, m: (0, 0))
    act = pl.BlockSpec((rows, step), lambda f, m: (0, f))
    return pl.pallas_call(
        mlp_kernel,
        grid_spec=pltpu.PrefetchScalarGridSpec(
            num_scalar_prefetch=1,
            grid=(units // step,),
            in_specs=[tall, pl.BlockSpec((None, rows, model), lambda f, m: (m[0], 0, 0)),
                      pl.BlockSpec((model, step), lambda f, m: (0, f)),
                      pl.BlockSpec((step, model), lambda f, m: (f, 0))],
            out_specs=[act, act, tall, tall],
            scratch_shapes=[pltpu.VMEM((rows, model), F32)] * 2,
        ),
        out_shape=[jax.ShapeDtypeStruct((rows, units), BF)] * 2
        + [jax.ShapeDtypeStruct((rows, model), dtype)] * 2,
        compiler_params=pltpu.CompilerParams(vmem_limit_bytes=30 << 20),
        cost_estimate=pl.CostEstimate(
            flops=8 * rows * units * model, bytes_accessed=16 << 20, transcendentals=rows * units),
        name="mlp",
    )(which, normed, cot, w_up, w_down)


def turn_kernel(
    me, dn_own, dn_got, middle, cot, a_one, a_two, w_one, w_two, gain,
    dmiddle, dbranch, da_one, da_two, row_one, row_two, sums,
):
    step = pl.program_id(0)
    dn = dn_own[...] + dn_got[...].astype(F32)
    unit, inverse = row_stats(middle[...])
    value = cot[...].astype(F32) + norm_back(dn, unit, inverse, gain[...])
    dmiddle[...] = value
    low = value.astype(BF)
    dbranch[...] = low
    for a, w, da, row in ((a_one, w_one, da_one, row_one), (a_two, w_two, da_two, row_two)):
        grad = dot_nt(low, w[...]).astype(BF)
        da[...] = grad
        product = (grad.astype(F32) * a[...].astype(F32)).T
        heads = row.shape[0]
        row[:, 0, :] = jnp.sum(product.reshape(heads, -1, TILE), axis=1)

    @pl.when(step == 0)
    def _():
        sums[...] = jnp.zeros_like(sums)

    sums[0:1, :] += jnp.sum(dn * unit, axis=0, keepdims=True)
    sums[1:2, :] += jnp.sum(dn, axis=0, keepdims=True)


def turn(me, dn_own, dn_got, middle, cot, a_one, a_two, w_one, w_two, gain, heads):
    rows, model = middle.shape
    width = a_one.shape[1]
    tall = pl.BlockSpec((TILE, model), lambda i, m: (i, 0))
    part = pl.BlockSpec((TILE, width), lambda i, m: (i, 0))
    lane = pl.BlockSpec((heads, 1, TILE), lambda i, m: (0, 0, i))
    fixed = lambda shape: pl.BlockSpec(shape, lambda i, m: (0, 0))
    return pl.pallas_call(
        turn_kernel,
        grid_spec=pltpu.PrefetchScalarGridSpec(
            num_scalar_prefetch=1,
            grid=(rows // TILE,),
            in_specs=[tall, tall, tall,
                      pl.BlockSpec((None, TILE, model), lambda i, m: (m[0], i, 0)),
                      part, part, fixed((width, model)), fixed((width, model)), fixed((1, model))],
            out_specs=[tall, tall, part, part, lane, lane, fixed((8, model))],
        ),
        out_shape=[
            jax.ShapeDtypeStruct((rows, model), F32),
            jax.ShapeDtypeStruct((rows, model), BF),
            jax.ShapeDtypeStruct((rows, width), BF),
            jax.ShapeDtypeStruct((rows, width), BF),
            jax.ShapeDtypeStruct((heads, 1, rows), F32),
            jax.ShapeDtypeStruct((heads, 1, rows), F32),
            jax.ShapeDtypeStruct((8, model), F32),
        ],
        compiler_params=pltpu.CompilerParams(vmem_limit_bytes=30 << 20),
        cost_estimate=pl.CostEstimate(
            flops=4 * rows * width * model, bytes_accessed=12 << 20, transcendentals=0),
        name="turn",
    )(me, dn_own, dn_got, middle, cot, a_one, a_two, w_one, w_two, gain.reshape(1, model))


def finish_kernel(
    me, base, back, dpacked, w_comp, tokens, dmiddle, gain, grad, sums, total, *, rows
):
    model = base.shape[1]
    padded = dpacked.shape[0]
    for lane in range(model // 128):
        wide = slice(lane * 128, (lane + 1) * 128)
        total[lane, :rows, :] = base[:, wide] + back[:, wide].astype(F32)
        total[lane, rows:, :] = jnp.zeros((total.shape[1] - rows, 128), F32)
    for tap in range(3):
        place = pl.ds(tap, padded, stride=3)
        term = dot_nt(dpacked[...], w_comp[tap])
        for lane in range(model // 128):
            value = total[lane, place, :] + term[:, lane * 128 : (lane + 1) * 128]
            total[lane, place, :] = value
    one = jnp.zeros((1, model), F32)
    two = jnp.zeros((1, model), F32)
    for start in range(0, rows, 128):
        part = slice(start, start + 128)
        dn = jnp.concatenate([total[lane, part, :] for lane in range(model // 128)], 1)
        unit, inverse = row_stats(tokens[part, :].astype(F32))
        value = dmiddle[part, :] + norm_back(dn, unit, inverse, gain[...])
        grad[part, :] = value.astype(BF)
        one = one + jnp.sum(dn * unit, axis=0, keepdims=True)
        two = two + jnp.sum(dn, axis=0, keepdims=True)
    sums[0:1, :] = one
    sums[1:2, :] = two


def finish(me, base, back, dpacked, w_comp, tokens, dmiddle, gain):
    rows, model = base.shape
    padded = dpacked.shape[0]
    fixed = lambda *shape: pl.BlockSpec(shape, lambda i, m: (0,) * len(shape))
    return pl.pallas_call(
        functools.partial(finish_kernel, rows=rows),
        grid_spec=pltpu.PrefetchScalarGridSpec(
            num_scalar_prefetch=1,
            grid=(1,),
            in_specs=[fixed(rows, model), fixed(rows, model), fixed(padded, model),
                      fixed(*w_comp.shape),
                      pl.BlockSpec((None, rows, model), lambda i, m: (m[0], 0, 0)),
                      fixed(rows, model), fixed(1, model)],
            out_specs=[fixed(rows, model), fixed(8, model)],
            scratch_shapes=[pltpu.VMEM((model // 128, 3 * padded + 8, 128), F32)],
        ),
        out_shape=[
            jax.ShapeDtypeStruct((rows, model), BF),
            jax.ShapeDtypeStruct((8, model), F32),
        ],
        compiler_params=pltpu.CompilerParams(vmem_limit_bytes=36 << 20),
        cost_estimate=pl.CostEstimate(
            flops=6 * padded * model * model, bytes_accessed=16 << 20, transcendentals=0),
        name="finish",
    )(me, base, back, dpacked, w_comp, tokens, dmiddle, gain.reshape(1, model))


def weight_kernel(core, *refs, plan, block, share):
    if share:
        operands, (keep, send, held) = refs[:-3], refs[-3:]
    else:
        operands, held = refs[:-1], refs[-1]
    tall = held.shape[0]
    at = 0
    for pairs, columns in plan:
        for start in range(0, columns, block):
            wide = slice(start, min(start + block, columns))
            value = None
            for a, b in pairs:
                term = lax.dot_general(
                    operands[a][...], operands[b][:, wide], (((0,), (0,)), ((), ())),
                    preferred_element_type=F32,
                )
                value = term if value is None else value + term
            held[:, at + start : at + wide.stop] = value.astype(BF)
        at += columns
    if not share:
        return
    mine = core[0]
    for index in range(tall // (2 * share)):
        here = slice(index * share, (index + 1) * share)
        keep[here, :] = held[pl.ds(index * 2 * share + mine * share, share), :]
        send[here, :] = held[pl.ds(index * 2 * share + (1 - mine) * share, share), :]


def weight_grads(scalars, sections, share, model, name, tall=512):
    operands, specs, plan, total = [], [], [], 0
    known = {}

    def place(array, kind, at, columns, depth):
        key = (id(array), kind, at, columns)
        if key not in known:
            known[key] = len(operands)
            operands.append(array)
            if kind == "b":
                col, row = at
                spec = pl.BlockSpec(
                    (depth, columns), lambda i, c, f=col // columns, r=row // depth: (r, f)
                )
            elif array.ndim == 3:
                spec = pl.BlockSpec((None, depth, tall), lambda i, c, t=at: ((c[1] + t) % 2, 0, i))
            else:
                spec = pl.BlockSpec((depth, tall), lambda i, c, f=at // tall: (0, f + i))
            specs.append(spec)
        return known[key]

    for pairs in sections:
        columns = pairs[0][4]
        plan.append(
            (
                [
                    (
                        place(a, "a", pa, 0, a.shape[-2]),
                        place(b, "b", pb, columns, a.shape[-2]),
                    )
                    for a, pa, b, pb, _ in pairs
                ],
                columns,
            )
        )
        total += columns
    tile = tall // 2 if share else tall
    out = [pl.BlockSpec((tile, total), lambda i, c: (i, 0))] * (2 if share else 1)
    shape = [jax.ShapeDtypeStruct((tile * (model // tall), total), BF)] * len(out)
    flops = sum(2 * model * p[4] * p[0].shape[-2] for pairs in sections for p in pairs)
    return pl.pallas_call(
        functools.partial(weight_kernel, plan=tuple(plan), block=512, share=share),
        grid_spec=pltpu.PrefetchScalarGridSpec(
            num_scalar_prefetch=1,
            grid=(model // tall,),
            in_specs=specs,
            out_specs=out,
            scratch_shapes=[pltpu.VMEM((tall, total), BF)] if share else [],
        ),
        out_shape=shape,
        compiler_params=pltpu.CompilerParams(vmem_limit_bytes=40 << 20),
        cost_estimate=pl.CostEstimate(flops=flops, bytes_accessed=16 << 20, transcendentals=0),
        name=name,
    )(scalars, *operands)


def after(x, *others):
    return lax.optimization_barrier((x,) + others)[0]


def halve_blocks(x, bits, position):
    blocks = lax.axis_size("blk")
    count = blocks.bit_length() - 1
    x = x.reshape((2,) * count + (x.shape[0] // blocks, x.shape[1]))
    left = list(range(count - 1, -1, -1))
    for bit in bits:
        axis = left.index(bit)
        mine = (position >> bit) & 1
        away = lax.dynamic_index_in_dim(x, 1 - mine, axis, keepdims=False)
        here = lax.dynamic_index_in_dim(x, mine, axis, keepdims=False)
        x = here + swap(away, "blk", 1 << bit)
        left.remove(bit)
    return x


def reduce_blocks(x):
    return lax.psum_scatter(x, "blk", scatter_dimension=0, tiled=True)


def butterfly(x):
    x = x + swap(x, "dp")
    step = 1
    while step < lax.axis_size("blk"):
        x = x + swap(x, "blk", step)
        step *= 2
    return x + swap(x, "head")


def in_order(mine, first, second, axis):
    return jnp.where(
        mine == 0, jnp.concatenate([first, second], axis), jnp.concatenate([second, first], axis)
    )


def pick(x, index, axis=0):
    return lax.dynamic_index_in_dim(x, index, axis, keepdims=False)


def shards(
    tokens, doc_ids, w_qkv, w_out, slopes, w_up, w_down, w_comp, comp_bias,
    norm1_gain, norm1_bias, norm2_gain, norm2_bias, out_cot, recon_cot,
):
    seqs, rows, model = tokens.shape
    heads = slopes.shape[0]
    width = w_qkv.shape[2]
    hd = width // heads
    slots = rows // 3
    used = 3 * slots
    padded = -(-slots // 16) * 16
    memory = CSEGS * slots
    position = lax.axis_index("blk")
    core = lax.axis_index("dp")
    me = lax.axis_index("head")
    ot = 1 - me
    scaling = hd ** (-0.5)
    half = model // 2
    share = model // (lax.axis_size("blk") * lax.axis_size("dp"))
    bits = lax.axis_size("blk").bit_length() - 1
    rising = list(range(bits))
    falling = [1, 0] + rising[2:]
    scalars = jnp.stack([core, me]).astype(jnp.int32)
    me_arg, ot_arg = me.reshape(1).astype(jnp.int32), ot.reshape(1).astype(jnp.int32)

    small = jnp.concatenate(
        [pick(recon_cot, ot), jnp.pad(slopes, (0, rows - heads)).reshape(1, rows)], 0
    )
    small_got = swap(small, "head")
    half_rows = model // 2
    qkv_part = lax.dynamic_slice_in_dim(after(w_qkv, small), core * half_rows, half_rows, 1)
    far_qkv = swap(qkv_part, "head")
    groups = ("own", "oth")

    normed, tri_own, tri_oth = front(
        me_arg, after(tokens, qkv_part), norm1_gain, norm1_bias, slots, padded
    )
    halo = shift(normed, "blk", 1)
    packed = dot(tri_own, w_comp.reshape(3 * model, model)) + comp_bias
    packed = packed.astype(BF)
    parity = position % 2
    lag2 = shift(packed, "blk", 2)

    out_part = lax.dynamic_slice_in_dim(
        after(w_out, packed), core * (width // 2), width // 2, 0
    )
    far_out = swap(out_part, "head")

    docs = pick(doc_ids, me)
    query_doc = lax.dynamic_slice_in_dim(docs, position * rows, rows, 0).reshape(1, rows)
    padded_doc = jnp.concatenate([jnp.full(((CSEGS + 1) * rows,), -1, jnp.int32), docs])
    window = lax.dynamic_slice_in_dim(padded_doc, position * rows, (CSEGS + 2) * rows, 0)
    window = jnp.broadcast_to(window[:, None], ((CSEGS + 2) * rows, 128))
    far = far_log(position.reshape(1).astype(jnp.int32), window, after(query_doc, out_part), slots)

    weights, outs = {"own": w_qkv}, {"own": w_out}
    cots = {"own": pick(recon_cot, me).reshape(heads, 1, rows)}
    slope = {"own": slopes}
    q, ko, vo, kc, vc, rec, kf, vf, att, lse = ({} for _ in range(10))
    q["own"], ko["own"], vo["own"], kc["own"], vc["own"] = project(
        normed, after(packed, far), w_qkv
    )
    lag2 = after(lag2, q["own"])
    lag4 = shift(lag2, "blk", 2)
    small_got = after(small_got, q["own"])
    cots["oth"] = small_got[:heads].reshape(heads, 1, rows)
    slope["oth"] = small_got[heads, :heads]
    rec["own"] = recon_both(
        after(q["own"], small_got), ko["own"], vo["own"], kc["own"], vc["own"], cots["own"],
        slots, scaling,
    )
    lag4 = after(lag4, rec["own"][0])
    lag3 = swap(jnp.where(parity == 0, lag2, lag4), "blk", 1)
    far_qkv = after(far_qkv, rec["own"][0])
    near_qkv = swap(far_qkv, "dp")
    mem = jnp.zeros((rows, model), BF)
    for index, lag in enumerate((lag4, lag3, lag2)):
        place = (index * slots, rows - (index + 1) * slots)
        mem = mem + jnp.pad(lag[:slots], (place, (0, 0)))
    for g in groups:
        if g == "oth":
            near_qkv = after(near_qkv, att["own"])
            weights[g] = in_order(core, far_qkv, near_qkv, 1)
            outs[g] = in_order(core, far_out, after(near_out, att["own"]), 0)
            q[g], ko[g], vo[g], kc[g], vc[g] = project(normed, packed, weights[g])
        kf[g], vf[g] = project_distant(halo, after(mem, q[g], far_qkv), weights[g])
        if g == "own":
            far_out = after(far_out, kf[g])
            near_out = swap(far_out, "dp")
        att[g], lse[g] = attend_forward(
            slope[g], q[g], after(kf[g], far_out), vf[g], ko[g], vo[g], far, scaling
        )

    middle, n2_own = middle_norm(
        me_arg, tokens, att["own"], att["oth"], w_out, outs["oth"], norm2_gain, norm2_bias
    )
    n2_oth = swap(n2_own, "head")
    rec["oth"] = recon_both(
        after(q["oth"], n2_own), ko["oth"], vo["oth"], kc["oth"], vc["oth"], cots["oth"], slots,
        scaling,
    )
    hid_own, din_own, dn_own, ffn_own = mlp(
        me_arg, after(n2_own, rec["oth"][0]), out_cot, w_up, w_down, F32
    )
    hid_oth, din_oth, dn_oth, ffn_oth = mlp(
        ot_arg, after(n2_oth, dn_own), out_cot, w_up, w_down, BF
    )
    dn_got = swap(dn_oth, "head")
    units = w_up.shape[1]
    (up_down_part,) = weight_grads(
        scalars,
        [
            [(n2_own, 0, din_own, (0, 0), units), (n2_oth, 0, din_oth, (0, 0), units)],
            [(out_cot, 0, hid_own, (0, 0), units), (out_cot, 1, hid_oth, (0, 0), units)],
        ],
        0, model, "mlp_grads",
    )
    up_down = lax.psum_scatter(up_down_part, ("blk", "dp"), scatter_dimension=0, tiled=True)
    dn_got = after(dn_got, up_down_part)
    ffn_got = swap(after(ffn_oth, dn_got), "head")

    dmiddle, dbranch, datt_own, datt_oth, row_own, row_oth, sums2 = turn(
        me_arg, dn_own, dn_got, middle, out_cot, att["own"], att["oth"], w_out, outs["oth"],
        norm2_gain, heads,
    )
    datt = {"own": datt_own, "oth": datt_oth}
    row = {"own": row_own, "oth": row_oth}
    back, near, grads = {}, {}, {}

    def far_back(g, first):
        back[g] = attend_backward(
            slope[g], q[g], after(datt[g], first), lse[g], row[g], far, kf[g], vf[g], False, [],
            scaling,
        )

    def near_back(g, first):
        r = rec[g]
        near[g] = attend_backward(
            slope[g], q[g], after(datt[g], first), lse[g], row[g], far, ko[g], vo[g], True,
            [back[g][0], r[1], r[2], r[3]], scaling,
        )

    def group_grads(g, first):
        r = rec[g]
        sections = [[(normed, 0, near[g][0], (0, 0), width)]]
        for i in (1, 2):
            sections.append(
                [
                    (normed, 0, near[g][i], (0, 0), width),
                    (packed, 0, r[3 + i], (0, 0), width),
                    (halo, 0, back[g][i], (0, 0), width),
                    (mem, 0, back[g][i], (0, rows), width),
                ]
            )
        sections.append([(after(dbranch, first), 0, att[g], (0, 0), width)])
        grads[g] = weight_grads(scalars, sections, share, model, "attention_grads")

    far_back("oth", dbranch)
    far_back("own", back["oth"][0])
    ffn_got = after(ffn_got, back["own"][0])
    lo_own = (middle + (ffn_own + ffn_got.astype(F32))).astype(BF)
    lo_got = swap(lo_own, "head")
    ddistant = sum(
        dot_nt(after(back[g][1], lo_own), weights[g][1]) + dot_nt(back[g][2], weights[g][2])
        for g in groups
    ).astype(BF)
    halo_back = shift(ddistant[:rows], "blk", -1)
    back4 = ddistant[rows : rows + slots]
    back3 = ddistant[rows + slots : rows + 2 * slots]
    back2 = ddistant[rows + 2 * slots : rows + memory]
    got3 = swap(back3, "blk", 1)
    near_back("oth", ddistant)
    group_grads("oth", near["oth"][0])
    cross_got = swap(grads["oth"][1], "dp")
    got3 = after(got3, grads["oth"][1])
    nothing = jnp.zeros_like(got3)
    back4 = back4 + jnp.where(parity == 1, got3, nothing)
    back2 = back2 + jnp.where(parity == 0, got3, nothing)
    got4 = shift(back4, "blk", -2)
    near_back("own", back4)
    cross = grads["oth"][0] + after(cross_got, near["own"][0], lo_got)
    cross_one = swap(cross[:, : 2 * width], "head")
    back2 = back2 + after(got4, near["own"][0])
    slot_back = shift(back2, "blk", -2)
    group_grads("own", after(back2, cross))
    own_got = swap(grads["own"][1], "dp")
    base = sum(
        dot_nt(after(near[g][i], grads["own"][1]), weights[g][i]) for g in groups for i in range(3)
    )
    slot_base = sum(
        dot_nt(rec[g][3 + i].astype(BF), weights[g][i]) for g in groups for i in (1, 2)
    )
    dpacked = slot_base + jnp.pad(
        after(slot_back, base), ((0, padded - slots), (0, 0))
    ).astype(F32)
    dpacked = dpacked.astype(BF)
    dp_mine = lax.dynamic_slice_in_dim(dpacked, me * half, half, 1)
    dp_got = swap(lax.dynamic_slice_in_dim(dpacked, ot * half, half, 1), "head")
    late = grads["own"][0] + after(own_got, dpacked)
    cross_one = after(cross_one, late)
    cross_two = swap(after(cross[:, 2 * width :], cross_one), "head")
    late_one = late[:, : 2 * width] + cross_one
    late_qk = halve_blocks(late_one, rising, position)
    grad_own, sums1 = finish(
        me_arg, base, halo_back, dpacked, w_comp, tokens, after(dmiddle, late_one), norm1_gain
    )
    dp_got = after(dp_got, grad_own)
    keep, send = weight_grads(
        scalars,
        [
            [
                (tri_own, tap * model, dp_mine, (0, 0), half),
                (tri_oth, tap * model, dp_got, (0, 0), half),
            ]
            for tap in range(3)
        ],
        share, model, "pack_grads",
    )
    comp_got = swap(send, "dp")
    cross_two = after(cross_two, keep)
    grad_got = swap(after(grad_own, cross_two), "head")
    late_vo = halve_blocks(late[:, 2 * width :] + cross_two, falling, position)
    comp = halve_blocks(keep + comp_got, falling, position)
    comp_got = swap(comp, "head")
    comp_all = in_order(
        me, comp.reshape(share, 3, half), comp_got.reshape(share, 3, half), 2
    ).astype(F32)

    dslopes = {}
    for g in groups:
        total = back[g][3] + near[g][3]
        dslopes[g] = -jnp.sum(total[:, 2] - total[:, 0] * total[:, 1], axis=1)
    both = in_order(me, dslopes["own"], dslopes["oth"], 0)
    dcomp_bias = jnp.sum(dpacked.astype(F32), axis=0)
    vector = jnp.concatenate(
        [sums1[0], sums1[1], sums2[0], sums2[1], dcomp_bias, jnp.pad(both, (0, 128 - 2 * heads))]
    )
    vector = butterfly(vector.reshape(-1, 128)).reshape(-1)
    slope_sum = lax.dynamic_slice_in_dim(vector, 5 * model + me * heads, heads, 0)

    recon_own = rec["own"][0].reshape(heads, rows)
    recon_got = swap(rec["oth"][0].reshape(heads, rows), "head")
    recon = in_order(me, recon_own[None], recon_got[None], 0)
    layer_out = in_order(me, lo_own[None], lo_got[None], 0)
    grad_tokens = in_order(me, grad_own[None], grad_got[None], 0)
    late = jnp.concatenate([late_qk, late_vo], 1).astype(F32)
    up_down = up_down.astype(F32)
    return (
        layer_out,
        recon,
        grad_tokens,
        jnp.transpose(late[:, : 3 * width].reshape(share, 3, width), (1, 0, 2)),
        late[:, 3 * width :].T,
        slope_sum,
        up_down[:, :units],
        up_down[:, units:].T,
        jnp.transpose(comp_all, (1, 0, 2)),
        vector[4 * model : 5 * model],
        vector[:model],
        vector[model : 2 * model],
        vector[2 * model : 3 * model],
        vector[3 * model : 4 * model],
    )


def solution(mesh):
    in_specs = (
        P("dp", "blk", None),
        P("dp", None),
        P(None, None, "head"),
        P("head", None),
        P("head"),
        P(None, "head"),
        P("head", None),
        P(),
        P(),
        P(),
        P(),
        P(),
        P(),
        P("dp", "blk", None),
        P("dp", "head", "blk"),
    )
    out_specs = (
        P("dp", "blk", None),
        P("dp", "head", "blk"),
        P("dp", "blk", None),
        P(None, ("blk", "dp"), "head"),
        P("head", ("blk", "dp")),
        P("head"),
        P(("blk", "dp"), "head"),
        P("head", ("blk", "dp")),
        P(None, ("blk", "dp"), None),
        P(),
        P(),
        P(),
        P(),
        P(),
    )
    return jax.shard_map(shards, mesh=mesh, in_specs=in_specs, out_specs=out_specs, check_vma=False)
```

```python
import functools
import math

import jax
import jax.numpy as jnp
from jax import lax
from jax.experimental import pallas as pl
from jax.experimental.pallas import tpu as pltpu
from jax.sharding import PartitionSpec as P

CSEGS = 3
EPS = 1e-05
FAR = 1e30
LOG2E = math.log2(math.e)
BF = jnp.bfloat16
F32 = jnp.float32
TILE = 256
SHARE = 1 << 24
TAIL = 1.0


LIMITS = {"recon_both": 10.3, "mlp": 20.7, "mlp_grads": 27.7, "branches": 23.3, "turn": 17.4, "attention_grads": 26.4, "spread": 17.4, "pack_grads": 19.1, "finish": 21.1}


def limit(name):
    return int(LIMITS.get(name, 14.0) * (1 << 20))


def cost(us):
    return pl.CostEstimate(flops=int(us * SHARE), bytes_accessed=1 << 10, transcendentals=0)

NT = (((1,), (1,)), ((), ()))
GELU_A = math.sqrt(2.0 / math.pi)
GELU_B = 0.044715


def dot(a, b):
    return jnp.dot(a, b, preferred_element_type=F32)


def dot_nt(a, b):
    return lax.dot_general(a, b, NT, preferred_element_type=F32)


def dot_tn(a, b):
    return lax.dot_general(a, b, (((0,), (0,)), ((), ())), preferred_element_type=F32)


def shift(x, axis, by):
    devices = lax.axis_size(axis)
    pairs = [(i, i + by) for i in range(devices) if 0 <= i + by < devices]
    return lax.ppermute(x, axis, pairs)


def trade(x):
    return lax.all_to_all(x, "dp", 0, 0)


def swap(x, axis, step=1):
    devices = lax.axis_size(axis)
    return lax.ppermute(x, axis, [(i, i ^ step) for i in range(devices)])


def call(
    kernel, deps=(), gates=(), prefetch=0, in_specs=None, from_hbm=False, to_hbm=False, **rest
):
    def run(*operands):
        count = len(operands)
        if from_hbm:
            operands = operands[:prefetch] + tuple(
                pltpu.with_memory_space_constraint(x, pltpu.HBM)
                if spec.memory_space is None else x
                for x, spec in zip(operands[prefetch:], in_specs)
            )
        passed = len(deps) + len(gates)
        specs = in_specs or [pl.BlockSpec(memory_space=pltpu.VMEM)] * count
        far = pl.BlockSpec(memory_space=pltpu.HBM)
        specs = list(specs) + [far] * passed

        def body(*refs):
            refs = refs[:count] + refs[count + passed :]
            results = count + len(rest_out)
            kernel(*refs[:results], *refs[results + len(gates) :])

        rest_out = list(rest["out_shape"])
        if to_hbm:
            rest_out = [pltpu.HBM(x.shape, x.dtype) for x in rest_out]
        settings = dict(rest)
        settings["out_shape"] = rest_out + [jax.ShapeDtypeStruct(g.shape, g.dtype) for g in gates]
        if gates:
            plain = [pl.BlockSpec(memory_space=pltpu.VMEM)] * len(rest_out)
            settings["out_specs"] = list(rest.get("out_specs", plain)) + [far] * len(gates)
            settings["input_output_aliases"] = {
                count + len(deps) + i: len(rest_out) + i for i in range(len(gates))
            }
        if prefetch:
            grid = {
                key: settings.pop(key)
                for key in ("grid", "out_specs", "scratch_shapes") if key in settings
            }
            settings["grid_spec"] = pltpu.PrefetchScalarGridSpec(
                num_scalar_prefetch=prefetch, in_specs=specs, **grid
            )
        else:
            settings["in_specs"] = specs
        return pl.pallas_call(body, **settings)(*operands, *deps, *gates)

    return run


def still(shape, index_map):
    return pl.BlockSpec(shape, index_map, pipeline_mode=pl.Buffered(1))


def row_stats(x):
    center = x - jnp.mean(x, axis=-1, keepdims=True)
    inverse = lax.rsqrt(jnp.mean(center * center, axis=-1, keepdims=True) + EPS)
    return center * inverse, inverse


def norm_back(grad, unit, inverse, gain):
    scaled = grad * gain
    mean_one = jnp.mean(scaled, axis=-1, keepdims=True)
    mean_two = jnp.mean(scaled * unit, axis=-1, keepdims=True)
    return inverse * (scaled - mean_one - unit * mean_two)


def front_kernel(me, own, other, gain, bias, normed, tri_own, tri_other, unit, *, slots):
    rows, model = own.shape
    padded = tri_own.shape[0]
    for source, tri in ((own, tri_own), (other, tri_other)):
        for start in range(0, rows, 128):
            part = slice(start, start + 128)
            x, _ = row_stats(source[part, :].astype(F32))
            x = x * gain[...] + bias[...]
            for lane in range(model // 128):
                unit[lane, part, :] = x[:, lane * 128 : (lane + 1) * 128]
            if source is own:
                normed[part, :] = x.astype(BF)
        live = lax.broadcasted_iota(jnp.int32, (padded, 128), 0) < slots
        for lane in range(model // 128):
            unit[lane, rows:, :] = jnp.zeros((unit.shape[1] - rows, 128), F32)
            for tap in range(3):
                at = tap * model + lane * 128
                rows_of = unit[lane, pl.ds(tap, padded, stride=3), :]
                tri[:, at : at + 128] = jnp.where(live, rows_of, 0.0).astype(BF)


def front(me, tokens, gain, bias, slots, padded, deps=(), gates=()):
    _, rows, model = tokens.shape
    tri = jax.ShapeDtypeStruct((padded, 3 * model), BF)
    fixed = lambda shape: still(shape, lambda i, m: (0, 0))
    pick = lambda turn: still((None, rows, model), lambda i, m: ((m[0] + turn) % 2, 0, 0))
    return call(
        functools.partial(front_kernel, slots=slots),
        deps=deps,
        gates=gates,
        **dict(
            prefetch=1,
            grid=(1,),
            in_specs=[pick(0), pick(1), fixed((1, model)), fixed((1, model))],
            out_specs=[fixed((rows, model)), fixed((padded, 3 * model)), fixed((padded, 3 * model))],
            scratch_shapes=[pltpu.VMEM((model // 128, 3 * padded + 8, 128), F32)],
        ),
        out_shape=[jax.ShapeDtypeStruct((rows, model), BF), tri, tri],
        compiler_params=pltpu.CompilerParams(vmem_limit_bytes=limit("front")),
        cost_estimate=cost(0.02),
        name="front",
    )(me, tokens, tokens, gain.reshape(1, model), bias.reshape(1, model))


def distant_kernel(halo, mem, w, kf, vf):
    rows = halo.shape[0]
    for index, out in ((1, kf), (2, vf)):
        out[:rows, :] = dot(halo[...], w[index]).astype(BF)
        out[rows:, :] = dot(mem[...], w[index]).astype(BF)


def project_distant(halo, mem, w, deps=(), gates=()):
    rows, model = halo.shape
    width = w.shape[2]
    shape = jax.ShapeDtypeStruct((2 * rows, width), BF)
    return call(
        distant_kernel,
        deps=deps,
        gates=gates,
        out_shape=[shape, shape],
        compiler_params=pltpu.CompilerParams(vmem_limit_bytes=limit("project_distant")),
        cost_estimate=cost(2.1),
        name="project_distant",
    )(halo, mem, w)


def far_kernel(place, docs, query, out, mem, *, slots, rows):
    position = place[0]
    for seg in range(CSEGS):
        mem[seg * slots : (seg + 1) * slots, :] = docs[pl.ds(seg * rows, slots, stride=3), :]
    mem[CSEGS * slots :, :] = jnp.full((rows - CSEGS * slots, 128), -1, jnp.int32)
    column = lax.broadcasted_iota(jnp.int32, (1, rows), 1)
    step = 64
    for start in range(0, 3 * rows, step):
        local = lax.broadcasted_iota(jnp.int32, (step, 1), 0) + start % rows
        if start < rows:
            doc = docs[CSEGS * rows + start : CSEGS * rows + start + step, :1]
            where, live = local - rows, position > 0
        elif start < 2 * rows:
            doc = mem[start - rows : start - rows + step, :1]
            lead = sum((local >= seg * slots).astype(jnp.int32) for seg in range(1, CSEGS + 1))
            where = (lead - 1 - CSEGS) * rows + 3 * (local - lead * slots) + 1
            live = position - 1 - CSEGS + lead >= 0
        else:
            at = (CSEGS + 1) * rows + start - 2 * rows
            doc = docs[at : at + step, :1]
            where, live = local, position >= 0
        doc = jnp.where(live, doc, -2)
        apart = column - where
        seen = (apart >= 0) & (doc == query[...])
        value = jnp.log((1 + jnp.maximum(apart, 0)).astype(F32))
        out[start : start + step, :] = jnp.where(seen, value, FAR)


def far_log(place, docs, query, slots, deps=(), gates=()):
    rows = query.shape[1]
    return call(
        functools.partial(far_kernel, slots=slots, rows=rows),
        deps=deps,
        gates=gates,
        in_specs=[
            pl.BlockSpec(memory_space=pltpu.SMEM),
            pl.BlockSpec(memory_space=pltpu.VMEM),
            pl.BlockSpec(memory_space=pltpu.VMEM),
        ],
        out_shape=[jax.ShapeDtypeStruct((3 * rows, rows), F32)],
        scratch_shapes=[pltpu.VMEM((rows, 128), jnp.int32)],
        compiler_params=pltpu.CompilerParams(vmem_limit_bytes=limit("far_log")),
        cost_estimate=cost(0.02),
        name="far_log",
    )(place, docs, query)


def project_kernel(normed, packed, w, q, k, v, kc, vc):
    for index, out in enumerate((q, k, v)):
        out[...] = dot(normed[...], w[index]).astype(BF)
    kc[...] = dot(packed[...], w[1]).astype(BF)
    vc[...] = dot(packed[...], w[2]).astype(BF)


def project(normed, packed, w, deps=(), gates=()):
    rows, model = normed.shape
    padded, width = packed.shape[0], w.shape[2]
    near = jax.ShapeDtypeStruct((rows, width), BF)
    little = jax.ShapeDtypeStruct((padded, width), BF)
    return call(
        project_kernel,
        deps=deps,
        gates=gates,
        out_shape=[near, near, near, little, little],
        compiler_params=pltpu.CompilerParams(vmem_limit_bytes=limit("project")),
        cost_estimate=cost(2.0),
        name="project",
    )(normed, packed, w)


def forward_kernel(slopes, q, kf, vf, ko, vo, far, out, lse, *, scaling):
    head = pl.program_id(0)
    c1 = scaling * LOG2E
    c2 = slopes[head] * LOG2E
    rows, reach = q.shape[0], kf.shape[0]
    vft, vot = vf[...].T, vo[...].T
    for qi in range(rows // TILE):
        qs = slice(qi * TILE, (qi + 1) * TILE)
        until = (qi + 1) * TILE
        qb = q[qs, :]
        near = dot_nt(ko[:until, :], qb) * c1 - c2 * far[reach : reach + until, qs]
        away = dot_nt(kf[...], qb) * c1 - c2 * far[:reach, qs]
        top = jnp.maximum(
            jnp.max(near, axis=0, keepdims=True), jnp.max(away, axis=0, keepdims=True)
        )
        near = jnp.exp2(near - top)
        away = jnp.exp2(away - top)
        total = jnp.sum(near, axis=0, keepdims=True) + jnp.sum(away, axis=0, keepdims=True)
        mixed = dot(vot[:, :until], near.astype(BF)) + dot(vft, away.astype(BF))
        out[qs, :] = (mixed / total).T.astype(BF)
        lse[0, :, qs] = top + jnp.log2(total)


def attend_forward(slopes, q, kf, vf, ko, vo, far, scaling, deps=(), gates=()):
    rows, width = q.shape
    reach = kf.shape[0]
    heads = slopes.shape[0]
    hd = width // heads
    near = pl.BlockSpec((rows, hd), lambda h: (0, h))
    wide = pl.BlockSpec((reach, hd), lambda h: (0, h))
    return call(
        functools.partial(forward_kernel, scaling=scaling),
        deps=deps,
        gates=gates,
        grid=(heads,),
        in_specs=[
            pl.BlockSpec(memory_space=pltpu.SMEM), near, wide, wide, near, near,
            still((reach + rows, rows), lambda h: (0, 0)),
        ],
        out_specs=[near, pl.BlockSpec((1, 1, rows), lambda h: (h, 0, 0))],
        out_shape=[
            jax.ShapeDtypeStruct((rows, width), BF),
            jax.ShapeDtypeStruct((heads, 1, rows), F32),
        ],
        compiler_params=pltpu.CompilerParams(vmem_limit_bytes=limit("attend_forward")),
        cost_estimate=cost(3.2),
        name="attend_forward",
    )(slopes, q, kf, vf, ko, vo, far)


def backward_kernel(slopes, q, do, lse, dot_row, far, k, v, *refs, scaling, own):
    head = pl.program_id(0)
    c1 = scaling * LOG2E
    c2 = slopes[head] * LOG2E
    extras = refs[:-4]
    dq, dk_out, dv_out, sums_out = refs[-4:]
    rows, hd = q.shape
    keys = k.shape[0]
    tall = rows
    dqs = [None] * (rows // TILE)
    for ki in range(keys // tall):
        base = ki * tall
        kt = k[base : base + tall, :].T
        dks, dvs = [], []
        for qi in range(rows // TILE):
            qs = slice(qi * TILE, (qi + 1) * TILE)
            until = (qi + 1) * TILE if own else tall
            ks = slice(base, base + until)
            qb, db = q[qs, :], do[qs, :]
            dist = far[ks, qs]
            s = dot_nt(k[ks, :], qb) * c1 - c2 * dist
            p = jnp.exp2(s - lse[0, :, qs])
            dp = dot_nt(v[ks, :], db)
            ds = p * (dp - dot_row[0, :, qs])
            for index, value in enumerate((ds, p * dist, ds * dist)):
                value = jnp.sum(value, axis=0, keepdims=True)
                if ki > 0:
                    value = value + sums_out[0, index : index + 1, qs]
                sums_out[0, index : index + 1, qs] = value
            p = p.astype(BF)
            ds = ds.astype(BF)
            dvs.append(dot(p, db))
            dks.append(dot(ds, qb))
            value = dot(kt[:, :until], ds)
            if ki > 0:
                value = value + dqs[qi]
            dqs[qi] = value
            if ki == keys // tall - 1:
                value = value.T * scaling
                if own:
                    value = value + extras[0][qs, :].astype(F32) + extras[1][qs, :].astype(F32)
                dq[qs, :] = value.astype(BF)
        for start in range(0, tall, TILE):
            ks = slice(base + start, base + start + TILE)
            dk = sum(d[start : start + TILE, :] for d in dks if d.shape[0] > start) * scaling
            dv = sum(d[start : start + TILE, :] for d in dvs if d.shape[0] > start)
            if own:
                dk = dk + extras[2][ks, :].astype(F32)
                dv = dv + extras[3][ks, :].astype(F32)
            dk_out[ks, :] = dk.astype(BF)
            dv_out[ks, :] = dv.astype(BF)


def attend_backward(
    slopes, q, do, lse, dot_row, far, k, v, own, extras, scaling, deps=(), gates=(), late=False
):
    rows, width = q.shape
    keys = k.shape[0]
    heads = slopes.shape[0]
    hd = width // heads
    near = pl.BlockSpec((rows, hd), lambda h: (0, h))
    wide = pl.BlockSpec((keys, hd), lambda h: (0, h))
    lane = pl.BlockSpec((1, 1, rows), lambda h: (h, 0, 0))
    place = far.shape[0] // keys - 1 if own else 0
    return call(
        functools.partial(backward_kernel, scaling=scaling, own=own),
        deps=deps,
        gates=gates,
        grid=(heads,),
        in_specs=[
            pl.BlockSpec(memory_space=pltpu.SMEM), near, near, lane, lane,
            still((keys, rows), lambda h: (place, 0)), wide, wide,
        ]
        + [near] * len(extras),
        out_specs=[near, wide, wide, pl.BlockSpec((1, 8, rows), lambda h: (h, 0, 0))],
        out_shape=[
            jax.ShapeDtypeStruct((rows, width), BF),
            jax.ShapeDtypeStruct((keys, width), BF),
            jax.ShapeDtypeStruct((keys, width), BF),
            jax.ShapeDtypeStruct((heads, 8, rows), F32),
        ],
        compiler_params=pltpu.CompilerParams(vmem_limit_bytes=limit("far" if not own else "own")),
        cost_estimate=cost(TAIL * (5 if own else 9)),
        from_hbm=late,
        to_hbm=own,
        name="attend_backward_own" if own else "attend_backward_far",
    )(slopes, q, do, lse, dot_row, far, k, v, *extras)


def recon_kernel(q, ko, vo, kc, vc, cot, recon, dq, dk, dv, dkc, dvc, *, slots, scaling):
    rows, hd = q.shape
    c1 = scaling * LOG2E
    comp_rows = kc.shape[0]
    live = lax.broadcasted_iota(jnp.int32, (comp_rows, TILE), 0) < slots
    kct, vct, kot, vot = kc[...].T, vc[...].T, ko[...].T, vo[...].T
    for qi in range(rows // TILE):
        qs = slice(qi * TILE, (qi + 1) * TILE)
        qb = q[qs, :]
        full_s = dot_nt(ko[...], qb) * c1
        full_p = jnp.exp2(full_s - jnp.max(full_s, axis=0, keepdims=True))
        full_p = full_p * (1.0 / jnp.sum(full_p, axis=0, keepdims=True))
        full_low = full_p.astype(BF)
        comp_s = jnp.where(live, dot_nt(kc[...], qb) * c1, -FAR)
        comp_p = jnp.exp2(comp_s - jnp.max(comp_s, axis=0, keepdims=True))
        comp_p = comp_p * (1.0 / jnp.sum(comp_p, axis=0, keepdims=True))
        comp_low = comp_p.astype(BF)
        full, comp = dot(vot, full_low), dot(vct, comp_low)
        spread = full - comp
        recon[0, :, qs] = jnp.sum(spread * spread, axis=0, keepdims=True) / hd**0.5
        dfull = spread * (cot[0, :, qs] * (2.0 / hd**0.5))
        dfull_low = dfull.astype(BF)
        dfull_rows = dfull_low.T
        full_dw = dot(vo[...], dfull_low)
        comp_dw = dot(vc[...], dfull_low)
        row = jnp.sum(full_p * full_dw, axis=0, keepdims=True)
        full_ds = (full_p * (full_dw - row)).astype(BF)
        row = jnp.sum(comp_p * comp_dw, axis=0, keepdims=True)
        comp_ds = (comp_p * (row - comp_dw)).astype(BF)
        dq[qs, :] = ((dot(kot, full_ds) + dot(kct, comp_ds)).T * scaling).astype(BF)
        terms = (
            dot(full_ds, qb) * scaling, dot(full_low, dfull_rows),
            dot(comp_ds, qb) * scaling, -dot(comp_low, dfull_rows),
        )
        values = terms if qi == 0 else [a + b for a, b in zip(values, terms)]
    for ref, value in zip((dk, dv, dkc, dvc), values):
        ref[...] = value.astype(ref.dtype)


def recon_both(q, ko, vo, kc, vc, cot, slots, scaling, deps=(), gates=()):
    rows, width = q.shape
    heads = cot.shape[0]
    hd = width // heads
    comp_rows = kc.shape[0]
    near = pl.BlockSpec((rows, hd), lambda h: (0, h))
    small = pl.BlockSpec((comp_rows, hd), lambda h: (0, h))
    lane = pl.BlockSpec((1, 1, rows), lambda h: (h, 0, 0))
    big = jax.ShapeDtypeStruct((rows, width), BF)
    little = jax.ShapeDtypeStruct((comp_rows, width), BF)
    return call(
        functools.partial(recon_kernel, slots=slots, scaling=scaling),
        deps=deps,
        gates=gates,
        grid=(heads,),
        in_specs=[near, near, near, small, small, lane],
        out_specs=[lane, near, near, near, small, small],
        out_shape=[jax.ShapeDtypeStruct((heads, 1, rows), F32), big, big, big, little, little],
        compiler_params=pltpu.CompilerParams(vmem_limit_bytes=limit("recon_both")),
        cost_estimate=cost(4.3),
        to_hbm=True,
        name="recon_both",
    )(q, ko, vo, kc, vc, cot)


def middle_kernel(me, tokens, a_one, a_two, w_one, w_two, gain, bias, middle, normed):
    value = tokens[...].astype(F32) + (dot(a_one[...], w_one[...]) + dot(a_two[...], w_two[...]))
    middle[...] = value
    unit, _ = row_stats(value)
    normed[...] = (unit * gain[...] + bias[...]).astype(BF)


def middle_norm(me, tokens, a_one, a_two, w_one, w_two, gain, bias, deps=(), gates=()):
    _, rows, model = tokens.shape
    width = a_one.shape[1]
    tall = pl.BlockSpec((TILE, model), lambda i, m: (i, 0))
    part = pl.BlockSpec((TILE, width), lambda i, m: (i, 0))
    fixed = lambda shape: still(shape, lambda i, m: (0, 0))
    return call(
        middle_kernel,
        deps=deps,
        gates=gates,
        **dict(
            prefetch=1,
            grid=(rows // TILE,),
            in_specs=[pl.BlockSpec((None, TILE, model), lambda i, m: (m[0], i, 0)), part, part,
                      fixed((width, model)), fixed((width, model)), fixed((1, model)),
                      fixed((1, model))],
            out_specs=[tall, tall],
        ),
        out_shape=[jax.ShapeDtypeStruct((rows, model), F32), jax.ShapeDtypeStruct((rows, model), BF)],
        compiler_params=pltpu.CompilerParams(vmem_limit_bytes=limit("middle_norm")),
        cost_estimate=cost(1.1),
        name="middle_norm",
    )(me, tokens, a_one, a_two, w_one, w_two, gain.reshape(1, model), bias.reshape(1, model))


def mlp_kernel(which, normed, cot, w_up, w_down, hidden, dinner, dnormed, dn_sum):
    step = pl.program_id(0)
    inner = dot(normed[...], w_up[...])
    dhidden = dot_nt(cot[...], w_down[...])
    square = inner * inner
    inside = jnp.tanh(inner * (GELU_A + (GELU_A * GELU_B) * square))
    bent = 0.5 * (1.0 + inside)
    hidden[...] = (inner * bent).astype(BF)
    slope = bent + inner * (0.5 - 0.5 * inside * inside) * (
        GELU_A + (3.0 * GELU_A * GELU_B) * square
    )
    dlow = (dhidden * slope).astype(BF)
    dinner[...] = dlow
    dn = dot_nt(dlow, w_up[...])

    @pl.when(step == 0)
    def _():
        dn_sum[...] = dn

    @pl.when(step > 0)
    def _():
        dn_sum[...] += dn

    @pl.when(step == pl.num_programs(0) - 1)
    def _():
        dnormed[...] = dn_sum[...].astype(dnormed.dtype)


def mlp(which, normed, cot, w_up, w_down, dtype, deps=(), gates=()):
    rows, model = normed.shape
    units = w_up.shape[1]
    step = 512
    tall = still((rows, model), lambda f, m: (0, 0))
    act = pl.BlockSpec((rows, step), lambda f, m: (0, f))
    return call(
        mlp_kernel,
        deps=deps,
        gates=gates,
        **dict(
            prefetch=1,
            grid=(units // step,),
            in_specs=[tall, still((None, rows, model), lambda f, m: (m[0], 0, 0)),
                      pl.BlockSpec((model, step), lambda f, m: (0, f)),
                      pl.BlockSpec((step, model), lambda f, m: (f, 0))],
            out_specs=[act, act, tall],
            scratch_shapes=[pltpu.VMEM((rows, model), F32)],
        ),
        out_shape=[jax.ShapeDtypeStruct((rows, units), BF)] * 2
        + [jax.ShapeDtypeStruct((rows, model), dtype)],
        compiler_params=pltpu.CompilerParams(vmem_limit_bytes=limit("mlp")),
        cost_estimate=cost(6.4),
        name="mlp",
    )(which, normed, cot, w_up, w_down)


def branch_kernel(own, oth, w_down, out_own, out_oth, sum_own, sum_oth):
    step = pl.program_id(0)
    for source, total, out in ((own, sum_own, out_own), (oth, sum_oth, out_oth)):
        part = dot(source[...], w_down[...])

        @pl.when(step == 0)
        def _():
            total[...] = part

        @pl.when(step > 0)
        def _():
            total[...] += part

        @pl.when(step == pl.num_programs(0) - 1)
        def _():
            out[...] = total[...].astype(out.dtype)


def branches(own, oth, w_down, deps=(), gates=()):
    rows, units = own.shape
    model = w_down.shape[1]
    step = 512
    tall = still((rows, model), lambda f: (0, 0))
    act = pl.BlockSpec((rows, step), lambda f: (0, f))
    return call(
        branch_kernel,
        deps=deps,
        gates=gates,
        grid=(units // step,),
        in_specs=[act, act, pl.BlockSpec((step, model), lambda f: (f, 0))],
        out_specs=[tall, tall],
        out_shape=[jax.ShapeDtypeStruct((rows, model), BF)] * 2,
        scratch_shapes=[pltpu.VMEM((rows, model), F32)] * 2,
        compiler_params=pltpu.CompilerParams(vmem_limit_bytes=limit("branches")),
        cost_estimate=cost(TAIL * 6),
        name="branches",
    )(own, oth, w_down)


def turn_kernel(
    me, dn_own, dn_got, middle, cot, a_one, a_two, w_one, w_two, gain,
    dbranch, da_one, da_two, row_one, row_two, sums,
):
    step = pl.program_id(0)
    dn = dn_own[...].astype(F32) + dn_got[...].astype(F32)
    unit, inverse = row_stats(middle[...])
    value = cot[...].astype(F32) + norm_back(dn, unit, inverse, gain[...])
    low = value.astype(BF)
    dbranch[...] = low
    for a, w, da, row in ((a_one, w_one, da_one, row_one), (a_two, w_two, da_two, row_two)):
        grad = dot_nt(low, w[...]).astype(BF)
        da[...] = grad
        product = (grad.astype(F32) * a[...].astype(F32)).T
        heads = row.shape[0]
        row[:, 0, :] = jnp.sum(product.reshape(heads, -1, TILE), axis=1)

    @pl.when(step == 0)
    def _():
        sums[...] = jnp.zeros_like(sums)

    sums[0:1, :] += jnp.sum(dn * unit, axis=0, keepdims=True)
    sums[1:2, :] += jnp.sum(dn, axis=0, keepdims=True)


def turn(me, dn_own, dn_got, middle, cot, a_one, a_two, w_one, w_two, gain, heads, deps=(), gates=()):
    rows, model = middle.shape
    width = a_one.shape[1]
    tall = pl.BlockSpec((TILE, model), lambda i, m: (i, 0))
    part = pl.BlockSpec((TILE, width), lambda i, m: (i, 0))
    lane = pl.BlockSpec((heads, 1, TILE), lambda i, m: (0, 0, i))
    fixed = lambda shape: still(shape, lambda i, m: (0, 0))
    return call(
        turn_kernel,
        deps=deps,
        gates=gates,
        **dict(
            prefetch=1,
            grid=(rows // TILE,),
            in_specs=[tall, tall, tall,
                      pl.BlockSpec((None, TILE, model), lambda i, m: (m[0], i, 0)),
                      part, part, fixed((width, model)), fixed((width, model)), fixed((1, model))],
            out_specs=[tall, part, part, lane, lane, fixed((8, model))],
        ),
        out_shape=[
            jax.ShapeDtypeStruct((rows, model), BF),
            jax.ShapeDtypeStruct((rows, width), BF),
            jax.ShapeDtypeStruct((rows, width), BF),
            jax.ShapeDtypeStruct((heads, 1, rows), F32),
            jax.ShapeDtypeStruct((heads, 1, rows), F32),
            jax.ShapeDtypeStruct((8, model), F32),
        ],
        compiler_params=pltpu.CompilerParams(vmem_limit_bytes=limit("turn")),
        cost_estimate=cost(TAIL * 5),
        name="turn",
    )(me, dn_own, dn_got, middle, cot, a_one, a_two, w_one, w_two, gain.reshape(1, model))


def spread_kernel(ka, va, kb, vb, wka, wva, wkb, wvb, near, four, three, two, held, *, slots):
    step = pl.program_id(0)
    value = dot_nt(ka[...], wka[...]) + dot_nt(va[...], wva[...])
    value = value + dot_nt(kb[...], wkb[...]) + dot_nt(vb[...], wvb[...])

    @pl.when(step == 0)
    def _():
        near[...] = value.astype(BF)

    @pl.when(step == 1)
    def _():
        rows = value.shape[0]
        held[:rows, :] = value
        held[rows:, :] = jnp.zeros((held.shape[0] - rows, value.shape[1]), F32)
        padded = four.shape[0]
        live = lax.broadcasted_iota(jnp.int32, four.shape, 0) < slots
        for index, out in enumerate((four, three, two)):
            part = held[index * slots : index * slots + padded, :]
            out[...] = jnp.where(live, part, 0.0).astype(BF)


def spread(ka, va, kb, vb, wa, wb, slots, padded, deps=(), gates=()):
    rows, width = ka.shape[0] // 2, ka.shape[1]
    model = wa.shape[1]
    part = pl.BlockSpec((rows, width), lambda i: (i, 0))
    weight = lambda t: still((None, model, width), lambda i: (t, 0, 0))
    fixed = lambda *shape: still(shape, lambda i: (0, 0))
    little = jax.ShapeDtypeStruct((padded, model), BF)
    return call(
        functools.partial(spread_kernel, slots=slots),
        deps=deps,
        gates=gates,
        grid=(2,),
        in_specs=[part] * 4 + [weight(1), weight(2)] * 2,
        out_specs=[fixed(rows, model)] + [fixed(padded, model)] * 3,
        out_shape=[jax.ShapeDtypeStruct((rows, model), BF), little, little, little],
        scratch_shapes=[pltpu.VMEM((rows + 16, model), F32)],
        compiler_params=pltpu.CompilerParams(vmem_limit_bytes=limit("spread")),
        cost_estimate=cost(TAIL * 6),
        name="spread",
    )(ka, va, kb, vb, wa, wa, wb, wb)


def base_kernel(q, k, v, kc, vc, w, *refs, more):
    before, slot_before = refs[:2] if more else (None, None)
    base, slot_base, total, slot_total = refs[-4:]
    step = pl.program_id(0)
    for index, part in enumerate((q, k, v)):

        @pl.when(step == index)
        def _():
            value = dot_nt(part[...], w[...])
            if index > 0:
                value = value + total[...]
            elif more:
                value = value + before[...].astype(F32)
            if index == 2:
                base[...] = value.astype(BF)
            else:
                total[...] = value

    for index, part in enumerate((kc, vc)):

        @pl.when(step == index + 1)
        def _():
            value = dot_nt(part[...], w[...])
            if index > 0:
                value = value + slot_total[...]
            elif more:
                value = value + slot_before[...].astype(F32)
            if index == 1:
                slot_base[...] = value.astype(BF)
            else:
                slot_total[...] = value


def base_rows(near, slot, w, before, deps=(), gates=()):
    rows, width = near[0].shape
    padded = slot[0].shape[0]
    model = w.shape[1]
    fixed = lambda *shape: still(shape, lambda i: (0, 0))
    outs = [fixed(rows, model), fixed(padded, model)]
    return call(
        functools.partial(base_kernel, more=bool(before)),
        deps=deps,
        gates=gates,
        grid=(3,),
        in_specs=[fixed(rows, width)] * 3 + [fixed(padded, width)] * 2
        + [pl.BlockSpec((None, model, width), lambda i: (i, 0, 0))]
        + outs[: len(before)],
        out_specs=outs,
        out_shape=[
            jax.ShapeDtypeStruct((rows, model), BF),
            jax.ShapeDtypeStruct((padded, model), BF),
        ],
        scratch_shapes=[pltpu.VMEM((rows, model), F32), pltpu.VMEM((padded, model), F32)],
        compiler_params=pltpu.CompilerParams(vmem_limit_bytes=limit("base_rows")),
        cost_estimate=cost(TAIL * 3),
        from_hbm=True,
        name="base_rows",
    )(*near, *slot, w, *before)


def packed_kernel(me, base, *refs):
    gots, (dpacked, mine, away, bias) = refs[:-4], refs[-4:]
    value = sum(part[...].astype(F32) for part in (base, *gots)).astype(BF)
    dpacked[...] = value
    half = mine.shape[1]
    first, second = value[:, :half], value[:, half:]
    low = me[0] == 0
    mine[...] = jnp.where(low, first, second)
    away[...] = jnp.where(low, second, first)
    bias[0:1, :] = jnp.sum(value.astype(F32), axis=0, keepdims=True)


def packed_back(me, base, gots, deps=(), gates=()):
    padded, model = base.shape
    whole = pl.BlockSpec(memory_space=pltpu.VMEM)
    little = jax.ShapeDtypeStruct((padded, model // 2), BF)
    return call(
        packed_kernel,
        deps=deps,
        gates=gates,
        in_specs=[pl.BlockSpec(memory_space=pltpu.SMEM), whole] + [whole] * len(gots),
        out_shape=[jax.ShapeDtypeStruct((padded, model), BF), little, little,
                   jax.ShapeDtypeStruct((8, model), F32)],
        compiler_params=pltpu.CompilerParams(vmem_limit_bytes=limit("packed_back")),
        cost_estimate=cost(TAIL * 400),
        name="packed_back",
    )(me, base, *gots)


def finish_kernel(
    me, base, back, dpacked, w_comp, tokens, dmiddle, gain, grad, sums, total, *, rows
):
    model = base.shape[1]
    padded = dpacked.shape[0]
    for lane in range(model // 128):
        wide = slice(lane * 128, (lane + 1) * 128)
        total[lane, :rows, :] = base[:, wide].astype(F32) + back[:, wide].astype(F32)
        total[lane, rows:, :] = jnp.zeros((total.shape[1] - rows, 128), F32)
    for tap in range(3):
        place = pl.ds(tap, padded, stride=3)
        term = dot_nt(dpacked[...], w_comp[tap])
        for lane in range(model // 128):
            value = total[lane, place, :] + term[:, lane * 128 : (lane + 1) * 128]
            total[lane, place, :] = value
    one = jnp.zeros((1, model), F32)
    two = jnp.zeros((1, model), F32)
    for start in range(0, rows, 128):
        part = slice(start, start + 128)
        dn = jnp.concatenate([total[lane, part, :] for lane in range(model // 128)], 1)
        unit, inverse = row_stats(tokens[part, :].astype(F32))
        value = dmiddle[part, :].astype(F32) + norm_back(dn, unit, inverse, gain[...])
        grad[part, :] = value.astype(BF)
        one = one + jnp.sum(dn * unit, axis=0, keepdims=True)
        two = two + jnp.sum(dn, axis=0, keepdims=True)
    sums[0:1, :] = one
    sums[1:2, :] = two


def finish(me, base, back, dpacked, w_comp, tokens, dmiddle, gain, deps=(), gates=()):
    rows, model = base.shape
    padded = dpacked.shape[0]
    fixed = lambda *shape: still(shape, lambda i, m: (0,) * len(shape))
    return call(
        functools.partial(finish_kernel, rows=rows),
        deps=deps,
        gates=gates,
        **dict(
            prefetch=1,
            grid=(1,),
            in_specs=[fixed(rows, model), fixed(rows, model), fixed(padded, model),
                      fixed(*w_comp.shape),
                      still((None, rows, model), lambda i, m: (m[0], 0, 0)),
                      fixed(rows, model), fixed(1, model)],
            out_specs=[fixed(rows, model), fixed(8, model)],
            scratch_shapes=[pltpu.VMEM((model // 128, 3 * padded + 8, 128), F32)],
        ),
        out_shape=[
            jax.ShapeDtypeStruct((rows, model), BF),
            jax.ShapeDtypeStruct((8, model), F32),
        ],
        compiler_params=pltpu.CompilerParams(vmem_limit_bytes=limit("finish")),
        cost_estimate=cost(TAIL * 4),
        name="finish",
    )(me, base, back, dpacked, w_comp, tokens, dmiddle, gain.reshape(1, model))


def weight_kernel(core, *refs, plan, block, share):
    if share:
        operands, (parts, token, held) = refs[:-3], refs[-3:]
    else:
        operands, (held, token) = refs[:-2], refs[-2:]
    token[...] = jnp.zeros_like(token)
    tall = held.shape[0]
    at = 0
    for pairs, columns in plan:
        for start in range(0, columns, block):
            wide = slice(start, min(start + block, columns))
            value = None
            for a, b in pairs:
                term = lax.dot_general(
                    operands[a][...], operands[b][:, wide], (((0,), (0,)), ((), ())),
                    preferred_element_type=F32,
                )
                value = term if value is None else value + term
            held[:, at + start : at + wide.stop] = value.astype(BF)
        at += columns
    if not share:
        return
    for index in range(tall // (2 * share)):
        for side in range(2):
            here = (2 * index + side) * share
            parts[side, index * share : (index + 1) * share, :] = held[here : here + share, :]


def weight_grads(scalars, sections, share, model, name, tall=512, deps=(), gates=()):
    operands, specs, plan, total = [], [], [], 0
    known = {}

    def place(array, kind, at, columns, depth):
        key = (id(array), kind, at, columns)
        if key not in known:
            known[key] = len(operands)
            operands.append(array)
            if kind == "b":
                col, row = at
                spec = still(
                    (depth, columns), lambda i, c, f=col // columns, r=row // depth: (r, f)
                )
            elif array.ndim == 3:
                spec = pl.BlockSpec((None, depth, tall), lambda i, c, t=at: ((c[1] + t) % 2, 0, i))
            else:
                spec = pl.BlockSpec((depth, tall), lambda i, c, f=at // tall: (0, f + i))
            specs.append(spec)
        return known[key]

    for pairs in sections:
        columns = pairs[0][4]
        plan.append(
            (
                [
                    (
                        place(a, "a", pa, 0, a.shape[-2]),
                        place(b, "b", pb, columns, a.shape[-2]),
                    )
                    for a, pa, b, pb, _ in pairs
                ],
                columns,
            )
        )
        total += columns
    tile = tall // 2 if share else tall
    if share:
        out = [pl.BlockSpec((2, tile, total), lambda i, c: (0, i, 0))]
        shape = [jax.ShapeDtypeStruct((2, tile * (model // tall), total), BF)]
    else:
        out = [pl.BlockSpec((tile, total), lambda i, c: (i, 0))]
        shape = [jax.ShapeDtypeStruct((model, total), BF)]
    out.append(pl.BlockSpec((8, 128), lambda i, c: (0, 0)))
    shape.append(jax.ShapeDtypeStruct((8, 128), F32))
    flops = sum(2 * model * p[4] * p[0].shape[-2] for pairs in sections for p in pairs)
    return call(
        functools.partial(weight_kernel, plan=tuple(plan), block=512, share=share),
        deps=deps,
        gates=gates,
        **dict(
            prefetch=1,
            grid=(model // tall,),
            in_specs=specs,
            out_specs=out,
            scratch_shapes=[pltpu.VMEM((tall, total), BF)] if share else [],
        ),
        out_shape=shape,
        compiler_params=pltpu.CompilerParams(vmem_limit_bytes=limit(name)),
        cost_estimate=cost(TAIL * flops * 1.4e-9),
        to_hbm=True,
        name=name,
    )(scalars, *operands)


def sum_kernel(*refs, split):
    terms, outs = refs[:-split], refs[-split:]
    total = sum(term[...].astype(F32) for term in terms)
    wide = total.shape[1] // split
    for index, out in enumerate(outs):
        out[...] = total[:, index * wide : (index + 1) * wide].astype(out.dtype)


def add(terms, split, name, deps=(), gates=()):
    rows, columns = terms[0].shape[-2:]
    wide = columns // split
    tile = 128 if rows % 128 == 0 else rows
    blocks, operands = [], []
    for term in terms:
        if term.ndim == 3:
            for t in range(term.shape[0]):
                blocks.append(pl.BlockSpec((None, tile, columns), lambda i, t=t: (t, i, 0)))
                operands.append(term)
        else:
            blocks.append(pl.BlockSpec((tile, columns), lambda i: (i, 0)))
            operands.append(term)
    return call(
        functools.partial(sum_kernel, split=split),
        deps=deps,
        gates=gates,
        grid=(rows // tile,),
        in_specs=blocks,
        out_specs=[pl.BlockSpec((tile, wide), lambda i: (i, 0))] * split,
        out_shape=[jax.ShapeDtypeStruct((rows, wide), BF)] * split,
        compiler_params=pltpu.CompilerParams(vmem_limit_bytes=limit(name)),
        cost_estimate=cost(TAIL * 2),
        from_hbm=True,
        name=name,
    )(*operands)


def halve_kernel(bit, *refs, blocks, stride, terms):
    parts, outs = refs[:terms], refs[terms:]
    rows = parts[0].shape[0] // blocks
    mine = bit[0]
    if len(outs) == 1:
        outs[0][...] = sum(part[...].astype(F32) for part in parts).astype(outs[0].dtype)
        return
    for out, side in zip(outs, (mine, 1 - mine)):
        for j in range(blocks // 2):
            at = (j // stride * 2 * stride + j % stride) * rows + side * (stride * rows)
            place = pl.ds(pl.multiple_of(at, rows), rows)
            total = sum(part[place, :].astype(F32) for part in parts)
            out[j * rows : (j + 1) * rows, :] = total.astype(BF)


def halve(bit, parts, blocks, stride, columns, deps=(), gates=()):
    rows = parts[0][0].shape[-2]
    last = blocks == 1
    shape = jax.ShapeDtypeStruct((rows if last else rows // 2, columns), F32 if last else BF)
    return call(
        functools.partial(halve_kernel, blocks=blocks, stride=stride, terms=len(parts)),
        deps=deps,
        gates=gates,
        **dict(
            prefetch=1,
            grid=(1,),
            in_specs=[
                still((rows, columns), lambda i, m, f=part[1] // columns: (0, f))
                if len(part) == 2
                else still(
                    (None, rows, columns), lambda i, m, f=part[1] // columns, t=part[2]: (t, 0, f)
                )
                for part in parts
            ],
            out_specs=[still(shape.shape, lambda i, m: (0, 0))] * (1 if last else 2),
        ),
        out_shape=[shape] * (1 if last else 2),
        compiler_params=pltpu.CompilerParams(vmem_limit_bytes=limit("halve")),
        cost_estimate=cost(TAIL * 3),
        name="halve",
    )(bit, *[part[0] for part in parts])


class Halving:
    def __init__(self, parts, columns, order, position):
        self.parts, self.columns, self.order = parts, columns, list(order)
        self.position = position
        self.blocks = lax.axis_size("blk")
        self.left = list(range(self.blocks.bit_length() - 2, -1, -1))

    def step(self, *deps, gates=()):
        bit = self.order.pop(0)
        place = len(self.left) - 1 - self.left.index(bit)
        mine = scalar((self.position >> bit) & 1)
        keep, away, *rest = halve(
            mine, self.parts, self.blocks, 1 << place, self.columns, deps, gates
        )
        self.parts = [(keep, 0), (swap(away, "blk", 1 << bit), 0)]
        self.left.remove(bit)
        self.blocks //= 2
        return (away, *rest) if rest else away

    def last(self, *deps):
        while self.order:
            self.step(*deps)
        return halve(scalar(self.position), self.parts, 1, 1, self.columns, deps)[0]


def scalar(x):
    return x.reshape(1).astype(jnp.int32)


def total_kernel(one, two, out):
    out[...] = one[...] + two[...]


def butterfly_steps():
    blocks = lax.axis_size("blk")
    return [("dp", 1)] + [("blk", 1 << i) for i in range(blocks.bit_length() - 1)] + [("head", 1)]


def butterfly_add(x, got, deps=()):
    whole = pl.BlockSpec(memory_space=pltpu.VMEM)
    return call(
        total_kernel,
        deps=deps,
        in_specs=[whole, whole],
        out_shape=[jax.ShapeDtypeStruct(x.shape, F32)],
        cost_estimate=cost(TAIL),
        name="small_sum",
    )(x, got)[0]


def in_order(mine, first, second, axis):
    return jnp.where(
        mine == 0, jnp.concatenate([first, second], axis), jnp.concatenate([second, first], axis)
    )


def pick(x, index, axis=0):
    return lax.dynamic_index_in_dim(x, index, axis, keepdims=False)


def shards(
    tokens, doc_ids, w_qkv, w_out, slopes, w_up, w_down, w_comp, comp_bias,
    norm1_gain, norm1_bias, norm2_gain, norm2_bias, out_cot, recon_cot,
):
    seqs, rows, model = tokens.shape
    heads = slopes.shape[0]
    width = w_qkv.shape[2]
    hd = width // heads
    slots = rows // 3
    used = 3 * slots
    padded = -(-slots // 16) * 16
    memory = CSEGS * slots
    position = lax.axis_index("blk")
    core = lax.axis_index("dp")
    me = lax.axis_index("head")
    ot = 1 - me
    scaling = hd ** (-0.5)
    half = model // 2
    share = model // (lax.axis_size("blk") * lax.axis_size("dp"))
    bits = lax.axis_size("blk").bit_length() - 1
    rising = list(range(bits))
    falling = [1, 0] + rising[2:]
    scalars = jnp.stack([core, me]).astype(jnp.int32)
    me_arg, ot_arg = me.reshape(1).astype(jnp.int32), ot.reshape(1).astype(jnp.int32)

    small = jnp.concatenate(
        [pick(recon_cot, ot), jnp.pad(slopes, (0, rows - heads)).reshape(1, rows)], 0
    )
    small_got = swap(small, "head")
    half_rows = model // 2
    qkv_part = lax.dynamic_slice_in_dim(w_qkv, core * half_rows, half_rows, 1)
    out_part = lax.dynamic_slice_in_dim(w_out, core * half_rows, half_rows, 1)
    far_part = jnp.concatenate([qkv_part, out_part[None]], 0)
    far_got = swap(far_part, "head")
    groups = ("own", "oth")

    normed, tri_own, tri_oth = front(
        me_arg, tokens, norm1_gain, norm1_bias, slots, padded, deps=(far_part, small)
    )
    halo = shift(normed, "blk", 1)
    packed = dot(tri_own, w_comp.reshape(3 * model, model)) + comp_bias
    packed = packed.astype(BF)
    lag2, lag3 = shift(packed, "blk", 2), shift(packed, "blk", 3)

    docs = pick(doc_ids, me)
    query_doc = lax.dynamic_slice_in_dim(docs, position * rows, rows, 0).reshape(1, rows)
    padded_doc = jnp.concatenate([jnp.full(((CSEGS + 1) * rows,), -1, jnp.int32), docs])
    window = lax.dynamic_slice_in_dim(padded_doc, position * rows, (CSEGS + 2) * rows, 0)
    window = jnp.broadcast_to(window[:, None], ((CSEGS + 2) * rows, 128))
    (far,) = far_log(
        position.reshape(1).astype(jnp.int32), window, query_doc, slots, deps=(packed,)
    )

    weights, outs = {"own": w_qkv}, {"own": w_out}
    cots = {"own": pick(recon_cot, me).reshape(heads, 1, rows)}
    slope = {"own": slopes}
    q, ko, vo, kc, vc, rec, kf, vf, att, lse = ({} for _ in range(10))
    q["own"], ko["own"], vo["own"], kc["own"], vc["own"], lag2 = project(
        normed, packed, w_qkv, deps=(far,), gates=(lag2,)
    )
    lag4 = shift(lag2, "blk", 2)
    cots["oth"] = small_got[:heads].reshape(heads, 1, rows)
    slope["oth"] = small_got[heads, :heads]
    rec["own"] = recon_both(
        q["own"], ko["own"], vo["own"], kc["own"], vc["own"], cots["own"], slots, scaling,
    )
    mem = jnp.zeros((rows, model), BF)
    for index, lag in enumerate((lag4, lag3, lag2)):
        place = (index * slots, rows - (index + 1) * slots)
        mem = mem + jnp.pad(lag[:slots], (place, (0, 0)))
    kf["own"], vf["own"], far_got = project_distant(
        halo, mem, w_qkv, deps=(rec["own"][0],), gates=(far_got,)
    )
    near_got = swap(far_got, "dp")
    att["own"], lse["own"] = attend_forward(
        slope["own"], q["own"], kf["own"], vf["own"], ko["own"], vo["own"], far, scaling
    )
    weights["oth"] = in_order(core, far_got[:3], near_got[:3], 1)
    outs["oth"] = in_order(core, far_got[3], near_got[3], 1)
    q["oth"], ko["oth"], vo["oth"], kc["oth"], vc["oth"] = project(
        normed, packed, weights["oth"], deps=(att["own"],)
    )
    kf["oth"], vf["oth"] = project_distant(halo, mem, weights["oth"], deps=(q["oth"],))
    att["oth"], lse["oth"] = attend_forward(
        slope["oth"], q["oth"], kf["oth"], vf["oth"], ko["oth"], vo["oth"], far, scaling
    )

    middle, n2_own = middle_norm(
        me_arg, tokens, att["own"], att["oth"], w_out, outs["oth"], norm2_gain, norm2_bias
    )
    n2_oth = swap(n2_own, "head")
    rec["oth"] = recon_both(
        q["oth"], ko["oth"], vo["oth"], kc["oth"], vc["oth"], cots["oth"], slots, scaling,
        deps=(n2_own,),
    )
    hid_own, din_own, dn_own = mlp(
        me_arg, n2_own, out_cot, w_up, w_down, BF, deps=(rec["oth"][0],)
    )
    hid_oth, din_oth, dn_oth = mlp(
        ot_arg, n2_oth, out_cot, w_up, w_down, BF, deps=(dn_own,)
    )
    dn_got = swap(dn_oth, "head")
    units = w_up.shape[1]
    up_down, token = weight_grads(
        scalars,
        [
            [(n2_own, 0, din_own, (0, 0), units), (n2_oth, 0, din_oth, (0, 0), units)],
            [(out_cot, 0, hid_own, (0, 0), units), (out_cot, 1, hid_oth, (0, 0), units)],
        ],
        0, model, "mlp_grads", deps=(dn_oth,),
    )
    ffn_own, ffn_oth = branches(hid_own, hid_oth, w_down, deps=(token,))
    up_down = lax.psum_scatter(up_down, ("blk", "dp"), scatter_dimension=0, tiled=True)
    (
        dbranch, datt_own, datt_oth, row_own, row_oth, sums2,
        ffn_oth, recon_oth,
    ) = turn(
        me_arg, dn_own, dn_got, middle, out_cot, att["own"], att["oth"], w_out, outs["oth"],
        norm2_gain, heads, gates=(ffn_oth, rec["oth"][0]),
    )
    ffn_got = swap(ffn_oth, "head")
    recon_got = swap(recon_oth.reshape(heads, rows), "head")
    datt = {"own": datt_own, "oth": datt_oth}
    row = {"own": row_own, "oth": row_oth}
    back, near, grads = {}, {}, {}

    def far_back(g, *deps):
        back[g] = attend_backward(
            slope[g], q[g], datt[g], lse[g], row[g], far, kf[g], vf[g], False, [], scaling,
            deps=deps, late=g == "own",
        )

    def near_back(g, *deps, gates=()):
        r = rec[g]
        near[g] = attend_backward(
            slope[g], q[g], datt[g], lse[g], row[g], far, ko[g], vo[g], True,
            [back[g][0], r[1], r[2], r[3]], scaling, deps=deps, gates=gates, late=g == "own",
        )

    def group_grads(g, *deps, gates=()):
        r = rec[g]
        sections = [[(normed, 0, near[g][0], (0, 0), width)]]
        for i in (1, 2):
            sections.append(
                [
                    (normed, 0, near[g][i], (0, 0), width),
                    (packed, 0, r[3 + i], (0, 0), width),
                    (halo, 0, back[g][i], (0, 0), width),
                    (mem, 0, back[g][i], (0, rows), width),
                ]
            )
        sections.append([(dbranch, 0, att[g], (0, 0), width)])
        grads[g] = weight_grads(
            scalars, sections, share, model, "attention_grads", deps=deps, gates=gates
        )

    far_back("oth", dbranch)
    near_back("oth")
    group_grads("oth")
    cross = trade(grads["oth"][0])
    far_back("own", grads["oth"][1])
    (lo_own,) = add((middle, ffn_own, ffn_got), 1, "layer_sum", deps=(back["own"][3],))
    (cross,) = add((cross,), 1, "cross_sum", deps=(lo_own,))
    cross_got = swap(cross, "head")
    halo_part, back4, back3, back2 = spread(
        back["oth"][1], back["oth"][2], back["own"][1], back["own"][2], weights["oth"], w_qkv,
        slots, padded, deps=(cross,),
    )
    slot_gots = [
        shift(part, "blk", -lag)
        for part, lag in zip((back4, back3, back2), range(CSEGS + 1, 1, -1))
    ]
    near_back("own", halo_part)
    group_grads("own")
    own = trade(grads["own"][0])
    base_oth = base_rows(
        near["oth"][:3], rec["oth"][4:6], weights["oth"], [], deps=(grads["own"][1],)
    )
    base, slot_base = base_rows(near["own"][:3], rec["own"][4:6], w_qkv, base_oth)
    wide = 2 * width
    late_qk = Halving([(own, 0, 0), (own, 0, 1), (cross_got, 0)], wide, rising, position)
    late_vo = Halving([(own, wide, 0), (own, wide, 1), (cross_got, wide)], wide, falling, position)
    moved = late_qk.step(base)
    moved = late_vo.step(moved)
    dpacked, dp_mine, dp_away, bias_sum, halo_part, lo_own = packed_back(
        me_arg, slot_base, slot_gots, deps=(moved,), gates=(halo_part, lo_own)
    )
    dp_got = swap(dp_away, "head")
    halo_back = shift(halo_part, "blk", -1)
    lo_got = swap(lo_own, "head")
    send, token = weight_grads(
        scalars,
        [
            [
                (tri_own, tap * model, dp_mine, (0, 0), half),
                (tri_oth, tap * model, dp_got, (0, 0), half),
            ]
            for tap in range(3)
        ],
        share, model, "pack_grads",
    )
    comp = trade(send)
    comp = Halving([(comp, 0, 0), (comp, 0, 1)], 3 * half, falling, position)
    moved = comp.step(token)
    moved = late_qk.step(moved)
    moved = late_vo.step(moved)
    grad_own, sums1 = finish(
        me_arg, base, halo_back, dpacked, w_comp, tokens, dbranch, norm1_gain,
        deps=(recon_got, moved),
    )
    dslopes = {}
    for g in groups:
        total = back[g][3] + near[g][3]
        dslopes[g] = -jnp.sum(total[:, 2] - total[:, 0] * total[:, 1], axis=1)
    both = in_order(me, dslopes["own"], dslopes["oth"], 0)
    vector = jnp.concatenate(
        [sums1[0], sums1[1], sums2[0], sums2[1], bias_sum[0], jnp.pad(both, (0, 128 - 2 * heads))]
    ).reshape(-1, 128)
    rounds = butterfly_steps()
    vector_got = swap(vector, *rounds.pop(0))
    moved, grad_away = comp.step(sums1, gates=(grad_own,))
    grad_got = swap(grad_away, "head")
    vector = butterfly_add(vector, vector_got, deps=(moved,))
    vector_got = swap(vector, *rounds.pop(0))
    moved = vector
    while late_qk.order or comp.order:
        if late_qk.order:
            moved = late_qk.step(moved)
            moved = late_vo.step(moved)
        if comp.order:
            moved = comp.step(moved)
        vector = butterfly_add(vector, vector_got, deps=(moved,))
        vector_got = swap(vector, *rounds.pop(0))
        moved = vector
    late_qk = late_qk.last(moved)
    late_vo = late_vo.last(late_qk)
    while len(rounds) > 1:
        vector = butterfly_add(vector, vector_got, deps=(late_vo,))
        vector_got = swap(vector, *rounds.pop(0))
    vector = butterfly_add(vector, vector_got, deps=(late_vo,))
    vector_got = swap(vector, *rounds.pop(0))
    comp = comp.last(vector)
    vector = (vector + vector_got).reshape(-1)
    comp = comp.astype(BF)
    comp_got = swap(comp, "head")
    comp_all = in_order(
        me, comp.reshape(share, 3, half), comp_got.reshape(share, 3, half), 2
    ).astype(F32)

    slope_sum = lax.dynamic_slice_in_dim(vector, 5 * model + me * heads, heads, 0)

    recon_own = rec["own"][0].reshape(heads, rows)
    recon = in_order(me, recon_own[None], recon_got[None], 0)
    layer_out = in_order(me, lo_own[None], lo_got[None], 0)
    grad_tokens = in_order(me, grad_own[None], grad_got[None], 0)
    late = jnp.concatenate([late_qk, late_vo], 1)
    return (
        layer_out,
        recon,
        grad_tokens,
        jnp.transpose(late[:, : 3 * width].reshape(share, 3, width), (1, 0, 2)),
        late[:, 3 * width :].T,
        slope_sum,
        up_down[:, :units].astype(F32),
        up_down[:, units:].astype(F32).T,
        jnp.transpose(comp_all, (1, 0, 2)),
        vector[4 * model : 5 * model],
        vector[:model],
        vector[model : 2 * model],
        vector[2 * model : 3 * model],
        vector[3 * model : 4 * model],
    )


def solution(mesh):
    in_specs = (
        P("dp", "blk", None),
        P("dp", None),
        P(None, None, "head"),
        P("head", None),
        P("head"),
        P(None, "head"),
        P("head", None),
        P(),
        P(),
        P(),
        P(),
        P(),
        P(),
        P("dp", "blk", None),
        P("dp", "head", "blk"),
    )
    out_specs = (
        P("dp", "blk", None),
        P("dp", "head", "blk"),
        P("dp", "blk", None),
        P(None, ("blk", "dp"), "head"),
        P("head", ("blk", "dp")),
        P("head"),
        P(("blk", "dp"), "head"),
        P("head", ("blk", "dp")),
        P(None, ("blk", "dp"), None),
        P(),
        P(),
        P(),
        P(),
        P(),
    )
    return jax.shard_map(shards, mesh=mesh, in_specs=in_specs, out_specs=out_specs, check_vma=False)
```

```python
import functools
import math

import jax
import jax.numpy as jnp
from jax import lax
from jax.experimental import pallas as pl
from jax.experimental.pallas import tpu as pltpu
from jax.sharding import PartitionSpec as P

CSEGS = 3
EPS = 1e-05
FAR = 1e30
LOG2E = math.log2(math.e)
BF = jnp.bfloat16
F32 = jnp.float32
TILE = 256
SHARE = 1 << 24
TAIL = 1.0


LIMITS = {"recon_both": 10.3, "mlp": 20.7, "mlp_grads": 27.7, "branches": 23.3, "turn": 17.4, "attention_grads": 26.4, "spread": 17.4, "pack_grads": 19.1, "finish": 21.1}


def limit(name):
    return int(LIMITS.get(name, 14.0) * (1 << 20))


def cost(us):
    return pl.CostEstimate(flops=int(us * SHARE), bytes_accessed=1 << 10, transcendentals=0)

NT = (((1,), (1,)), ((), ()))
GELU_A = math.sqrt(2.0 / math.pi)
GELU_B = 0.044715


def dot(a, b):
    return jnp.dot(a, b, preferred_element_type=F32)


def dot_nt(a, b):
    return lax.dot_general(a, b, NT, preferred_element_type=F32)


def dot_tn(a, b):
    return lax.dot_general(a, b, (((0,), (0,)), ((), ())), preferred_element_type=F32)


def shift(x, axis, by):
    devices = lax.axis_size(axis)
    pairs = [(i, i + by) for i in range(devices) if 0 <= i + by < devices]
    return lax.ppermute(x, axis, pairs)


def trade(x):
    return lax.all_to_all(x, "dp", 0, 0)


def swap(x, axis, step=1):
    devices = lax.axis_size(axis)
    return lax.ppermute(x, axis, [(i, i ^ step) for i in range(devices)])


def call(
    kernel, deps=(), gates=(), prefetch=0, in_specs=None, from_hbm=False, to_hbm=False, **rest
):
    def run(*operands):
        count = len(operands)
        if from_hbm:
            operands = operands[:prefetch] + tuple(
                pltpu.with_memory_space_constraint(x, pltpu.HBM)
                if spec.memory_space is None else x
                for x, spec in zip(operands[prefetch:], in_specs)
            )
        passed = len(deps) + len(gates)
        specs = in_specs or [pl.BlockSpec(memory_space=pltpu.VMEM)] * count
        far = pl.BlockSpec(memory_space=pltpu.HBM)
        specs = list(specs) + [far] * passed

        def body(*refs):
            refs = refs[:count] + refs[count + passed :]
            results = count + len(rest_out)
            kernel(*refs[:results], *refs[results + len(gates) :])

        rest_out = list(rest["out_shape"])
        if to_hbm:
            rest_out = [pltpu.HBM(x.shape, x.dtype) for x in rest_out]
        settings = dict(rest)
        settings["out_shape"] = rest_out + [jax.ShapeDtypeStruct(g.shape, g.dtype) for g in gates]
        if gates:
            plain = [pl.BlockSpec(memory_space=pltpu.VMEM)] * len(rest_out)
            settings["out_specs"] = list(rest.get("out_specs", plain)) + [far] * len(gates)
            settings["input_output_aliases"] = {
                count + len(deps) + i: len(rest_out) + i for i in range(len(gates))
            }
        if prefetch:
            grid = {
                key: settings.pop(key)
                for key in ("grid", "out_specs", "scratch_shapes") if key in settings
            }
            settings["grid_spec"] = pltpu.PrefetchScalarGridSpec(
                num_scalar_prefetch=prefetch, in_specs=specs, **grid
            )
        else:
            settings["in_specs"] = specs
        return pl.pallas_call(body, **settings)(*operands, *deps, *gates)

    return run


def still(shape, index_map):
    return pl.BlockSpec(shape, index_map, pipeline_mode=pl.Buffered(1))


def row_stats(x):
    center = x - jnp.mean(x, axis=-1, keepdims=True)
    inverse = lax.rsqrt(jnp.mean(center * center, axis=-1, keepdims=True) + EPS)
    return center * inverse, inverse


def norm_back(grad, unit, inverse, gain):
    scaled = grad * gain
    mean_one = jnp.mean(scaled, axis=-1, keepdims=True)
    mean_two = jnp.mean(scaled * unit, axis=-1, keepdims=True)
    return inverse * (scaled - mean_one - unit * mean_two)


def front_kernel(me, own, other, gain, bias, normed, tri_own, tri_other, unit, *, slots):
    rows, model = own.shape
    padded = tri_own.shape[0]
    for source, tri in ((own, tri_own), (other, tri_other)):
        for start in range(0, rows, 128):
            part = slice(start, start + 128)
            x, _ = row_stats(source[part, :].astype(F32))
            x = x * gain[...] + bias[...]
            for lane in range(model // 128):
                unit[lane, part, :] = x[:, lane * 128 : (lane + 1) * 128]
            if source is own:
                normed[part, :] = x.astype(BF)
        live = lax.broadcasted_iota(jnp.int32, (padded, 128), 0) < slots
        for lane in range(model // 128):
            unit[lane, rows:, :] = jnp.zeros((unit.shape[1] - rows, 128), F32)
            for tap in range(3):
                at = tap * model + lane * 128
                rows_of = unit[lane, pl.ds(tap, padded, stride=3), :]
                tri[:, at : at + 128] = jnp.where(live, rows_of, 0.0).astype(BF)


def front(me, tokens, gain, bias, slots, padded, deps=(), gates=()):
    _, rows, model = tokens.shape
    tri = jax.ShapeDtypeStruct((padded, 3 * model), BF)
    fixed = lambda shape: still(shape, lambda i, m: (0, 0))
    pick = lambda turn: still((None, rows, model), lambda i, m: ((m[0] + turn) % 2, 0, 0))
    return call(
        functools.partial(front_kernel, slots=slots),
        deps=deps,
        gates=gates,
        **dict(
            prefetch=1,
            grid=(1,),
            in_specs=[pick(0), pick(1), fixed((1, model)), fixed((1, model))],
            out_specs=[fixed((rows, model)), fixed((padded, 3 * model)), fixed((padded, 3 * model))],
            scratch_shapes=[pltpu.VMEM((model // 128, 3 * padded + 8, 128), F32)],
        ),
        out_shape=[jax.ShapeDtypeStruct((rows, model), BF), tri, tri],
        compiler_params=pltpu.CompilerParams(vmem_limit_bytes=limit("front")),
        cost_estimate=cost(0.02),
        name="front",
    )(me, tokens, tokens, gain.reshape(1, model), bias.reshape(1, model))


def norm_kernel(rows, gain, bias, normed):
    unit, _ = row_stats(rows[...].astype(F32))
    normed[...] = (unit * gain[...] + bias[...]).astype(BF)


def norm_halo(rows, gain, bias, deps=(), gates=()):
    count, model = rows.shape
    tall = pl.BlockSpec((TILE, model), lambda i: (i, 0))
    fixed = pl.BlockSpec((1, model), lambda i: (0, 0))
    return call(
        norm_kernel,
        deps=deps,
        gates=gates,
        grid=(count // TILE,),
        in_specs=[tall, fixed, fixed],
        out_specs=[tall],
        out_shape=[jax.ShapeDtypeStruct((count, model), BF)],
        compiler_params=pltpu.CompilerParams(vmem_limit_bytes=limit("norm_halo")),
        cost_estimate=cost(2),
        name="norm_halo",
    )(rows, gain.reshape(1, model), bias.reshape(1, model))


def distant_kernel(halo, mem, w, kf, vf):
    rows = halo.shape[0]
    for index, out in ((1, kf), (2, vf)):
        out[:rows, :] = dot(halo[...], w[index]).astype(BF)
        out[rows:, :] = dot(mem[...], w[index]).astype(BF)


def project_distant(halo, mem, w, deps=(), gates=()):
    rows, model = halo.shape
    width = w.shape[2]
    shape = jax.ShapeDtypeStruct((2 * rows, width), BF)
    return call(
        distant_kernel,
        deps=deps,
        gates=gates,
        out_shape=[shape, shape],
        compiler_params=pltpu.CompilerParams(vmem_limit_bytes=limit("project_distant")),
        cost_estimate=cost(2.1),
        name="project_distant",
    )(halo, mem, w)


def far_kernel(place, docs, query, out, mem, *, slots, rows):
    position = place[0]
    for seg in range(CSEGS):
        mem[seg * slots : (seg + 1) * slots, :] = docs[pl.ds(seg * rows, slots, stride=3), :]
    mem[CSEGS * slots :, :] = jnp.full((rows - CSEGS * slots, 128), -1, jnp.int32)
    column = lax.broadcasted_iota(jnp.int32, (1, rows), 1)
    step = 64
    for start in range(0, 3 * rows, step):
        local = lax.broadcasted_iota(jnp.int32, (step, 1), 0) + start % rows
        if start < rows:
            doc = docs[CSEGS * rows + start : CSEGS * rows + start + step, :1]
            where, live = local - rows, position > 0
        elif start < 2 * rows:
            doc = mem[start - rows : start - rows + step, :1]
            lead = sum((local >= seg * slots).astype(jnp.int32) for seg in range(1, CSEGS + 1))
            where = (lead - 1 - CSEGS) * rows + 3 * (local - lead * slots) + 1
            live = position - 1 - CSEGS + lead >= 0
        else:
            at = (CSEGS + 1) * rows + start - 2 * rows
            doc = docs[at : at + step, :1]
            where, live = local, position >= 0
        doc = jnp.where(live, doc, -2)
        apart = column - where
        seen = (apart >= 0) & (doc == query[...])
        value = jnp.log((1 + jnp.maximum(apart, 0)).astype(F32))
        out[start : start + step, :] = jnp.where(seen, value, FAR)


def far_log(place, docs, query, slots, deps=(), gates=()):
    rows = query.shape[1]
    return call(
        functools.partial(far_kernel, slots=slots, rows=rows),
        deps=deps,
        gates=gates,
        in_specs=[
            pl.BlockSpec(memory_space=pltpu.SMEM),
            pl.BlockSpec(memory_space=pltpu.VMEM),
            pl.BlockSpec(memory_space=pltpu.VMEM),
        ],
        out_shape=[jax.ShapeDtypeStruct((3 * rows, rows), F32)],
        scratch_shapes=[pltpu.VMEM((rows, 128), jnp.int32)],
        compiler_params=pltpu.CompilerParams(vmem_limit_bytes=limit("far_log")),
        cost_estimate=cost(0.02),
        name="far_log",
    )(place, docs, query)


def project_kernel(normed, packed, w, q, k, v, kc, vc):
    for index, out in enumerate((q, k, v)):
        out[...] = dot(normed[...], w[index]).astype(BF)
    kc[...] = dot(packed[...], w[1]).astype(BF)
    vc[...] = dot(packed[...], w[2]).astype(BF)


def project(normed, packed, w, deps=(), gates=()):
    rows, model = normed.shape
    padded, width = packed.shape[0], w.shape[2]
    near = jax.ShapeDtypeStruct((rows, width), BF)
    little = jax.ShapeDtypeStruct((padded, width), BF)
    return call(
        project_kernel,
        deps=deps,
        gates=gates,
        out_shape=[near, near, near, little, little],
        compiler_params=pltpu.CompilerParams(vmem_limit_bytes=limit("project")),
        cost_estimate=cost(2.0),
        name="project",
    )(normed, packed, w)


def forward_kernel(slopes, q, kf, vf, ko, vo, far, out, lse, *, scaling):
    head = pl.program_id(0)
    c1 = scaling * LOG2E
    c2 = slopes[head] * LOG2E
    rows, reach = q.shape[0], kf.shape[0]
    vft, vot = vf[...].T, vo[...].T
    for qi in range(rows // TILE):
        qs = slice(qi * TILE, (qi + 1) * TILE)
        until = (qi + 1) * TILE
        qb = q[qs, :]
        near = dot_nt(ko[:until, :], qb) * c1 - c2 * far[reach : reach + until, qs]
        away = dot_nt(kf[...], qb) * c1 - c2 * far[:reach, qs]
        top = jnp.maximum(
            jnp.max(near, axis=0, keepdims=True), jnp.max(away, axis=0, keepdims=True)
        )
        near = jnp.exp2(near - top)
        away = jnp.exp2(away - top)
        total = jnp.sum(near, axis=0, keepdims=True) + jnp.sum(away, axis=0, keepdims=True)
        mixed = dot(vot[:, :until], near.astype(BF)) + dot(vft, away.astype(BF))
        out[qs, :] = (mixed / total).T.astype(BF)
        lse[0, :, qs] = top + jnp.log2(total)


def attend_forward(slopes, q, kf, vf, ko, vo, far, scaling, deps=(), gates=()):
    rows, width = q.shape
    reach = kf.shape[0]
    heads = slopes.shape[0]
    hd = width // heads
    near = pl.BlockSpec((rows, hd), lambda h: (0, h))
    wide = pl.BlockSpec((reach, hd), lambda h: (0, h))
    return call(
        functools.partial(forward_kernel, scaling=scaling),
        deps=deps,
        gates=gates,
        grid=(heads,),
        in_specs=[
            pl.BlockSpec(memory_space=pltpu.SMEM), near, wide, wide, near, near,
            still((reach + rows, rows), lambda h: (0, 0)),
        ],
        out_specs=[near, pl.BlockSpec((1, 1, rows), lambda h: (h, 0, 0))],
        out_shape=[
            jax.ShapeDtypeStruct((rows, width), BF),
            jax.ShapeDtypeStruct((heads, 1, rows), F32),
        ],
        compiler_params=pltpu.CompilerParams(vmem_limit_bytes=limit("attend_forward")),
        cost_estimate=cost(3.2),
        name="attend_forward",
    )(slopes, q, kf, vf, ko, vo, far)


def backward_kernel(slopes, q, do, lse, dot_row, far, k, v, *refs, scaling, own):
    head = pl.program_id(0)
    c1 = scaling * LOG2E
    c2 = slopes[head] * LOG2E
    extras = refs[:-4]
    dq, dk_out, dv_out, sums_out = refs[-4:]
    rows, hd = q.shape
    keys = k.shape[0]
    tall = rows
    dqs = [None] * (rows // TILE)
    for ki in range(keys // tall):
        base = ki * tall
        kt = k[base : base + tall, :].T
        dks, dvs = [], []
        for qi in range(rows // TILE):
            qs = slice(qi * TILE, (qi + 1) * TILE)
            until = (qi + 1) * TILE if own else tall
            ks = slice(base, base + until)
            qb, db = q[qs, :], do[qs, :]
            dist = far[ks, qs]
            s = dot_nt(k[ks, :], qb) * c1 - c2 * dist
            p = jnp.exp2(s - lse[0, :, qs])
            dp = dot_nt(v[ks, :], db)
            ds = p * (dp - dot_row[0, :, qs])
            for index, value in enumerate((ds, p * dist, ds * dist)):
                value = jnp.sum(value, axis=0, keepdims=True)
                if ki > 0:
                    value = value + sums_out[0, index : index + 1, qs]
                sums_out[0, index : index + 1, qs] = value
            p = p.astype(BF)
            ds = ds.astype(BF)
            dvs.append(dot(p, db))
            dks.append(dot(ds, qb))
            value = dot(kt[:, :until], ds)
            if ki > 0:
                value = value + dqs[qi]
            dqs[qi] = value
            if ki == keys // tall - 1:
                value = value.T * scaling
                if own:
                    value = value + extras[0][qs, :].astype(F32) + extras[1][qs, :].astype(F32)
                dq[qs, :] = value.astype(BF)
        for start in range(0, tall, TILE):
            ks = slice(base + start, base + start + TILE)
            dk = sum(d[start : start + TILE, :] for d in dks if d.shape[0] > start) * scaling
            dv = sum(d[start : start + TILE, :] for d in dvs if d.shape[0] > start)
            if own:
                dk = dk + extras[2][ks, :].astype(F32)
                dv = dv + extras[3][ks, :].astype(F32)
            dk_out[ks, :] = dk.astype(BF)
            dv_out[ks, :] = dv.astype(BF)


def attend_backward(
    slopes, q, do, lse, dot_row, far, k, v, own, extras, scaling, deps=(), gates=(), late=False
):
    rows, width = q.shape
    keys = k.shape[0]
    heads = slopes.shape[0]
    hd = width // heads
    near = pl.BlockSpec((rows, hd), lambda h: (0, h))
    wide = pl.BlockSpec((keys, hd), lambda h: (0, h))
    lane = pl.BlockSpec((1, 1, rows), lambda h: (h, 0, 0))
    place = far.shape[0] // keys - 1 if own else 0
    return call(
        functools.partial(backward_kernel, scaling=scaling, own=own),
        deps=deps,
        gates=gates,
        grid=(heads,),
        in_specs=[
            pl.BlockSpec(memory_space=pltpu.SMEM), near, near, lane, lane,
            still((keys, rows), lambda h: (place, 0)), wide, wide,
        ]
        + [near] * len(extras),
        out_specs=[near, wide, wide, pl.BlockSpec((1, 8, rows), lambda h: (h, 0, 0))],
        out_shape=[
            jax.ShapeDtypeStruct((rows, width), BF),
            jax.ShapeDtypeStruct((keys, width), BF),
            jax.ShapeDtypeStruct((keys, width), BF),
            jax.ShapeDtypeStruct((heads, 8, rows), F32),
        ],
        compiler_params=pltpu.CompilerParams(vmem_limit_bytes=limit("far" if not own else "own")),
        cost_estimate=cost(TAIL * (5 if own else 9)),
        from_hbm=late,
        name="attend_backward_own" if own else "attend_backward_far",
    )(slopes, q, do, lse, dot_row, far, k, v, *extras)


def recon_kernel(q, ko, vo, kc, vc, cot, recon, dq, dk, dv, dkc, dvc, *, slots, scaling):
    rows, hd = q.shape
    c1 = scaling * LOG2E
    comp_rows = kc.shape[0]
    live = lax.broadcasted_iota(jnp.int32, (comp_rows, TILE), 0) < slots
    kct, vct, kot, vot = kc[...].T, vc[...].T, ko[...].T, vo[...].T
    for qi in range(rows // TILE):
        qs = slice(qi * TILE, (qi + 1) * TILE)
        qb = q[qs, :]
        full_s = dot_nt(ko[...], qb) * c1
        full_p = jnp.exp2(full_s - jnp.max(full_s, axis=0, keepdims=True))
        full_p = full_p * (1.0 / jnp.sum(full_p, axis=0, keepdims=True))
        full_low = full_p.astype(BF)
        comp_s = jnp.where(live, dot_nt(kc[...], qb) * c1, -FAR)
        comp_p = jnp.exp2(comp_s - jnp.max(comp_s, axis=0, keepdims=True))
        comp_p = comp_p * (1.0 / jnp.sum(comp_p, axis=0, keepdims=True))
        comp_low = comp_p.astype(BF)
        full, comp = dot(vot, full_low), dot(vct, comp_low)
        spread = full - comp
        recon[0, :, qs] = jnp.sum(spread * spread, axis=0, keepdims=True) / hd**0.5
        dfull = spread * (cot[0, :, qs] * (2.0 / hd**0.5))
        dfull_low = dfull.astype(BF)
        dfull_rows = dfull_low.T
        full_dw = dot(vo[...], dfull_low)
        comp_dw = dot(vc[...], dfull_low)
        row = jnp.sum(full_p * full_dw, axis=0, keepdims=True)
        full_ds = (full_p * (full_dw - row)).astype(BF)
        row = jnp.sum(comp_p * comp_dw, axis=0, keepdims=True)
        comp_ds = (comp_p * (row - comp_dw)).astype(BF)
        dq[qs, :] = ((dot(kot, full_ds) + dot(kct, comp_ds)).T * scaling).astype(BF)
        terms = (
            dot(full_ds, qb) * scaling, dot(full_low, dfull_rows),
            dot(comp_ds, qb) * scaling, -dot(comp_low, dfull_rows),
        )
        values = terms if qi == 0 else [a + b for a, b in zip(values, terms)]
    for ref, value in zip((dk, dv, dkc, dvc), values):
        ref[...] = value.astype(ref.dtype)


def recon_both(q, ko, vo, kc, vc, cot, slots, scaling, deps=(), gates=()):
    rows, width = q.shape
    heads = cot.shape[0]
    hd = width // heads
    comp_rows = kc.shape[0]
    near = pl.BlockSpec((rows, hd), lambda h: (0, h))
    small = pl.BlockSpec((comp_rows, hd), lambda h: (0, h))
    lane = pl.BlockSpec((1, 1, rows), lambda h: (h, 0, 0))
    big = jax.ShapeDtypeStruct((rows, width), BF)
    little = jax.ShapeDtypeStruct((comp_rows, width), BF)
    return call(
        functools.partial(recon_kernel, slots=slots, scaling=scaling),
        deps=deps,
        gates=gates,
        grid=(heads,),
        in_specs=[near, near, near, small, small, lane],
        out_specs=[lane, near, near, near, small, small],
        out_shape=[jax.ShapeDtypeStruct((heads, 1, rows), F32), big, big, big, little, little],
        compiler_params=pltpu.CompilerParams(vmem_limit_bytes=limit("recon_both")),
        cost_estimate=cost(4.3),
        to_hbm=True,
        name="recon_both",
    )(q, ko, vo, kc, vc, cot)


def middle_kernel(me, tokens, a_one, a_two, w_one, w_two, gain, bias, middle, normed):
    value = tokens[...].astype(F32) + (dot(a_one[...], w_one[...]) + dot(a_two[...], w_two[...]))
    middle[...] = value
    unit, _ = row_stats(value)
    normed[...] = (unit * gain[...] + bias[...]).astype(BF)


def middle_norm(me, tokens, a_one, a_two, w_one, w_two, gain, bias, deps=(), gates=()):
    _, rows, model = tokens.shape
    width = a_one.shape[1]
    tall = pl.BlockSpec((TILE, model), lambda i, m: (i, 0))
    part = pl.BlockSpec((TILE, width), lambda i, m: (i, 0))
    fixed = lambda shape: still(shape, lambda i, m: (0, 0))
    return call(
        middle_kernel,
        deps=deps,
        gates=gates,
        **dict(
            prefetch=1,
            grid=(rows // TILE,),
            in_specs=[pl.BlockSpec((None, TILE, model), lambda i, m: (m[0], i, 0)), part, part,
                      fixed((width, model)), fixed((width, model)), fixed((1, model)),
                      fixed((1, model))],
            out_specs=[tall, tall],
        ),
        out_shape=[jax.ShapeDtypeStruct((rows, model), F32), jax.ShapeDtypeStruct((rows, model), BF)],
        compiler_params=pltpu.CompilerParams(vmem_limit_bytes=limit("middle_norm")),
        cost_estimate=cost(1.1),
        name="middle_norm",
    )(me, tokens, a_one, a_two, w_one, w_two, gain.reshape(1, model), bias.reshape(1, model))


def mlp_kernel(which, normed, cot, w_up, w_down, hidden, dinner, dnormed, dn_sum):
    step = pl.program_id(0)
    inner = dot(normed[...], w_up[...])
    dhidden = dot_nt(cot[...], w_down[...])
    square = inner * inner
    inside = jnp.tanh(inner * (GELU_A + (GELU_A * GELU_B) * square))
    bent = 0.5 * (1.0 + inside)
    hidden[...] = (inner * bent).astype(BF)
    slope = bent + inner * (0.5 - 0.5 * inside * inside) * (
        GELU_A + (3.0 * GELU_A * GELU_B) * square
    )
    dlow = (dhidden * slope).astype(BF)
    dinner[...] = dlow
    dn = dot_nt(dlow, w_up[...])

    @pl.when(step == 0)
    def _():
        dn_sum[...] = dn

    @pl.when(step > 0)
    def _():
        dn_sum[...] += dn

    @pl.when(step == pl.num_programs(0) - 1)
    def _():
        dnormed[...] = dn_sum[...].astype(dnormed.dtype)


def mlp(which, normed, cot, w_up, w_down, dtype, deps=(), gates=()):
    rows, model = normed.shape
    units = w_up.shape[1]
    step = 512
    tall = still((rows, model), lambda f, m: (0, 0))
    act = pl.BlockSpec((rows, step), lambda f, m: (0, f))
    return call(
        mlp_kernel,
        deps=deps,
        gates=gates,
        **dict(
            prefetch=1,
            grid=(units // step,),
            in_specs=[tall, still((None, rows, model), lambda f, m: (m[0], 0, 0)),
                      pl.BlockSpec((model, step), lambda f, m: (0, f)),
                      pl.BlockSpec((step, model), lambda f, m: (f, 0))],
            out_specs=[act, act, tall],
            scratch_shapes=[pltpu.VMEM((rows, model), F32)],
        ),
        out_shape=[jax.ShapeDtypeStruct((rows, units), BF)] * 2
        + [jax.ShapeDtypeStruct((rows, model), dtype)],
        compiler_params=pltpu.CompilerParams(vmem_limit_bytes=limit("mlp")),
        cost_estimate=cost(6.4),
        name="mlp",
    )(which, normed, cot, w_up, w_down)


def branch_kernel(own, oth, w_down, out_own, out_oth, sum_own, sum_oth):
    step = pl.program_id(0)
    for source, total, out in ((own, sum_own, out_own), (oth, sum_oth, out_oth)):
        part = dot(source[...], w_down[...])

        @pl.when(step == 0)
        def _():
            total[...] = part

        @pl.when(step > 0)
        def _():
            total[...] += part

        @pl.when(step == pl.num_programs(0) - 1)
        def _():
            out[...] = total[...].astype(out.dtype)


def branches(own, oth, w_down, deps=(), gates=()):
    rows, units = own.shape
    model = w_down.shape[1]
    step = 512
    tall = still((rows, model), lambda f: (0, 0))
    act = pl.BlockSpec((rows, step), lambda f: (0, f))
    return call(
        branch_kernel,
        deps=deps,
        gates=gates,
        grid=(units // step,),
        in_specs=[act, act, pl.BlockSpec((step, model), lambda f: (f, 0))],
        out_specs=[tall, tall],
        out_shape=[jax.ShapeDtypeStruct((rows, model), BF)] * 2,
        scratch_shapes=[pltpu.VMEM((rows, model), F32)] * 2,
        compiler_params=pltpu.CompilerParams(vmem_limit_bytes=limit("branches")),
        cost_estimate=cost(TAIL * 6),
        from_hbm=True,
        name="branches",
    )(own, oth, w_down)


def turn_kernel(
    me, dn_own, dn_got, middle, cot, a_one, a_two, w_one, w_two, gain,
    dbranch, da_one, da_two, row_one, row_two, sums,
):
    step = pl.program_id(0)
    dn = dn_own[...].astype(F32) + dn_got[...].astype(F32)
    unit, inverse = row_stats(middle[...])
    value = cot[...].astype(F32) + norm_back(dn, unit, inverse, gain[...])
    low = value.astype(BF)
    dbranch[...] = low
    for a, w, da, row in ((a_one, w_one, da_one, row_one), (a_two, w_two, da_two, row_two)):
        grad = dot_nt(low, w[...]).astype(BF)
        da[...] = grad
        product = (grad.astype(F32) * a[...].astype(F32)).T
        heads = row.shape[0]
        row[:, 0, :] = jnp.sum(product.reshape(heads, -1, TILE), axis=1)

    @pl.when(step == 0)
    def _():
        sums[...] = jnp.zeros_like(sums)

    sums[0:1, :] += jnp.sum(dn * unit, axis=0, keepdims=True)
    sums[1:2, :] += jnp.sum(dn, axis=0, keepdims=True)


def turn(me, dn_own, dn_got, middle, cot, a_one, a_two, w_one, w_two, gain, heads, deps=(), gates=()):
    rows, model = middle.shape
    width = a_one.shape[1]
    tall = pl.BlockSpec((TILE, model), lambda i, m: (i, 0))
    part = pl.BlockSpec((TILE, width), lambda i, m: (i, 0))
    lane = pl.BlockSpec((heads, 1, TILE), lambda i, m: (0, 0, i))
    fixed = lambda shape: still(shape, lambda i, m: (0, 0))
    return call(
        turn_kernel,
        deps=deps,
        gates=gates,
        **dict(
            prefetch=1,
            grid=(rows // TILE,),
            in_specs=[tall, tall, tall,
                      pl.BlockSpec((None, TILE, model), lambda i, m: (m[0], i, 0)),
                      part, part, fixed((width, model)), fixed((width, model)), fixed((1, model))],
            out_specs=[tall, part, part, lane, lane, fixed((8, model))],
        ),
        out_shape=[
            jax.ShapeDtypeStruct((rows, model), BF),
            jax.ShapeDtypeStruct((rows, width), BF),
            jax.ShapeDtypeStruct((rows, width), BF),
            jax.ShapeDtypeStruct((heads, 1, rows), F32),
            jax.ShapeDtypeStruct((heads, 1, rows), F32),
            jax.ShapeDtypeStruct((8, model), F32),
        ],
        compiler_params=pltpu.CompilerParams(vmem_limit_bytes=limit("turn")),
        cost_estimate=cost(TAIL * 5),
        name="turn",
    )(me, dn_own, dn_got, middle, cot, a_one, a_two, w_one, w_two, gain.reshape(1, model))


def spread_kernel(ka, va, kb, vb, wka, wva, wkb, wvb, near, four, three, two, held, *, slots):
    step = pl.program_id(0)
    value = dot_nt(ka[...], wka[...]) + dot_nt(va[...], wva[...])
    value = value + dot_nt(kb[...], wkb[...]) + dot_nt(vb[...], wvb[...])

    @pl.when(step == 0)
    def _():
        near[...] = value.astype(BF)

    @pl.when(step == 1)
    def _():
        rows = value.shape[0]
        held[:rows, :] = value
        held[rows:, :] = jnp.zeros((held.shape[0] - rows, value.shape[1]), F32)
        padded = four.shape[0]
        live = lax.broadcasted_iota(jnp.int32, four.shape, 0) < slots
        for index, out in enumerate((four, three, two)):
            part = held[index * slots : index * slots + padded, :]
            out[...] = jnp.where(live, part, 0.0).astype(BF)


def spread(ka, va, kb, vb, wa, wb, slots, padded, deps=(), gates=()):
    rows, width = ka.shape[0] // 2, ka.shape[1]
    model = wa.shape[1]
    part = pl.BlockSpec((rows, width), lambda i: (i, 0))
    weight = lambda t: still((None, model, width), lambda i: (t, 0, 0))
    fixed = lambda *shape: still(shape, lambda i: (0, 0))
    little = jax.ShapeDtypeStruct((padded, model), BF)
    return call(
        functools.partial(spread_kernel, slots=slots),
        deps=deps,
        gates=gates,
        grid=(2,),
        in_specs=[part] * 4 + [weight(1), weight(2)] * 2,
        out_specs=[fixed(rows, model)] + [fixed(padded, model)] * 3,
        out_shape=[jax.ShapeDtypeStruct((rows, model), BF), little, little, little],
        scratch_shapes=[pltpu.VMEM((rows + 16, model), F32)],
        compiler_params=pltpu.CompilerParams(vmem_limit_bytes=limit("spread")),
        cost_estimate=cost(TAIL * 6),
        name="spread",
    )(ka, va, kb, vb, wa, wa, wb, wb)


def base_kernel(q, k, v, kc, vc, w, *refs, more):
    before, slot_before = refs[:2] if more else (None, None)
    base, slot_base, total, slot_total = refs[-4:]
    step = pl.program_id(0)
    for index, part in enumerate((q, k, v)):

        @pl.when(step == index)
        def _():
            value = dot_nt(part[...], w[...])
            if index > 0:
                value = value + total[...]
            elif more:
                value = value + before[...].astype(F32)
            if index == 2:
                base[...] = value.astype(BF)
            else:
                total[...] = value

    for index, part in enumerate((kc, vc)):

        @pl.when(step == index + 1)
        def _():
            value = dot_nt(part[...], w[...])
            if index > 0:
                value = value + slot_total[...]
            elif more:
                value = value + slot_before[...].astype(F32)
            if index == 1:
                slot_base[...] = value.astype(BF)
            else:
                slot_total[...] = value


def base_rows(near, slot, w, before, deps=(), gates=()):
    rows, width = near[0].shape
    padded = slot[0].shape[0]
    model = w.shape[1]
    fixed = lambda *shape: still(shape, lambda i: (0, 0))
    outs = [fixed(rows, model), fixed(padded, model)]
    return call(
        functools.partial(base_kernel, more=bool(before)),
        deps=deps,
        gates=gates,
        grid=(3,),
        in_specs=[fixed(rows, width)] * 3 + [fixed(padded, width)] * 2
        + [pl.BlockSpec((None, model, width), lambda i: (i, 0, 0))]
        + outs[: len(before)],
        out_specs=outs,
        out_shape=[
            jax.ShapeDtypeStruct((rows, model), BF),
            jax.ShapeDtypeStruct((padded, model), BF),
        ],
        scratch_shapes=[pltpu.VMEM((rows, model), F32), pltpu.VMEM((padded, model), F32)],
        compiler_params=pltpu.CompilerParams(vmem_limit_bytes=limit("base_rows")),
        cost_estimate=cost(TAIL * 3),
        from_hbm=True,
        name="base_rows",
    )(*near, *slot, w, *before)


def packed_kernel(me, base, *refs):
    gots, (dpacked, mine, away, bias) = refs[:-4], refs[-4:]
    value = sum(part[...].astype(F32) for part in (base, *gots)).astype(BF)
    dpacked[...] = value
    half = mine.shape[1]
    first, second = value[:, :half], value[:, half:]
    low = me[0] == 0
    mine[...] = jnp.where(low, first, second)
    away[...] = jnp.where(low, second, first)
    bias[0:1, :] = jnp.sum(value.astype(F32), axis=0, keepdims=True)


def packed_back(me, base, gots, deps=(), gates=()):
    padded, model = base.shape
    whole = pl.BlockSpec(memory_space=pltpu.VMEM)
    little = jax.ShapeDtypeStruct((padded, model // 2), BF)
    return call(
        packed_kernel,
        deps=deps,
        gates=gates,
        in_specs=[pl.BlockSpec(memory_space=pltpu.SMEM), whole] + [whole] * len(gots),
        out_shape=[jax.ShapeDtypeStruct((padded, model), BF), little, little,
                   jax.ShapeDtypeStruct((8, model), F32)],
        compiler_params=pltpu.CompilerParams(vmem_limit_bytes=limit("packed_back")),
        cost_estimate=cost(TAIL * 400),
        name="packed_back",
    )(me, base, *gots)


def finish_kernel(
    me, base, back, dpacked, w_comp, tokens, dmiddle, gain, grad, sums, total, *, rows
):
    model = base.shape[1]
    padded = dpacked.shape[0]
    for lane in range(model // 128):
        wide = slice(lane * 128, (lane + 1) * 128)
        total[lane, :rows, :] = base[:, wide].astype(F32) + back[:, wide].astype(F32)
        total[lane, rows:, :] = jnp.zeros((total.shape[1] - rows, 128), F32)
    for tap in range(3):
        place = pl.ds(tap, padded, stride=3)
        term = dot_nt(dpacked[...], w_comp[tap])
        for lane in range(model // 128):
            value = total[lane, place, :] + term[:, lane * 128 : (lane + 1) * 128]
            total[lane, place, :] = value
    one = jnp.zeros((1, model), F32)
    two = jnp.zeros((1, model), F32)
    for start in range(0, rows, 128):
        part = slice(start, start + 128)
        dn = jnp.concatenate([total[lane, part, :] for lane in range(model // 128)], 1)
        unit, inverse = row_stats(tokens[part, :].astype(F32))
        value = dmiddle[part, :].astype(F32) + norm_back(dn, unit, inverse, gain[...])
        grad[part, :] = value.astype(BF)
        one = one + jnp.sum(dn * unit, axis=0, keepdims=True)
        two = two + jnp.sum(dn, axis=0, keepdims=True)
    sums[0:1, :] = one
    sums[1:2, :] = two


def finish(me, base, back, dpacked, w_comp, tokens, dmiddle, gain, deps=(), gates=()):
    rows, model = base.shape
    padded = dpacked.shape[0]
    fixed = lambda *shape: still(shape, lambda i, m: (0,) * len(shape))
    return call(
        functools.partial(finish_kernel, rows=rows),
        deps=deps,
        gates=gates,
        **dict(
            prefetch=1,
            grid=(1,),
            in_specs=[fixed(rows, model), fixed(rows, model), fixed(padded, model),
                      fixed(*w_comp.shape),
                      still((None, rows, model), lambda i, m: (m[0], 0, 0)),
                      fixed(rows, model), fixed(1, model)],
            out_specs=[fixed(rows, model), fixed(8, model)],
            scratch_shapes=[pltpu.VMEM((model // 128, 3 * padded + 8, 128), F32)],
        ),
        out_shape=[
            jax.ShapeDtypeStruct((rows, model), BF),
            jax.ShapeDtypeStruct((8, model), F32),
        ],
        compiler_params=pltpu.CompilerParams(vmem_limit_bytes=limit("finish")),
        cost_estimate=cost(TAIL * 4),
        name="finish",
    )(me, base, back, dpacked, w_comp, tokens, dmiddle, gain.reshape(1, model))


def weight_kernel(core, *refs, plan, block, share):
    if share:
        operands, (parts, token, held) = refs[:-3], refs[-3:]
    else:
        operands, (held, token) = refs[:-2], refs[-2:]
    token[...] = jnp.zeros_like(token)
    tall = held.shape[0]
    at = 0
    for pairs, columns in plan:
        for start in range(0, columns, block):
            wide = slice(start, min(start + block, columns))
            value = None
            for a, b in pairs:
                term = lax.dot_general(
                    operands[a][...], operands[b][:, wide], (((0,), (0,)), ((), ())),
                    preferred_element_type=F32,
                )
                value = term if value is None else value + term
            held[:, at + start : at + wide.stop] = value.astype(BF)
        at += columns
    if not share:
        return
    for index in range(tall // (2 * share)):
        for side in range(2):
            here = (2 * index + side) * share
            parts[side, index * share : (index + 1) * share, :] = held[here : here + share, :]


def weight_grads(scalars, sections, share, model, name, tall=512, deps=(), gates=()):
    operands, specs, plan, total = [], [], [], 0
    known = {}

    def place(array, kind, at, columns, depth):
        key = (id(array), kind, at, columns)
        if key not in known:
            known[key] = len(operands)
            operands.append(array)
            if kind == "b":
                col, row = at
                spec = still(
                    (depth, columns), lambda i, c, f=col // columns, r=row // depth: (r, f)
                )
            elif array.ndim == 3:
                spec = pl.BlockSpec((None, depth, tall), lambda i, c, t=at: ((c[1] + t) % 2, 0, i))
            else:
                spec = pl.BlockSpec((depth, tall), lambda i, c, f=at // tall: (0, f + i))
            specs.append(spec)
        return known[key]

    for pairs in sections:
        columns = pairs[0][4]
        plan.append(
            (
                [
                    (
                        place(a, "a", pa, 0, a.shape[-2]),
                        place(b, "b", pb, columns, a.shape[-2]),
                    )
                    for a, pa, b, pb, _ in pairs
                ],
                columns,
            )
        )
        total += columns
    tile = tall // 2 if share else tall
    if share:
        out = [pl.BlockSpec((2, tile, total), lambda i, c: (0, i, 0))]
        shape = [jax.ShapeDtypeStruct((2, tile * (model // tall), total), BF)]
    else:
        out = [pl.BlockSpec((tile, total), lambda i, c: (i, 0))]
        shape = [jax.ShapeDtypeStruct((model, total), BF)]
    out.append(pl.BlockSpec((8, 128), lambda i, c: (0, 0)))
    shape.append(jax.ShapeDtypeStruct((8, 128), F32))
    flops = sum(2 * model * p[4] * p[0].shape[-2] for pairs in sections for p in pairs)
    return call(
        functools.partial(weight_kernel, plan=tuple(plan), block=512, share=share),
        deps=deps,
        gates=gates,
        **dict(
            prefetch=1,
            grid=(model // tall,),
            in_specs=specs,
            out_specs=out,
            scratch_shapes=[pltpu.VMEM((tall, total), BF)] if share else [],
        ),
        out_shape=shape,
        compiler_params=pltpu.CompilerParams(vmem_limit_bytes=limit(name)),
        cost_estimate=cost(TAIL * flops * 1.4e-9),
        to_hbm=True,
        name=name,
    )(scalars, *operands)


def sum_kernel(*refs, split):
    terms, outs = refs[:-split], refs[-split:]
    total = sum(term[...].astype(F32) for term in terms)
    wide = total.shape[1] // split
    for index, out in enumerate(outs):
        out[...] = total[:, index * wide : (index + 1) * wide].astype(out.dtype)


def add(terms, split, name, deps=(), gates=()):
    rows, columns = terms[0].shape[-2:]
    wide = columns // split
    tile = TILE if rows % TILE == 0 else rows
    blocks, operands = [], []
    for term in terms:
        if term.ndim == 3:
            for t in range(term.shape[0]):
                blocks.append(pl.BlockSpec((None, tile, columns), lambda i, t=t: (t, i, 0)))
                operands.append(term)
        else:
            blocks.append(pl.BlockSpec((tile, columns), lambda i: (i, 0)))
            operands.append(term)
    return call(
        functools.partial(sum_kernel, split=split),
        deps=deps,
        gates=gates,
        grid=(rows // tile,),
        in_specs=blocks,
        out_specs=[pl.BlockSpec((tile, wide), lambda i: (i, 0))] * split,
        out_shape=[jax.ShapeDtypeStruct((rows, wide), BF)] * split,
        compiler_params=pltpu.CompilerParams(vmem_limit_bytes=limit(name)),
        cost_estimate=cost(TAIL * 2),
        from_hbm=True,
        name=name,
    )(*operands)


def halve_kernel(bit, *refs, blocks, stride, terms):
    parts, outs = refs[:terms], refs[terms:]
    rows = parts[0].shape[0] // blocks
    mine = bit[0]
    if len(outs) == 1:
        outs[0][...] = sum(part[...].astype(F32) for part in parts).astype(outs[0].dtype)
        return
    for out, side in zip(outs, (mine, 1 - mine)):
        for j in range(blocks // 2):
            at = (j // stride * 2 * stride + j % stride) * rows + side * (stride * rows)
            place = pl.ds(pl.multiple_of(at, rows), rows)
            total = sum(part[place, :].astype(F32) for part in parts)
            out[j * rows : (j + 1) * rows, :] = total.astype(BF)


def halve(bit, parts, blocks, stride, columns, deps=(), gates=()):
    rows = parts[0][0].shape[-2]
    last = blocks == 1
    shape = jax.ShapeDtypeStruct((rows if last else rows // 2, columns), F32 if last else BF)
    return call(
        functools.partial(halve_kernel, blocks=blocks, stride=stride, terms=len(parts)),
        deps=deps,
        gates=gates,
        **dict(
            prefetch=1,
            grid=(1,),
            in_specs=[
                still((rows, columns), lambda i, m, f=part[1] // columns: (0, f))
                if len(part) == 2
                else still(
                    (None, rows, columns), lambda i, m, f=part[1] // columns, t=part[2]: (t, 0, f)
                )
                for part in parts
            ],
            out_specs=[still(shape.shape, lambda i, m: (0, 0))] * (1 if last else 2),
        ),
        out_shape=[shape] * (1 if last else 2),
        compiler_params=pltpu.CompilerParams(vmem_limit_bytes=limit("halve")),
        cost_estimate=cost(TAIL * 3),
        name="halve",
    )(bit, *[part[0] for part in parts])


class Halving:
    def __init__(self, parts, columns, order, position):
        self.parts, self.columns, self.order = parts, columns, list(order)
        self.position = position
        self.blocks = lax.axis_size("blk")
        self.left = list(range(self.blocks.bit_length() - 2, -1, -1))

    def step(self, *deps, gates=()):
        bit = self.order.pop(0)
        place = len(self.left) - 1 - self.left.index(bit)
        mine = scalar((self.position >> bit) & 1)
        keep, away, *rest = halve(
            mine, self.parts, self.blocks, 1 << place, self.columns, deps, gates
        )
        self.parts = [(keep, 0), (swap(away, "blk", 1 << bit), 0)]
        self.left.remove(bit)
        self.blocks //= 2
        return (away, *rest) if rest else away

    def last(self, *deps):
        while self.order:
            self.step(*deps)
        return halve(scalar(self.position), self.parts, 1, 1, self.columns, deps)[0]


def scalar(x):
    return x.reshape(1).astype(jnp.int32)


def total_kernel(one, two, out):
    out[...] = one[...] + two[...]


def butterfly_steps():
    blocks = lax.axis_size("blk")
    return [("dp", 1)] + [("blk", 1 << i) for i in range(blocks.bit_length() - 1)] + [("head", 1)]


def butterfly_add(x, got, deps=()):
    whole = pl.BlockSpec(memory_space=pltpu.VMEM)
    return call(
        total_kernel,
        deps=deps,
        in_specs=[whole, whole],
        out_shape=[jax.ShapeDtypeStruct(x.shape, F32)],
        cost_estimate=cost(TAIL),
        name="small_sum",
    )(x, got)[0]


def in_order(mine, first, second, axis):
    return jnp.where(
        mine == 0, jnp.concatenate([first, second], axis), jnp.concatenate([second, first], axis)
    )


def pick(x, index, axis=0):
    return lax.dynamic_index_in_dim(x, index, axis, keepdims=False)


def shards(
    tokens, doc_ids, w_qkv, w_out, slopes, w_up, w_down, w_comp, comp_bias,
    norm1_gain, norm1_bias, norm2_gain, norm2_bias, out_cot, recon_cot,
):
    seqs, rows, model = tokens.shape
    heads = slopes.shape[0]
    width = w_qkv.shape[2]
    hd = width // heads
    slots = rows // 3
    used = 3 * slots
    padded = -(-slots // 16) * 16
    memory = CSEGS * slots
    position = lax.axis_index("blk")
    core = lax.axis_index("dp")
    me = lax.axis_index("head")
    ot = 1 - me
    scaling = hd ** (-0.5)
    half = model // 2
    share = model // (lax.axis_size("blk") * lax.axis_size("dp"))
    bits = lax.axis_size("blk").bit_length() - 1
    rising = list(range(bits))
    falling = [1, 0] + rising[2:]
    scalars = jnp.stack([core, me]).astype(jnp.int32)
    me_arg, ot_arg = me.reshape(1).astype(jnp.int32), ot.reshape(1).astype(jnp.int32)

    small = jnp.concatenate(
        [pick(recon_cot, ot), jnp.pad(slopes, (0, rows - heads)).reshape(1, rows)], 0
    )
    small_got = swap(small, "head")
    half_rows = model // 2
    qkv_part = lax.dynamic_slice_in_dim(w_qkv, core * half_rows, half_rows, 1)
    out_part = lax.dynamic_slice_in_dim(w_out, core * half_rows, half_rows, 1)
    far_part = jnp.concatenate([qkv_part, out_part[None]], 0)
    far_got = swap(far_part, "head")
    groups = ("own", "oth")

    halo_raw = shift(pick(tokens, me), "blk", 1)
    normed, tri_own, tri_oth = front(
        me_arg, tokens, norm1_gain, norm1_bias, slots, padded, deps=(far_part, small)
    )
    packed = dot(tri_own, w_comp.reshape(3 * model, model)) + comp_bias
    packed = packed.astype(BF)
    lag2, lag3 = shift(packed, "blk", 2), shift(packed, "blk", 3)

    docs = pick(doc_ids, me)
    query_doc = lax.dynamic_slice_in_dim(docs, position * rows, rows, 0).reshape(1, rows)
    padded_doc = jnp.concatenate([jnp.full(((CSEGS + 1) * rows,), -1, jnp.int32), docs])
    window = lax.dynamic_slice_in_dim(padded_doc, position * rows, (CSEGS + 2) * rows, 0)
    window = jnp.broadcast_to(window[:, None], ((CSEGS + 2) * rows, 128))
    (far,) = far_log(
        position.reshape(1).astype(jnp.int32), window, query_doc, slots, deps=(packed,)
    )

    weights, outs = {"own": w_qkv}, {"own": w_out}
    cots = {"own": pick(recon_cot, me).reshape(heads, 1, rows)}
    slope = {"own": slopes}
    q, ko, vo, kc, vc, rec, kf, vf, att, lse = ({} for _ in range(10))
    q["own"], ko["own"], vo["own"], kc["own"], vc["own"], lag2 = project(
        normed, packed, w_qkv, deps=(far,), gates=(lag2,)
    )
    lag4 = shift(lag2, "blk", 2)
    cots["oth"] = small_got[:heads].reshape(heads, 1, rows)
    slope["oth"] = small_got[heads, :heads]
    rec["own"] = recon_both(
        q["own"], ko["own"], vo["own"], kc["own"], vc["own"], cots["own"], slots, scaling,
    )
    mem = jnp.zeros((rows, model), BF)
    for index, lag in enumerate((lag4, lag3, lag2)):
        place = (index * slots, rows - (index + 1) * slots)
        mem = mem + jnp.pad(lag[:slots], (place, (0, 0)))
    halo = norm_halo(halo_raw, norm1_gain, norm1_bias, deps=(rec["own"][0],))[0]
    kf["own"], vf["own"], far_got = project_distant(halo, mem, w_qkv, gates=(far_got,))
    near_got = swap(far_got, "dp")
    att["own"], lse["own"] = attend_forward(
        slope["own"], q["own"], kf["own"], vf["own"], ko["own"], vo["own"], far, scaling
    )
    weights["oth"] = in_order(core, far_got[:3], near_got[:3], 1)
    outs["oth"] = in_order(core, far_got[3], near_got[3], 1)
    q["oth"], ko["oth"], vo["oth"], kc["oth"], vc["oth"] = project(
        normed, packed, weights["oth"], deps=(att["own"],)
    )
    kf["oth"], vf["oth"] = project_distant(halo, mem, weights["oth"], deps=(q["oth"],))
    att["oth"], lse["oth"] = attend_forward(
        slope["oth"], q["oth"], kf["oth"], vf["oth"], ko["oth"], vo["oth"], far, scaling
    )

    middle, n2_own = middle_norm(
        me_arg, tokens, att["own"], att["oth"], w_out, outs["oth"], norm2_gain, norm2_bias
    )
    n2_oth = swap(n2_own, "head")
    rec["oth"] = recon_both(
        q["oth"], ko["oth"], vo["oth"], kc["oth"], vc["oth"], cots["oth"], slots, scaling,
        deps=(n2_own,),
    )
    hid_own, din_own, dn_own = mlp(
        me_arg, n2_own, out_cot, w_up, w_down, BF, deps=(rec["oth"][0],)
    )
    hid_oth, din_oth, dn_oth = mlp(
        ot_arg, n2_oth, out_cot, w_up, w_down, BF, deps=(dn_own,)
    )
    dn_got = swap(dn_oth, "head")
    units = w_up.shape[1]
    up_down, token = weight_grads(
        scalars,
        [
            [(n2_own, 0, din_own, (0, 0), units), (n2_oth, 0, din_oth, (0, 0), units)],
            [(out_cot, 0, hid_own, (0, 0), units), (out_cot, 1, hid_oth, (0, 0), units)],
        ],
        0, model, "mlp_grads", deps=(dn_oth,),
    )
    ffn_own, ffn_oth = branches(hid_own, hid_oth, w_down, deps=(token,))
    up_down = lax.psum_scatter(up_down, ("blk", "dp"), scatter_dimension=0, tiled=True)
    (
        dbranch, datt_own, datt_oth, row_own, row_oth, sums2,
        ffn_oth, recon_oth,
    ) = turn(
        me_arg, dn_own, dn_got, middle, out_cot, att["own"], att["oth"], w_out, outs["oth"],
        norm2_gain, heads, gates=(ffn_oth, rec["oth"][0]),
    )
    ffn_got = swap(ffn_oth, "head")
    recon_got = swap(recon_oth.reshape(heads, rows), "head")
    datt = {"own": datt_own, "oth": datt_oth}
    row = {"own": row_own, "oth": row_oth}
    back, near, grads = {}, {}, {}

    def far_back(g, *deps):
        back[g] = attend_backward(
            slope[g], q[g], datt[g], lse[g], row[g], far, kf[g], vf[g], False, [], scaling,
            deps=deps, late=g == "own",
        )

    def near_back(g, *deps, gates=()):
        r = rec[g]
        near[g] = attend_backward(
            slope[g], q[g], datt[g], lse[g], row[g], far, ko[g], vo[g], True,
            [back[g][0], r[1], r[2], r[3]], scaling, deps=deps, gates=gates, late=g == "own",
        )

    def group_grads(g, *deps, gates=()):
        r = rec[g]
        sections = [[(normed, 0, near[g][0], (0, 0), width)]]
        for i in (1, 2):
            sections.append(
                [
                    (normed, 0, near[g][i], (0, 0), width),
                    (packed, 0, r[3 + i], (0, 0), width),
                    (halo, 0, back[g][i], (0, 0), width),
                    (mem, 0, back[g][i], (0, rows), width),
                ]
            )
        sections.append([(dbranch, 0, att[g], (0, 0), width)])
        grads[g] = weight_grads(
            scalars, sections, share, model, "attention_grads", deps=deps, gates=gates
        )

    far_back("oth", dbranch)
    near_back("oth")
    group_grads("oth")
    cross = trade(grads["oth"][0])
    far_back("own", grads["oth"][1])
    (lo_own,) = add((middle, ffn_own, ffn_got), 1, "layer_sum", deps=(back["own"][3],))
    (cross,) = add((cross,), 1, "cross_sum", deps=(lo_own,))
    cross_got = swap(cross, "head")
    halo_part, back4, back3, back2 = spread(
        back["oth"][1], back["oth"][2], back["own"][1], back["own"][2], weights["oth"], w_qkv,
        slots, padded, deps=(cross,),
    )
    slot_gots = [
        shift(part, "blk", -lag)
        for part, lag in zip((back4, back3, back2), range(CSEGS + 1, 1, -1))
    ]
    near_back("own", halo_part)
    group_grads("own")
    own = trade(grads["own"][0])
    base_oth = base_rows(
        near["oth"][:3], rec["oth"][4:6], weights["oth"], [], deps=(grads["own"][1],)
    )
    base, slot_base = base_rows(near["own"][:3], rec["own"][4:6], w_qkv, base_oth)
    wide = 2 * width
    late = Halving([(own, 0, 0), (own, 0, 1), (cross_got, 0)], 2 * wide, rising, position)
    moved = late.step(base)
    dpacked, dp_mine, dp_away, bias_sum, halo_part, lo_own = packed_back(
        me_arg, slot_base, slot_gots, deps=(moved,), gates=(halo_part, lo_own)
    )
    dp_got = swap(dp_away, "head")
    halo_back = shift(halo_part, "blk", -1)
    lo_got = swap(lo_own, "head")
    send, token = weight_grads(
        scalars,
        [
            [
                (tri_own, tap * model, dp_mine, (0, 0), half),
                (tri_oth, tap * model, dp_got, (0, 0), half),
            ]
            for tap in range(3)
        ],
        share, model, "pack_grads",
    )
    comp = trade(send)
    comp = Halving([(comp, 0, 0), (comp, 0, 1)], 3 * half, falling, position)
    moved = comp.step(token)
    moved = late.step(moved)
    grad_own, sums1 = finish(
        me_arg, base, halo_back, dpacked, w_comp, tokens, dbranch, norm1_gain,
        deps=(recon_got, moved),
    )
    dslopes = {}
    for g in groups:
        total = back[g][3] + near[g][3]
        dslopes[g] = -jnp.sum(total[:, 2] - total[:, 0] * total[:, 1], axis=1)
    both = in_order(me, dslopes["own"], dslopes["oth"], 0)
    vector = jnp.concatenate(
        [sums1[0], sums1[1], sums2[0], sums2[1], bias_sum[0], jnp.pad(both, (0, 128 - 2 * heads))]
    ).reshape(-1, 128)
    rounds = butterfly_steps()
    vector_got = swap(vector, *rounds.pop(0))
    moved, grad_away = comp.step(sums1, gates=(grad_own,))
    grad_got = swap(grad_away, "head")
    vector = butterfly_add(vector, vector_got, deps=(moved,))
    vector_got = swap(vector, *rounds.pop(0))
    moved = vector
    while late.order or comp.order:
        if late.order:
            moved = late.step(moved)
        if comp.order:
            moved = comp.step(moved)
        vector = butterfly_add(vector, vector_got, deps=(moved,))
        vector_got = swap(vector, *rounds.pop(0))
        moved = vector
    up_sum, down_sum = up_down[:, :units].astype(F32), up_down[:, units:].astype(F32).T
    vector = butterfly_add(vector, vector_got, deps=(moved, up_sum, down_sum))
    vector_got = swap(vector, *rounds.pop(0))
    late = late.last(vector)
    while len(rounds) > 1:
        vector = butterfly_add(vector, vector_got, deps=(late,))
        vector_got = swap(vector, *rounds.pop(0))
    if rounds:
        vector = butterfly_add(vector, vector_got, deps=(late,))
        vector_got = swap(vector, *rounds.pop(0))
    grad_tokens = in_order(me, grad_own[None], grad_got[None], 0)
    comp = comp.last(vector, grad_tokens)
    vector = (vector + vector_got).reshape(-1)
    comp = comp.astype(BF)
    comp_got = swap(comp, "head")
    comp_all = in_order(
        me, comp.reshape(share, 3, half), comp_got.reshape(share, 3, half), 2
    ).astype(F32)

    slope_sum = lax.dynamic_slice_in_dim(vector, 5 * model + me * heads, heads, 0)

    recon_own = rec["own"][0].reshape(heads, rows)
    recon = in_order(me, recon_own[None], recon_got[None], 0)
    layer_out = in_order(me, lo_own[None], lo_got[None], 0)
    return (
        layer_out,
        recon,
        grad_tokens,
        jnp.transpose(late[:, : 3 * width].reshape(share, 3, width), (1, 0, 2)),
        late[:, 3 * width :].T,
        slope_sum,
        up_sum,
        down_sum,
        jnp.transpose(comp_all, (1, 0, 2)),
        vector[4 * model : 5 * model],
        vector[:model],
        vector[model : 2 * model],
        vector[2 * model : 3 * model],
        vector[3 * model : 4 * model],
    )


def solution(mesh):
    in_specs = (
        P("dp", "blk", None),
        P("dp", None),
        P(None, None, "head"),
        P("head", None),
        P("head"),
        P(None, "head"),
        P("head", None),
        P(),
        P(),
        P(),
        P(),
        P(),
        P(),
        P("dp", "blk", None),
        P("dp", "head", "blk"),
    )
    out_specs = (
        P("dp", "blk", None),
        P("dp", "head", "blk"),
        P("dp", "blk", None),
        P(None, ("blk", "dp"), "head"),
        P("head", ("blk", "dp")),
        P("head"),
        P(("blk", "dp"), "head"),
        P("head", ("blk", "dp")),
        P(None, ("blk", "dp"), None),
        P(),
        P(),
        P(),
        P(),
        P(),
    )
    return jax.shard_map(shards, mesh=mesh, in_specs=in_specs, out_specs=out_specs, check_vma=False)
```

```python
import functools
import math

import jax
import jax.numpy as jnp
from jax import lax
from jax.experimental import pallas as pl
from jax.experimental.pallas import tpu as pltpu
from jax.sharding import PartitionSpec as P

CSEGS = 3
EPS = 1e-05
FAR = 1e30
LOG2E = math.log2(math.e)
BF = jnp.bfloat16
F32 = jnp.float32
TILE = 256
GROUP = 2
OWN, OTH = 0, 1
BLK, DP, HEAD = "blk", "dp", "head"
SHARE = 1 << 24
TAIL = 1.0


def mib(count):
    return int(count * (1 << 20))


def cost(us):
    return pl.CostEstimate(flops=int(us * SHARE), bytes_accessed=1 << 10, transcendentals=0)

NT = (((1,), (1,)), ((), ()))
GELU_A = math.sqrt(2.0 / math.pi)
GELU_B = 0.044715


def dot(a, b):
    return jnp.dot(a, b, preferred_element_type=F32)


def dot_nt(a, b):
    return lax.dot_general(a, b, NT, preferred_element_type=F32)


def dot_tn(a, b):
    return lax.dot_general(a, b, (((0,), (0,)), ((), ())), preferred_element_type=F32)


def shift(x, axis, by):
    devices = lax.axis_size(axis)
    pairs = [(i, i + by) for i in range(devices) if 0 <= i + by < devices]
    return lax.ppermute(x, axis, pairs)


def trade(x):
    return lax.all_to_all(x, DP, 0, 0)


def swap(x, axis, step=1):
    devices = lax.axis_size(axis)
    return lax.ppermute(x, axis, [(i, i ^ step) for i in range(devices)])


def call(
    kernel, deps=(), gates=(), prefetch=0, in_specs=None, from_hbm=False, to_hbm=False, **rest
):
    def run(*operands):
        count = len(operands)
        if from_hbm:
            operands = operands[:prefetch] + tuple(
                pltpu.with_memory_space_constraint(x, pltpu.HBM)
                if spec.memory_space is None else x
                for x, spec in zip(operands[prefetch:], in_specs)
            )
        passed = len(deps) + len(gates)
        specs = in_specs or [pl.BlockSpec(memory_space=pltpu.VMEM)] * count
        far = pl.BlockSpec(memory_space=pltpu.HBM)
        specs = list(specs) + [far] * passed

        def body(*refs):
            refs = refs[:count] + refs[count + passed :]
            results = count + len(rest_out)
            kernel(*refs[:results], *refs[results + len(gates) :])

        rest_out = list(rest["out_shape"])
        if to_hbm:
            rest_out = [pltpu.HBM(x.shape, x.dtype) for x in rest_out]
        settings = dict(rest)
        settings["out_shape"] = rest_out + [jax.ShapeDtypeStruct(g.shape, g.dtype) for g in gates]
        if gates:
            plain = [pl.BlockSpec(memory_space=pltpu.VMEM)] * len(rest_out)
            settings["out_specs"] = list(rest.get("out_specs", plain)) + [far] * len(gates)
            settings["input_output_aliases"] = {
                count + len(deps) + i: len(rest_out) + i for i in range(len(gates))
            }
        if prefetch:
            grid = {
                key: settings.pop(key)
                for key in ("grid", "out_specs", "scratch_shapes") if key in settings
            }
            settings["grid_spec"] = pltpu.PrefetchScalarGridSpec(
                num_scalar_prefetch=prefetch, in_specs=specs, **grid
            )
        else:
            settings["in_specs"] = specs
        return pl.pallas_call(body, **settings)(*operands, *deps, *gates)

    return run


def by_heads(kernel, count, width):
    def body(*refs):
        for index in range(count):
            columns = slice(index * width, (index + 1) * width)
            views = []
            for ref in refs:
                if len(ref.shape) == 3:
                    views.append(ref.at[index : index + 1])
                elif len(ref.shape) == 2 and ref.dtype == BF:
                    views.append(ref.at[:, columns])
                else:
                    views.append(ref)
            kernel(pl.program_id(0) * count + index, *views)

    return body


def still(shape, index_map):
    return pl.BlockSpec(shape, index_map, pipeline_mode=pl.Buffered(1))


def row_stats(x):
    center = x - jnp.mean(x, axis=-1, keepdims=True)
    inverse = lax.rsqrt(jnp.mean(center * center, axis=-1, keepdims=True) + EPS)
    return center * inverse, inverse


def norm_back(grad, unit, inverse, gain):
    scaled = grad * gain
    mean_one = jnp.mean(scaled, axis=-1, keepdims=True)
    mean_two = jnp.mean(scaled * unit, axis=-1, keepdims=True)
    return inverse * (scaled - mean_one - unit * mean_two)


def front_kernel(me, own, other, gain, bias, normed, tri_own, tri_other, unit, *, slots):
    rows, model = own.shape
    padded = tri_own.shape[0]
    for source, tri in ((own, tri_own), (other, tri_other)):
        for start in range(0, rows, 128):
            part = slice(start, start + 128)
            x, _ = row_stats(source[part, :].astype(F32))
            x = x * gain[...] + bias[...]
            for lane in range(model // 128):
                unit[lane, part, :] = x[:, lane * 128 : (lane + 1) * 128]
            if source is own:
                normed[part, :] = x.astype(BF)
        live = lax.broadcasted_iota(jnp.int32, (padded, 128), 0) < slots
        for lane in range(model // 128):
            unit[lane, rows:, :] = jnp.zeros((unit.shape[1] - rows, 128), F32)
            for tap in range(3):
                at = tap * model + lane * 128
                rows_of = unit[lane, pl.ds(tap, padded, stride=3), :]
                tri[:, at : at + 128] = jnp.where(live, rows_of, 0.0).astype(BF)


def front(me, tokens, gain, bias, slots, padded, deps=(), gates=()):
    _, rows, model = tokens.shape
    tri = jax.ShapeDtypeStruct((padded, 3 * model), BF)
    fixed = lambda shape: still(shape, lambda i, m: (0, 0))
    pick = lambda turn: still((None, rows, model), lambda i, m: ((m[0] + turn) % 2, 0, 0))
    return call(
        functools.partial(front_kernel, slots=slots),
        deps=deps,
        gates=gates,
        **dict(
            prefetch=1,
            grid=(1,),
            in_specs=[pick(0), pick(1), fixed((1, model)), fixed((1, model))],
            out_specs=[fixed((rows, model)), fixed((padded, 3 * model)), fixed((padded, 3 * model))],
            scratch_shapes=[pltpu.VMEM((model // 128, 3 * padded + 8, 128), F32)],
        ),
        out_shape=[jax.ShapeDtypeStruct((rows, model), BF), tri, tri],
        compiler_params=pltpu.CompilerParams(vmem_limit_bytes=mib(14.0)),
        cost_estimate=cost(0.02),
    )(me, tokens, tokens, gain.reshape(1, model), bias.reshape(1, model))


def norm_kernel(rows, gain, bias, normed):
    unit, _ = row_stats(rows[...].astype(F32))
    normed[...] = (unit * gain[...] + bias[...]).astype(BF)


def norm_halo(rows, gain, bias, deps=(), gates=()):
    count, model = rows.shape
    tall = pl.BlockSpec((TILE, model), lambda i: (i, 0))
    fixed = pl.BlockSpec((1, model), lambda i: (0, 0))
    return call(
        norm_kernel,
        deps=deps,
        gates=gates,
        grid=(count // TILE,),
        in_specs=[tall, fixed, fixed],
        out_specs=[tall],
        out_shape=[jax.ShapeDtypeStruct((count, model), BF)],
        compiler_params=pltpu.CompilerParams(vmem_limit_bytes=mib(14.0)),
        cost_estimate=cost(2),
    )(rows, gain.reshape(1, model), bias.reshape(1, model))


def distant_kernel(halo, mem, w, kf, vf):
    rows = halo.shape[0]
    for index, out in ((1, kf), (2, vf)):
        out[:rows, :] = dot(halo[...], w[index]).astype(BF)
        out[rows:, :] = dot(mem[...], w[index]).astype(BF)


def project_distant(halo, mem, w, deps=(), gates=()):
    rows, model = halo.shape
    width = w.shape[2]
    shape = jax.ShapeDtypeStruct((2 * rows, width), BF)
    return call(
        distant_kernel,
        deps=deps,
        gates=gates,
        out_shape=[shape, shape],
        compiler_params=pltpu.CompilerParams(vmem_limit_bytes=mib(14.0)),
        cost_estimate=cost(2.1),
    )(halo, mem, w)


def far_kernel(place, docs, query, out, mem, *, slots, rows):
    position = place[0]
    for seg in range(CSEGS):
        mem[seg * slots : (seg + 1) * slots, :] = docs[pl.ds(seg * rows, slots, stride=3), :]
    mem[CSEGS * slots :, :] = jnp.full((rows - CSEGS * slots, 128), -1, jnp.int32)
    column = lax.broadcasted_iota(jnp.int32, (1, rows), 1)
    step = 64
    for start in range(0, 3 * rows, step):
        local = lax.broadcasted_iota(jnp.int32, (step, 1), 0) + start % rows
        if start < rows:
            doc = docs[CSEGS * rows + start : CSEGS * rows + start + step, :1]
            where, live = local - rows, position > 0
        elif start < 2 * rows:
            doc = mem[start - rows : start - rows + step, :1]
            lead = sum((local >= seg * slots).astype(jnp.int32) for seg in range(1, CSEGS + 1))
            where = (lead - 1 - CSEGS) * rows + 3 * (local - lead * slots) + 1
            live = position - 1 - CSEGS + lead >= 0
        else:
            at = (CSEGS + 1) * rows + start - 2 * rows
            doc = docs[at : at + step, :1]
            where, live = local, position >= 0
        doc = jnp.where(live, doc, -2)
        apart = column - where
        seen = (apart >= 0) & (doc == query[...])
        value = jnp.log((1 + jnp.maximum(apart, 0)).astype(F32))
        out[start : start + step, :] = jnp.where(seen, value, FAR)


def far_log(place, docs, query, slots, deps=(), gates=()):
    rows = query.shape[1]
    return call(
        functools.partial(far_kernel, slots=slots, rows=rows),
        deps=deps,
        gates=gates,
        in_specs=[
            pl.BlockSpec(memory_space=pltpu.SMEM),
            pl.BlockSpec(memory_space=pltpu.VMEM),
            pl.BlockSpec(memory_space=pltpu.VMEM),
        ],
        out_shape=[jax.ShapeDtypeStruct((3 * rows, rows), F32)],
        scratch_shapes=[pltpu.VMEM((rows, 128), jnp.int32)],
        compiler_params=pltpu.CompilerParams(vmem_limit_bytes=mib(14.0)),
        cost_estimate=cost(0.02),
    )(place, docs, query)


def project_kernel(normed, packed, w, q, k, v, kc, vc):
    for index, out in enumerate((q, k, v)):
        out[...] = dot(normed[...], w[index]).astype(BF)
    kc[...] = dot(packed[...], w[1]).astype(BF)
    vc[...] = dot(packed[...], w[2]).astype(BF)


def project(normed, packed, w, deps=(), gates=()):
    rows, model = normed.shape
    padded, width = packed.shape[0], w.shape[2]
    near = jax.ShapeDtypeStruct((rows, width), BF)
    little = jax.ShapeDtypeStruct((padded, width), BF)
    return call(
        project_kernel,
        deps=deps,
        gates=gates,
        out_shape=[near, near, near, little, little],
        compiler_params=pltpu.CompilerParams(vmem_limit_bytes=mib(14.0)),
        cost_estimate=cost(2.0),
    )(normed, packed, w)


def forward_kernel(head, slopes, q, kf, vf, ko, vo, far, out, lse, *, scaling):
    c1 = scaling * LOG2E
    c2 = slopes[head] * LOG2E
    rows, reach = q.shape[0], kf.shape[0]
    vft, vot = vf[...].T, vo[...].T
    for qi in range(rows // TILE):
        qs = slice(qi * TILE, (qi + 1) * TILE)
        until = (qi + 1) * TILE
        qb = q[qs, :]
        near = dot_nt(ko[:until, :], qb) * c1 - c2 * far[reach : reach + until, qs]
        away = dot_nt(kf[...], qb) * c1 - c2 * far[:reach, qs]
        top = jnp.maximum(
            jnp.max(near, axis=0, keepdims=True), jnp.max(away, axis=0, keepdims=True)
        )
        near = jnp.exp2(near - top)
        away = jnp.exp2(away - top)
        total = jnp.sum(near, axis=0, keepdims=True) + jnp.sum(away, axis=0, keepdims=True)
        mixed = dot(vot[:, :until], near.astype(BF)) + dot(vft, away.astype(BF))
        out[qs, :] = (mixed / total).T.astype(BF)
        lse[0, :, qs] = top + jnp.log2(total)


def attend_forward(slopes, q, kf, vf, ko, vo, far, scaling, deps=(), gates=()):
    rows, width = q.shape
    reach = kf.shape[0]
    heads = slopes.shape[0]
    hd = width // heads
    near = pl.BlockSpec((rows, GROUP * hd), lambda h: (0, h))
    wide = pl.BlockSpec((reach, GROUP * hd), lambda h: (0, h))
    return call(
        by_heads(functools.partial(forward_kernel, scaling=scaling), GROUP, hd),
        deps=deps,
        gates=gates,
        grid=(heads // GROUP,),
        in_specs=[
            pl.BlockSpec(memory_space=pltpu.SMEM), near, wide, wide, near, near,
            still((reach + rows, rows), lambda h: (0, 0)),
        ],
        out_specs=[near, pl.BlockSpec((GROUP, 1, rows), lambda h: (h, 0, 0))],
        out_shape=[
            jax.ShapeDtypeStruct((rows, width), BF),
            jax.ShapeDtypeStruct((heads, 1, rows), F32),
        ],
        compiler_params=pltpu.CompilerParams(vmem_limit_bytes=mib(14.0)),
        cost_estimate=cost(3.2),
    )(slopes, q, kf, vf, ko, vo, far)


def backward_kernel(head, slopes, q, do, lse, dot_row, far, k, v, *refs, scaling, own):
    c1 = scaling * LOG2E
    c2 = slopes[head] * LOG2E
    extras = refs[:-4]
    dq, dk_out, dv_out, sums_out = refs[-4:]
    rows, hd = q.shape
    keys = k.shape[0]
    tall = rows
    dqs = [None] * (rows // TILE)
    for ki in range(keys // tall):
        base = ki * tall
        kt = k[base : base + tall, :].T
        dks, dvs = [], []
        for qi in range(rows // TILE):
            qs = slice(qi * TILE, (qi + 1) * TILE)
            until = (qi + 1) * TILE if own else tall
            ks = slice(base, base + until)
            qb, db = q[qs, :], do[qs, :]
            dist = far[ks, qs]
            s = dot_nt(k[ks, :], qb) * c1 - c2 * dist
            p = jnp.exp2(s - lse[0, :, qs])
            dp = dot_nt(v[ks, :], db)
            ds = p * (dp - dot_row[0, :, qs])
            for index, value in enumerate((ds, p * dist, ds * dist)):
                value = jnp.sum(value, axis=0, keepdims=True)
                if ki > 0:
                    value = value + sums_out[0, index : index + 1, qs]
                sums_out[0, index : index + 1, qs] = value
            p = p.astype(BF)
            ds = ds.astype(BF)
            dvs.append(dot(p, db))
            dks.append(dot(ds, qb))
            value = dot(kt[:, :until], ds)
            if ki > 0:
                value = value + dqs[qi]
            dqs[qi] = value
            if ki == keys // tall - 1:
                value = value.T * scaling
                if own:
                    value = value + extras[0][qs, :].astype(F32) + extras[1][qs, :].astype(F32)
                dq[qs, :] = value.astype(BF)
        for start in range(0, tall, TILE):
            ks = slice(base + start, base + start + TILE)
            dk = sum(d[start : start + TILE, :] for d in dks if d.shape[0] > start) * scaling
            dv = sum(d[start : start + TILE, :] for d in dvs if d.shape[0] > start)
            if own:
                dk = dk + extras[2][ks, :].astype(F32)
                dv = dv + extras[3][ks, :].astype(F32)
            dk_out[ks, :] = dk.astype(BF)
            dv_out[ks, :] = dv.astype(BF)


def attend_backward(
    slopes, q, do, lse, dot_row, far, k, v, own, extras, scaling, deps=(), gates=(), late=False
):
    rows, width = q.shape
    keys = k.shape[0]
    heads = slopes.shape[0]
    hd = width // heads
    near = pl.BlockSpec((rows, GROUP * hd), lambda h: (0, h))
    wide = pl.BlockSpec((keys, GROUP * hd), lambda h: (0, h))
    lane = pl.BlockSpec((GROUP, 1, rows), lambda h: (h, 0, 0))
    place = far.shape[0] // keys - 1 if own else 0
    return call(
        by_heads(functools.partial(backward_kernel, scaling=scaling, own=own), GROUP, hd),
        deps=deps,
        gates=gates,
        grid=(heads // GROUP,),
        in_specs=[
            pl.BlockSpec(memory_space=pltpu.SMEM), near, near, lane, lane,
            still((keys, rows), lambda h: (place, 0)), wide, wide,
        ]
        + [near] * len(extras),
        out_specs=[near, wide, wide, pl.BlockSpec((GROUP, 8, rows), lambda h: (h, 0, 0))],
        out_shape=[
            jax.ShapeDtypeStruct((rows, width), BF),
            jax.ShapeDtypeStruct((keys, width), BF),
            jax.ShapeDtypeStruct((keys, width), BF),
            jax.ShapeDtypeStruct((heads, 8, rows), F32),
        ],
        compiler_params=pltpu.CompilerParams(vmem_limit_bytes=mib(14.0)),
        cost_estimate=cost(TAIL * (5 if own else 9)),
        from_hbm=late,
    )(slopes, q, do, lse, dot_row, far, k, v, *extras)


def recon_kernel(head, q, ko, vo, kc, vc, cot, recon, dq, dk, dv, dkc, dvc, *, slots, scaling):
    rows, hd = q.shape
    c1 = scaling * LOG2E
    comp_rows = kc.shape[0]
    live = lax.broadcasted_iota(jnp.int32, (comp_rows, TILE), 0) < slots
    kct, vct, kot, vot = kc[...].T, vc[...].T, ko[...].T, vo[...].T
    for qi in range(rows // TILE):
        qs = slice(qi * TILE, (qi + 1) * TILE)
        qb = q[qs, :]
        full_s = dot_nt(ko[...], qb) * c1
        full_p = jnp.exp2(full_s - jnp.max(full_s, axis=0, keepdims=True))
        full_p = full_p * (1.0 / jnp.sum(full_p, axis=0, keepdims=True))
        full_low = full_p.astype(BF)
        comp_s = jnp.where(live, dot_nt(kc[...], qb) * c1, -FAR)
        comp_p = jnp.exp2(comp_s - jnp.max(comp_s, axis=0, keepdims=True))
        comp_p = comp_p * (1.0 / jnp.sum(comp_p, axis=0, keepdims=True))
        comp_low = comp_p.astype(BF)
        full, comp = dot(vot, full_low), dot(vct, comp_low)
        spread = full - comp
        recon[0, :, qs] = jnp.sum(spread * spread, axis=0, keepdims=True) / hd**0.5
        dfull = spread * (cot[0, :, qs] * (2.0 / hd**0.5))
        dfull_low = dfull.astype(BF)
        dfull_rows = dfull_low.T
        full_dw = dot(vo[...], dfull_low)
        comp_dw = dot(vc[...], dfull_low)
        row = jnp.sum(full_p * full_dw, axis=0, keepdims=True)
        full_ds = (full_p * (full_dw - row)).astype(BF)
        row = jnp.sum(comp_p * comp_dw, axis=0, keepdims=True)
        comp_ds = (comp_p * (row - comp_dw)).astype(BF)
        dq[qs, :] = ((dot(kot, full_ds) + dot(kct, comp_ds)).T * scaling).astype(BF)
        terms = (
            dot(full_ds, qb) * scaling, dot(full_low, dfull_rows),
            dot(comp_ds, qb) * scaling, -dot(comp_low, dfull_rows),
        )
        values = terms if qi == 0 else [a + b for a, b in zip(values, terms)]
    for ref, value in zip((dk, dv, dkc, dvc), values):
        ref[...] = value.astype(ref.dtype)


def recon_both(q, ko, vo, kc, vc, cot, slots, scaling, deps=(), gates=()):
    rows, width = q.shape
    heads = cot.shape[0]
    hd = width // heads
    comp_rows = kc.shape[0]
    near = pl.BlockSpec((rows, GROUP * hd), lambda h: (0, h))
    small = pl.BlockSpec((comp_rows, GROUP * hd), lambda h: (0, h))
    lane = pl.BlockSpec((GROUP, 1, rows), lambda h: (h, 0, 0))
    big = jax.ShapeDtypeStruct((rows, width), BF)
    little = jax.ShapeDtypeStruct((comp_rows, width), BF)
    return call(
        by_heads(functools.partial(recon_kernel, slots=slots, scaling=scaling), GROUP, hd),
        deps=deps,
        gates=gates,
        grid=(heads // GROUP,),
        in_specs=[near, near, near, small, small, lane],
        out_specs=[lane, near, near, near, small, small],
        out_shape=[jax.ShapeDtypeStruct((heads, 1, rows), F32), big, big, big, little, little],
        compiler_params=pltpu.CompilerParams(vmem_limit_bytes=mib(10.3)),
        cost_estimate=cost(4.3),
        to_hbm=True,
    )(q, ko, vo, kc, vc, cot)


def middle_kernel(me, tokens, a_one, a_two, w_one, w_two, gain, bias, middle, normed):
    value = tokens[...].astype(F32) + (dot(a_one[...], w_one[...]) + dot(a_two[...], w_two[...]))
    middle[...] = value
    unit, _ = row_stats(value)
    normed[...] = (unit * gain[...] + bias[...]).astype(BF)


def middle_norm(me, tokens, a_one, a_two, w_one, w_two, gain, bias, deps=(), gates=()):
    _, rows, model = tokens.shape
    width = a_one.shape[1]
    tall = pl.BlockSpec((TILE, model), lambda i, m: (i, 0))
    part = pl.BlockSpec((TILE, width), lambda i, m: (i, 0))
    fixed = lambda shape: still(shape, lambda i, m: (0, 0))
    return call(
        middle_kernel,
        deps=deps,
        gates=gates,
        **dict(
            prefetch=1,
            grid=(rows // TILE,),
            in_specs=[pl.BlockSpec((None, TILE, model), lambda i, m: (m[0], i, 0)), part, part,
                      fixed((width, model)), fixed((width, model)), fixed((1, model)),
                      fixed((1, model))],
            out_specs=[tall, tall],
        ),
        out_shape=[jax.ShapeDtypeStruct((rows, model), F32), jax.ShapeDtypeStruct((rows, model), BF)],
        compiler_params=pltpu.CompilerParams(vmem_limit_bytes=mib(14.0)),
        cost_estimate=cost(1.1),
    )(me, tokens, a_one, a_two, w_one, w_two, gain.reshape(1, model), bias.reshape(1, model))


def mlp_kernel(which, normed, cot, w_up, w_down, hidden, dinner, dnormed, dn_sum):
    step = pl.program_id(0)
    inner = dot(normed[...], w_up[...])
    dhidden = dot_nt(cot[...], w_down[...])
    square = inner * inner
    inside = jnp.tanh(inner * (GELU_A + (GELU_A * GELU_B) * square))
    bent = 0.5 * (1.0 + inside)
    hidden[...] = (inner * bent).astype(BF)
    slope = bent + inner * (0.5 - 0.5 * inside * inside) * (
        GELU_A + (3.0 * GELU_A * GELU_B) * square
    )
    dlow = (dhidden * slope).astype(BF)
    dinner[...] = dlow
    dn = dot_nt(dlow, w_up[...])

    @pl.when(step == 0)
    def _():
        dn_sum[...] = dn

    @pl.when(step > 0)
    def _():
        dn_sum[...] += dn

    @pl.when(step == pl.num_programs(0) - 1)
    def _():
        dnormed[...] = dn_sum[...].astype(dnormed.dtype)


def mlp(which, normed, cot, w_up, w_down, dtype, deps=(), gates=()):
    rows, model = normed.shape
    units = w_up.shape[1]
    step = 512
    tall = still((rows, model), lambda f, m: (0, 0))
    act = pl.BlockSpec((rows, step), lambda f, m: (0, f))
    return call(
        mlp_kernel,
        deps=deps,
        gates=gates,
        **dict(
            prefetch=1,
            grid=(units // step,),
            in_specs=[tall, still((None, rows, model), lambda f, m: (m[0], 0, 0)),
                      pl.BlockSpec((model, step), lambda f, m: (0, f)),
                      pl.BlockSpec((step, model), lambda f, m: (f, 0))],
            out_specs=[act, act, tall],
            scratch_shapes=[pltpu.VMEM((rows, model), F32)],
        ),
        out_shape=[jax.ShapeDtypeStruct((rows, units), BF)] * 2
        + [jax.ShapeDtypeStruct((rows, model), dtype)],
        compiler_params=pltpu.CompilerParams(vmem_limit_bytes=mib(20.7)),
        cost_estimate=cost(6.4),
    )(which, normed, cot, w_up, w_down)


def branch_kernel(own, oth, w_down, out_own, out_oth, sum_own, sum_oth):
    step = pl.program_id(0)
    for source, total, out in ((own, sum_own, out_own), (oth, sum_oth, out_oth)):
        part = dot(source[...], w_down[...])

        @pl.when(step == 0)
        def _():
            total[...] = part

        @pl.when(step > 0)
        def _():
            total[...] += part

        @pl.when(step == pl.num_programs(0) - 1)
        def _():
            out[...] = total[...].astype(out.dtype)


def branches(own, oth, w_down, deps=(), gates=()):
    rows, units = own.shape
    model = w_down.shape[1]
    step = 512
    tall = still((rows, model), lambda f: (0, 0))
    act = pl.BlockSpec((rows, step), lambda f: (0, f))
    return call(
        branch_kernel,
        deps=deps,
        gates=gates,
        grid=(units // step,),
        in_specs=[act, act, pl.BlockSpec((step, model), lambda f: (f, 0))],
        out_specs=[tall, tall],
        out_shape=[jax.ShapeDtypeStruct((rows, model), BF)] * 2,
        scratch_shapes=[pltpu.VMEM((rows, model), F32)] * 2,
        compiler_params=pltpu.CompilerParams(vmem_limit_bytes=mib(23.3)),
        cost_estimate=cost(TAIL * 6),
        from_hbm=True,
    )(own, oth, w_down)


def turn_kernel(
    me, dn_own, dn_got, middle, cot, a_one, a_two, w_one, w_two, gain,
    dbranch, da_one, da_two, row_one, row_two, sums,
):
    step = pl.program_id(0)
    dn = dn_own[...].astype(F32) + dn_got[...].astype(F32)
    unit, inverse = row_stats(middle[...])
    value = cot[...].astype(F32) + norm_back(dn, unit, inverse, gain[...])
    low = value.astype(BF)
    dbranch[...] = low
    for a, w, da, row in ((a_one, w_one, da_one, row_one), (a_two, w_two, da_two, row_two)):
        grad = dot_nt(low, w[...]).astype(BF)
        da[...] = grad
        product = (grad.astype(F32) * a[...].astype(F32)).T
        heads = row.shape[0]
        row[:, 0, :] = jnp.sum(product.reshape(heads, -1, TILE), axis=1)

    @pl.when(step == 0)
    def _():
        sums[...] = jnp.zeros_like(sums)

    sums[0:1, :] += jnp.sum(dn * unit, axis=0, keepdims=True)
    sums[1:2, :] += jnp.sum(dn, axis=0, keepdims=True)


def turn(me, dn_own, dn_got, middle, cot, a_one, a_two, w_one, w_two, gain, heads, deps=(), gates=()):
    rows, model = middle.shape
    width = a_one.shape[1]
    tall = pl.BlockSpec((TILE, model), lambda i, m: (i, 0))
    part = pl.BlockSpec((TILE, width), lambda i, m: (i, 0))
    lane = pl.BlockSpec((heads, 1, TILE), lambda i, m: (0, 0, i))
    fixed = lambda shape: still(shape, lambda i, m: (0, 0))
    return call(
        turn_kernel,
        deps=deps,
        gates=gates,
        **dict(
            prefetch=1,
            grid=(rows // TILE,),
            in_specs=[tall, tall, tall,
                      pl.BlockSpec((None, TILE, model), lambda i, m: (m[0], i, 0)),
                      part, part, fixed((width, model)), fixed((width, model)), fixed((1, model))],
            out_specs=[tall, part, part, lane, lane, fixed((8, model))],
        ),
        out_shape=[
            jax.ShapeDtypeStruct((rows, model), BF),
            jax.ShapeDtypeStruct((rows, width), BF),
            jax.ShapeDtypeStruct((rows, width), BF),
            jax.ShapeDtypeStruct((heads, 1, rows), F32),
            jax.ShapeDtypeStruct((heads, 1, rows), F32),
            jax.ShapeDtypeStruct((8, model), F32),
        ],
        compiler_params=pltpu.CompilerParams(vmem_limit_bytes=mib(17.4)),
        cost_estimate=cost(TAIL * 5),
    )(me, dn_own, dn_got, middle, cot, a_one, a_two, w_one, w_two, gain.reshape(1, model))


def spread_kernel(ka, va, kb, vb, wka, wva, wkb, wvb, near, four, three, two, held, *, slots):
    step = pl.program_id(0)
    value = dot_nt(ka[...], wka[...]) + dot_nt(va[...], wva[...])
    value = value + dot_nt(kb[...], wkb[...]) + dot_nt(vb[...], wvb[...])

    @pl.when(step == 0)
    def _():
        near[...] = value.astype(BF)

    @pl.when(step == 1)
    def _():
        rows = value.shape[0]
        held[:rows, :] = value
        held[rows:, :] = jnp.zeros((held.shape[0] - rows, value.shape[1]), F32)
        padded = four.shape[0]
        live = lax.broadcasted_iota(jnp.int32, four.shape, 0) < slots
        for index, out in enumerate((four, three, two)):
            part = held[index * slots : index * slots + padded, :]
            out[...] = jnp.where(live, part, 0.0).astype(BF)


def spread(ka, va, kb, vb, wa, wb, slots, padded, deps=(), gates=()):
    rows, width = ka.shape[0] // 2, ka.shape[1]
    model = wa.shape[1]
    part = pl.BlockSpec((rows, width), lambda i: (i, 0))
    weight = lambda t: still((None, model, width), lambda i: (t, 0, 0))
    fixed = lambda *shape: still(shape, lambda i: (0, 0))
    little = jax.ShapeDtypeStruct((padded, model), BF)
    return call(
        functools.partial(spread_kernel, slots=slots),
        deps=deps,
        gates=gates,
        grid=(2,),
        in_specs=[part] * 4 + [weight(1), weight(2)] * 2,
        out_specs=[fixed(rows, model)] + [fixed(padded, model)] * 3,
        out_shape=[jax.ShapeDtypeStruct((rows, model), BF), little, little, little],
        scratch_shapes=[pltpu.VMEM((rows + 16, model), F32)],
        compiler_params=pltpu.CompilerParams(vmem_limit_bytes=mib(17.4)),
        cost_estimate=cost(TAIL * 6),
    )(ka, va, kb, vb, wa, wa, wb, wb)


def base_kernel(q, k, v, kc, vc, w, *refs, more):
    before, slot_before = refs[:2] if more else (None, None)
    base, slot_base, total, slot_total = refs[-4:]
    step = pl.program_id(0)
    for index, part in enumerate((q, k, v)):

        @pl.when(step == index)
        def _():
            value = dot_nt(part[...], w[...])
            if index > 0:
                value = value + total[...]
            elif more:
                value = value + before[...].astype(F32)
            if index == 2:
                base[...] = value.astype(BF)
            else:
                total[...] = value

    for index, part in enumerate((kc, vc)):

        @pl.when(step == index + 1)
        def _():
            value = dot_nt(part[...], w[...])
            if index > 0:
                value = value + slot_total[...]
            elif more:
                value = value + slot_before[...].astype(F32)
            if index == 1:
                slot_base[...] = value.astype(BF)
            else:
                slot_total[...] = value


def base_rows(near, slot, w, before, deps=(), gates=()):
    rows, width = near[0].shape
    padded = slot[0].shape[0]
    model = w.shape[1]
    fixed = lambda *shape: still(shape, lambda i: (0, 0))
    outs = [fixed(rows, model), fixed(padded, model)]
    return call(
        functools.partial(base_kernel, more=bool(before)),
        deps=deps,
        gates=gates,
        grid=(3,),
        in_specs=[fixed(rows, width)] * 3 + [fixed(padded, width)] * 2
        + [pl.BlockSpec((None, model, width), lambda i: (i, 0, 0))]
        + outs[: len(before)],
        out_specs=outs,
        out_shape=[
            jax.ShapeDtypeStruct((rows, model), BF),
            jax.ShapeDtypeStruct((padded, model), BF),
        ],
        scratch_shapes=[pltpu.VMEM((rows, model), F32), pltpu.VMEM((padded, model), F32)],
        compiler_params=pltpu.CompilerParams(vmem_limit_bytes=mib(14.0)),
        cost_estimate=cost(TAIL * 3),
        from_hbm=True,
    )(*near, *slot, w, *before)


def packed_kernel(me, base, *refs):
    gots, (dpacked, mine, away, bias) = refs[:-4], refs[-4:]
    value = sum(part[...].astype(F32) for part in (base, *gots)).astype(BF)
    dpacked[...] = value
    half = mine.shape[1]
    first, second = value[:, :half], value[:, half:]
    low = me[0] == 0
    mine[...] = jnp.where(low, first, second)
    away[...] = jnp.where(low, second, first)
    bias[0:1, :] = jnp.sum(value.astype(F32), axis=0, keepdims=True)


def packed_back(me, base, gots, deps=(), gates=()):
    padded, model = base.shape
    whole = pl.BlockSpec(memory_space=pltpu.VMEM)
    little = jax.ShapeDtypeStruct((padded, model // 2), BF)
    return call(
        packed_kernel,
        deps=deps,
        gates=gates,
        in_specs=[pl.BlockSpec(memory_space=pltpu.SMEM), whole] + [whole] * len(gots),
        out_shape=[jax.ShapeDtypeStruct((padded, model), BF), little, little,
                   jax.ShapeDtypeStruct((8, model), F32)],
        compiler_params=pltpu.CompilerParams(vmem_limit_bytes=mib(14.0)),
        cost_estimate=cost(TAIL * 400),
    )(me, base, *gots)


def finish_kernel(
    me, base, back, dpacked, w_comp, tokens, dmiddle, gain, grad, sums, total, *, rows
):
    model = base.shape[1]
    padded = dpacked.shape[0]
    for lane in range(model // 128):
        wide = slice(lane * 128, (lane + 1) * 128)
        total[lane, :rows, :] = base[:, wide].astype(F32) + back[:, wide].astype(F32)
        total[lane, rows:, :] = jnp.zeros((total.shape[1] - rows, 128), F32)
    for tap in range(3):
        place = pl.ds(tap, padded, stride=3)
        term = dot_nt(dpacked[...], w_comp[tap])
        for lane in range(model // 128):
            value = total[lane, place, :] + term[:, lane * 128 : (lane + 1) * 128]
            total[lane, place, :] = value
    one = jnp.zeros((1, model), F32)
    two = jnp.zeros((1, model), F32)
    for start in range(0, rows, 128):
        part = slice(start, start + 128)
        dn = jnp.concatenate([total[lane, part, :] for lane in range(model // 128)], 1)
        unit, inverse = row_stats(tokens[part, :].astype(F32))
        value = dmiddle[part, :].astype(F32) + norm_back(dn, unit, inverse, gain[...])
        grad[part, :] = value.astype(BF)
        one = one + jnp.sum(dn * unit, axis=0, keepdims=True)
        two = two + jnp.sum(dn, axis=0, keepdims=True)
    sums[0:1, :] = one
    sums[1:2, :] = two


def finish(me, base, back, dpacked, w_comp, tokens, dmiddle, gain, deps=(), gates=()):
    rows, model = base.shape
    padded = dpacked.shape[0]
    fixed = lambda *shape: still(shape, lambda i, m: (0,) * len(shape))
    return call(
        functools.partial(finish_kernel, rows=rows),
        deps=deps,
        gates=gates,
        **dict(
            prefetch=1,
            grid=(1,),
            in_specs=[fixed(rows, model), fixed(rows, model), fixed(padded, model),
                      fixed(*w_comp.shape),
                      still((None, rows, model), lambda i, m: (m[0], 0, 0)),
                      fixed(rows, model), fixed(1, model)],
            out_specs=[fixed(rows, model), fixed(8, model)],
            scratch_shapes=[pltpu.VMEM((model // 128, 3 * padded + 8, 128), F32)],
        ),
        out_shape=[
            jax.ShapeDtypeStruct((rows, model), BF),
            jax.ShapeDtypeStruct((8, model), F32),
        ],
        compiler_params=pltpu.CompilerParams(vmem_limit_bytes=mib(21.1)),
        cost_estimate=cost(TAIL * 4),
    )(me, base, back, dpacked, w_comp, tokens, dmiddle, gain.reshape(1, model))


def weight_kernel(core, *refs, plan, block, share):
    if share:
        operands, (parts, token, held) = refs[:-3], refs[-3:]
    else:
        operands, (held, token) = refs[:-2], refs[-2:]
    token[...] = jnp.zeros_like(token)
    tall = held.shape[0]
    at = 0
    for pairs, columns in plan:
        for start in range(0, columns, block):
            wide = slice(start, min(start + block, columns))
            value = None
            for a, b in pairs:
                term = lax.dot_general(
                    operands[a][...], operands[b][:, wide], (((0,), (0,)), ((), ())),
                    preferred_element_type=F32,
                )
                value = term if value is None else value + term
            held[:, at + start : at + wide.stop] = value.astype(BF)
        at += columns
    if not share:
        return
    for index in range(tall // (2 * share)):
        for side in range(2):
            here = (2 * index + side) * share
            parts[side, index * share : (index + 1) * share, :] = held[here : here + share, :]


def weight_grads(scalars, sections, share, model, limit, tall=512, deps=(), gates=()):
    operands, specs, plan, total = [], [], [], 0
    known = {}

    def place(array, kind, at, columns, depth):
        key = (id(array), kind, at, columns)
        if key not in known:
            known[key] = len(operands)
            operands.append(array)
            if kind == "b":
                col, row = at
                spec = still(
                    (depth, columns), lambda i, c, f=col // columns, r=row // depth: (r, f)
                )
            elif array.ndim == 3:
                spec = pl.BlockSpec((None, depth, tall), lambda i, c, t=at: ((c[1] + t) % 2, 0, i))
            else:
                spec = pl.BlockSpec((depth, tall), lambda i, c, f=at // tall: (0, f + i))
            specs.append(spec)
        return known[key]

    for pairs in sections:
        columns = pairs[0][4]
        plan.append(
            (
                [
                    (
                        place(a, "a", pa, 0, a.shape[-2]),
                        place(b, "b", pb, columns, a.shape[-2]),
                    )
                    for a, pa, b, pb, _ in pairs
                ],
                columns,
            )
        )
        total += columns
    tile = tall // 2 if share else tall
    if share:
        out = [pl.BlockSpec((2, tile, total), lambda i, c: (0, i, 0))]
        shape = [jax.ShapeDtypeStruct((2, tile * (model // tall), total), BF)]
    else:
        out = [pl.BlockSpec((tile, total), lambda i, c: (i, 0))]
        shape = [jax.ShapeDtypeStruct((model, total), BF)]
    out.append(pl.BlockSpec((8, 128), lambda i, c: (0, 0)))
    shape.append(jax.ShapeDtypeStruct((8, 128), F32))
    flops = sum(2 * model * p[4] * p[0].shape[-2] for pairs in sections for p in pairs)
    return call(
        functools.partial(weight_kernel, plan=tuple(plan), block=512, share=share),
        deps=deps,
        gates=gates,
        **dict(
            prefetch=1,
            grid=(model // tall,),
            in_specs=specs,
            out_specs=out,
            scratch_shapes=[pltpu.VMEM((tall, total), BF)] if share else [],
        ),
        out_shape=shape,
        compiler_params=pltpu.CompilerParams(vmem_limit_bytes=mib(limit)),
        cost_estimate=cost(TAIL * flops * 1.4e-9),
        to_hbm=True,
    )(scalars, *operands)


def sum_kernel(*refs, split):
    terms, outs = refs[:-split], refs[-split:]
    total = sum(term[...].astype(F32) for term in terms)
    wide = total.shape[1] // split
    for index, out in enumerate(outs):
        out[...] = total[:, index * wide : (index + 1) * wide].astype(out.dtype)


def add(terms, split, deps=(), gates=()):
    rows, columns = terms[0].shape[-2:]
    wide = columns // split
    tile = TILE if rows % TILE == 0 else rows
    blocks, operands = [], []
    for term in terms:
        if term.ndim == 3:
            for t in range(term.shape[0]):
                blocks.append(pl.BlockSpec((None, tile, columns), lambda i, t=t: (t, i, 0)))
                operands.append(term)
        else:
            blocks.append(pl.BlockSpec((tile, columns), lambda i: (i, 0)))
            operands.append(term)
    return call(
        functools.partial(sum_kernel, split=split),
        deps=deps,
        gates=gates,
        grid=(rows // tile,),
        in_specs=blocks,
        out_specs=[pl.BlockSpec((tile, wide), lambda i: (i, 0))] * split,
        out_shape=[jax.ShapeDtypeStruct((rows, wide), BF)] * split,
        compiler_params=pltpu.CompilerParams(vmem_limit_bytes=mib(14)),
        cost_estimate=cost(TAIL * 2),
        from_hbm=True,
    )(*operands)


def halve_kernel(bit, *refs, blocks, stride, terms):
    parts, outs = refs[:terms], refs[terms:]
    rows = parts[0].shape[0] // blocks
    mine = bit[0]
    if len(outs) == 1:
        outs[0][...] = sum(part[...].astype(F32) for part in parts).astype(outs[0].dtype)
        return
    for out, side in zip(outs, (mine, 1 - mine)):
        for j in range(blocks // 2):
            at = (j // stride * 2 * stride + j % stride) * rows + side * (stride * rows)
            place = pl.ds(pl.multiple_of(at, rows), rows)
            total = sum(part[place, :].astype(F32) for part in parts)
            out[j * rows : (j + 1) * rows, :] = total.astype(BF)


def halve(bit, parts, blocks, stride, columns, deps=(), gates=()):
    rows = parts[0][0].shape[-2]
    last = blocks == 1
    shape = jax.ShapeDtypeStruct((rows if last else rows // 2, columns), F32 if last else BF)
    return call(
        functools.partial(halve_kernel, blocks=blocks, stride=stride, terms=len(parts)),
        deps=deps,
        gates=gates,
        **dict(
            prefetch=1,
            grid=(1,),
            in_specs=[
                still((rows, columns), lambda i, m, f=part[1] // columns: (0, f))
                if len(part) == 2
                else still(
                    (None, rows, columns), lambda i, m, f=part[1] // columns, t=part[2]: (t, 0, f)
                )
                for part in parts
            ],
            out_specs=[still(shape.shape, lambda i, m: (0, 0))] * (1 if last else 2),
        ),
        out_shape=[shape] * (1 if last else 2),
        compiler_params=pltpu.CompilerParams(vmem_limit_bytes=mib(14.0)),
        cost_estimate=cost(TAIL * 3),
    )(bit, *[part[0] for part in parts])


class Halving:
    def __init__(self, parts, columns, order, position):
        self.parts, self.columns, self.order = parts, columns, list(order)
        self.position = position
        self.blocks = lax.axis_size(BLK)
        self.left = list(range(self.blocks.bit_length() - 2, -1, -1))

    def step(self, *deps, gates=()):
        bit = self.order.pop(0)
        place = len(self.left) - 1 - self.left.index(bit)
        mine = scalar((self.position >> bit) & 1)
        keep, away, *rest = halve(
            mine, self.parts, self.blocks, 1 << place, self.columns, deps, gates
        )
        self.parts = [(keep, 0), (swap(away, BLK, 1 << bit), 0)]
        self.left.remove(bit)
        self.blocks //= 2
        return (away, *rest) if rest else away

    def last(self, *deps):
        while self.order:
            self.step(*deps)
        return halve(scalar(self.position), self.parts, 1, 1, self.columns, deps)[0]


def scalar(x):
    return x.reshape(1).astype(jnp.int32)


def total_kernel(one, two, out):
    out[...] = one[...] + two[...]


def butterfly_steps():
    blocks = lax.axis_size(BLK)
    return [(DP, 1)] + [(BLK, 1 << i) for i in range(blocks.bit_length() - 1)] + [(HEAD, 1)]


def butterfly_add(x, got, deps=()):
    whole = pl.BlockSpec(memory_space=pltpu.VMEM)
    return call(
        total_kernel,
        deps=deps,
        in_specs=[whole, whole],
        out_shape=[jax.ShapeDtypeStruct(x.shape, F32)],
        cost_estimate=cost(TAIL),
    )(x, got)[0]


def in_order(mine, first, second, axis):
    return jnp.where(
        mine == 0, jnp.concatenate([first, second], axis), jnp.concatenate([second, first], axis)
    )


def pick(x, index, axis=0):
    return lax.dynamic_index_in_dim(x, index, axis, keepdims=False)


def shards(
    tokens, doc_ids, w_qkv, w_out, slopes, w_up, w_down, w_comp, comp_bias,
    norm1_gain, norm1_bias, norm2_gain, norm2_bias, out_cot, recon_cot,
):
    seqs, rows, model = tokens.shape
    heads = slopes.shape[0]
    width = w_qkv.shape[2]
    hd = width // heads
    slots = rows // 3
    used = 3 * slots
    padded = -(-slots // 16) * 16
    memory = CSEGS * slots
    position = lax.axis_index(BLK)
    core = lax.axis_index(DP)
    me = lax.axis_index(HEAD)
    ot = 1 - me
    scaling = hd ** (-0.5)
    half = model // 2
    share = model // (lax.axis_size(BLK) * lax.axis_size(DP))
    bits = lax.axis_size(BLK).bit_length() - 1
    rising = list(range(bits))
    falling = [1, 0] + rising[2:]
    scalars = jnp.stack([core, me]).astype(jnp.int32)
    me_arg, ot_arg = me.reshape(1).astype(jnp.int32), ot.reshape(1).astype(jnp.int32)

    small = jnp.concatenate(
        [pick(recon_cot, ot), jnp.pad(slopes, (0, rows - heads)).reshape(1, rows)], 0
    )
    small_got = swap(small, HEAD)
    half_rows = model // 2
    qkv_part = lax.dynamic_slice_in_dim(w_qkv, core * half_rows, half_rows, 1)
    out_part = lax.dynamic_slice_in_dim(w_out, core * half_rows, half_rows, 1)
    far_part = jnp.concatenate([qkv_part, out_part[None]], 0)
    far_got = swap(far_part, HEAD)
    groups = (OWN, OTH)

    halo_raw = shift(pick(tokens, me), BLK, 1)
    normed, tri_own, tri_oth = front(
        me_arg, tokens, norm1_gain, norm1_bias, slots, padded, deps=(far_part, small)
    )
    packed = dot(tri_own, w_comp.reshape(3 * model, model)) + comp_bias
    packed = packed.astype(BF)
    lag2, lag3 = shift(packed, BLK, 2), shift(packed, BLK, 3)

    docs = pick(doc_ids, me)
    query_doc = lax.dynamic_slice_in_dim(docs, position * rows, rows, 0).reshape(1, rows)
    padded_doc = jnp.concatenate([jnp.full(((CSEGS + 1) * rows,), -1, jnp.int32), docs])
    window = lax.dynamic_slice_in_dim(padded_doc, position * rows, (CSEGS + 2) * rows, 0)
    window = jnp.broadcast_to(window[:, None], ((CSEGS + 2) * rows, 128))
    (far,) = far_log(
        position.reshape(1).astype(jnp.int32), window, query_doc, slots, deps=(packed,)
    )

    weights, outs = {OWN: w_qkv}, {OWN: w_out}
    cots = {OWN: pick(recon_cot, me).reshape(heads, 1, rows)}
    slope = {OWN: slopes}
    q, ko, vo, kc, vc, rec, kf, vf, att, lse = ({} for _ in range(10))
    q[OWN], ko[OWN], vo[OWN], kc[OWN], vc[OWN], lag2 = project(
        normed, packed, w_qkv, deps=(far,), gates=(lag2,)
    )
    lag4 = shift(lag2, BLK, 2)
    cots[OTH] = small_got[:heads].reshape(heads, 1, rows)
    slope[OTH] = small_got[heads, :heads]
    rec[OWN] = recon_both(
        q[OWN], ko[OWN], vo[OWN], kc[OWN], vc[OWN], cots[OWN], slots, scaling,
    )
    mem = jnp.zeros((rows, model), BF)
    for index, lag in enumerate((lag4, lag3, lag2)):
        place = (index * slots, rows - (index + 1) * slots)
        mem = mem + jnp.pad(lag[:slots], (place, (0, 0)))
    halo = norm_halo(halo_raw, norm1_gain, norm1_bias, deps=(rec[OWN][0],))[0]
    kf[OWN], vf[OWN], far_got = project_distant(halo, mem, w_qkv, gates=(far_got,))
    near_got = swap(far_got, DP)
    att[OWN], lse[OWN] = attend_forward(
        slope[OWN], q[OWN], kf[OWN], vf[OWN], ko[OWN], vo[OWN], far, scaling
    )
    weights[OTH] = in_order(core, far_got[:3], near_got[:3], 1)
    outs[OTH] = in_order(core, far_got[3], near_got[3], 1)
    q[OTH], ko[OTH], vo[OTH], kc[OTH], vc[OTH] = project(
        normed, packed, weights[OTH], deps=(att[OWN],)
    )
    kf[OTH], vf[OTH] = project_distant(halo, mem, weights[OTH], deps=(q[OTH],))
    att[OTH], lse[OTH] = attend_forward(
        slope[OTH], q[OTH], kf[OTH], vf[OTH], ko[OTH], vo[OTH], far, scaling
    )

    middle, n2_own = middle_norm(
        me_arg, tokens, att[OWN], att[OTH], w_out, outs[OTH], norm2_gain, norm2_bias
    )
    n2_oth = swap(n2_own, HEAD)
    rec[OTH] = recon_both(
        q[OTH], ko[OTH], vo[OTH], kc[OTH], vc[OTH], cots[OTH], slots, scaling,
        deps=(n2_own,),
    )
    hid_own, din_own, dn_own = mlp(
        me_arg, n2_own, out_cot, w_up, w_down, BF, deps=(rec[OTH][0],)
    )
    hid_oth, din_oth, dn_oth = mlp(
        ot_arg, n2_oth, out_cot, w_up, w_down, BF, deps=(dn_own,)
    )
    dn_got = swap(dn_oth, HEAD)
    units = w_up.shape[1]
    up_down, token = weight_grads(
        scalars,
        [
            [(n2_own, 0, din_own, (0, 0), units), (n2_oth, 0, din_oth, (0, 0), units)],
            [(out_cot, 0, hid_own, (0, 0), units), (out_cot, 1, hid_oth, (0, 0), units)],
        ],
        0, model, 27.7, deps=(dn_oth,),
    )
    ffn_own, ffn_oth = branches(hid_own, hid_oth, w_down, deps=(token,))
    up_down = lax.psum_scatter(up_down, (BLK, DP), scatter_dimension=0, tiled=True)
    (
        dbranch, datt_own, datt_oth, row_own, row_oth, sums2,
        ffn_oth, recon_oth,
    ) = turn(
        me_arg, dn_own, dn_got, middle, out_cot, att[OWN], att[OTH], w_out, outs[OTH],
        norm2_gain, heads, gates=(ffn_oth, rec[OTH][0]),
    )
    ffn_got = swap(ffn_oth, HEAD)
    recon_got = swap(recon_oth.reshape(heads, rows), HEAD)
    datt = {OWN: datt_own, OTH: datt_oth}
    row = {OWN: row_own, OTH: row_oth}
    back, near, grads = {}, {}, {}

    def far_back(g, *deps):
        back[g] = attend_backward(
            slope[g], q[g], datt[g], lse[g], row[g], far, kf[g], vf[g], False, [], scaling,
            deps=deps, late=g == OWN,
        )

    def near_back(g, *deps, gates=()):
        r = rec[g]
        near[g] = attend_backward(
            slope[g], q[g], datt[g], lse[g], row[g], far, ko[g], vo[g], True,
            [back[g][0], r[1], r[2], r[3]], scaling, deps=deps, gates=gates, late=g == OWN,
        )

    def group_grads(g, *deps, gates=()):
        r = rec[g]
        sections = [[(normed, 0, near[g][0], (0, 0), width)]]
        for i in (1, 2):
            sections.append(
                [
                    (normed, 0, near[g][i], (0, 0), width),
                    (packed, 0, r[3 + i], (0, 0), width),
                    (halo, 0, back[g][i], (0, 0), width),
                    (mem, 0, back[g][i], (0, rows), width),
                ]
            )
        sections.append([(dbranch, 0, att[g], (0, 0), width)])
        grads[g] = weight_grads(
            scalars, sections, share, model, 26.4, deps=deps, gates=gates
        )

    far_back(OTH, dbranch)
    near_back(OTH)
    group_grads(OTH)
    cross = trade(grads[OTH][0])
    far_back(OWN, grads[OTH][1])
    (lo_own,) = add((middle, ffn_own, ffn_got), 1, deps=(back[OWN][3],))
    (cross,) = add((cross,), 1, deps=(lo_own,))
    cross_got = swap(cross, HEAD)
    halo_part, back4, back3, back2 = spread(
        back[OTH][1], back[OTH][2], back[OWN][1], back[OWN][2], weights[OTH], w_qkv,
        slots, padded, deps=(cross,),
    )
    slot_gots = [
        shift(part, BLK, -lag)
        for part, lag in zip((back4, back3, back2), range(CSEGS + 1, 1, -1))
    ]
    near_back(OWN, halo_part)
    group_grads(OWN)
    own = trade(grads[OWN][0])
    base_oth = base_rows(
        near[OTH][:3], rec[OTH][4:6], weights[OTH], [], deps=(grads[OWN][1],)
    )
    base, slot_base = base_rows(near[OWN][:3], rec[OWN][4:6], w_qkv, base_oth)
    wide = 2 * width
    late = Halving([(own, 0, 0), (own, 0, 1), (cross_got, 0)], 2 * wide, rising, position)
    moved = late.step(base)
    dpacked, dp_mine, dp_away, bias_sum, halo_part, lo_own = packed_back(
        me_arg, slot_base, slot_gots, deps=(moved,), gates=(halo_part, lo_own)
    )
    dp_got = swap(dp_away, HEAD)
    halo_back = shift(halo_part, BLK, -1)
    lo_got = swap(lo_own, HEAD)
    send, token = weight_grads(
        scalars,
        [
            [
                (tri_own, tap * model, dp_mine, (0, 0), half),
                (tri_oth, tap * model, dp_got, (0, 0), half),
            ]
            for tap in range(3)
        ],
        share, model, 19.1,
    )
    comp = trade(send)
    comp = Halving([(comp, 0, 0), (comp, 0, 1)], 3 * half, falling, position)
    moved = comp.step(token)
    moved = late.step(moved)
    grad_own, sums1 = finish(
        me_arg, base, halo_back, dpacked, w_comp, tokens, dbranch, norm1_gain,
        deps=(recon_got, moved),
    )
    dslopes = {}
    for g in groups:
        total = back[g][3] + near[g][3]
        dslopes[g] = -jnp.sum(total[:, 2] - total[:, 0] * total[:, 1], axis=1)
    both = in_order(me, dslopes[OWN], dslopes[OTH], 0)
    vector = jnp.concatenate(
        [sums1[0], sums1[1], sums2[0], sums2[1], bias_sum[0], jnp.pad(both, (0, 128 - 2 * heads))]
    ).reshape(-1, 128)
    rounds = butterfly_steps()
    vector_got = swap(vector, *rounds.pop(0))
    moved, grad_away = comp.step(sums1, gates=(grad_own,))
    grad_got = swap(grad_away, HEAD)
    vector = butterfly_add(vector, vector_got, deps=(moved,))
    vector_got = swap(vector, *rounds.pop(0))
    moved = vector
    while late.order or comp.order:
        if late.order:
            moved = late.step(moved)
        if comp.order:
            moved = comp.step(moved)
        vector = butterfly_add(vector, vector_got, deps=(moved,))
        vector_got = swap(vector, *rounds.pop(0))
        moved = vector
    up_sum, down_sum = up_down[:, :units].astype(F32), up_down[:, units:].astype(F32).T
    vector = butterfly_add(vector, vector_got, deps=(moved, up_sum, down_sum))
    vector_got = swap(vector, *rounds.pop(0))
    late = late.last(vector)
    while len(rounds) > 1:
        vector = butterfly_add(vector, vector_got, deps=(late,))
        vector_got = swap(vector, *rounds.pop(0))
    if rounds:
        vector = butterfly_add(vector, vector_got, deps=(late,))
        vector_got = swap(vector, *rounds.pop(0))
    grad_tokens = in_order(me, grad_own[None], grad_got[None], 0)
    comp = comp.last(vector, grad_tokens)
    vector = (vector + vector_got).reshape(-1)
    comp = comp.astype(BF)
    comp_got = swap(comp, HEAD)
    comp_all = in_order(
        me, comp.reshape(share, 3, half), comp_got.reshape(share, 3, half), 2
    ).astype(F32)

    slope_sum = lax.dynamic_slice_in_dim(vector, 5 * model + me * heads, heads, 0)

    recon_own = rec[OWN][0].reshape(heads, rows)
    recon = in_order(me, recon_own[None], recon_got[None], 0)
    layer_out = in_order(me, lo_own[None], lo_got[None], 0)
    return (
        layer_out,
        recon,
        grad_tokens,
        jnp.transpose(late[:, : 3 * width].reshape(share, 3, width), (1, 0, 2)),
        late[:, 3 * width :].T,
        slope_sum,
        up_sum,
        down_sum,
        jnp.transpose(comp_all, (1, 0, 2)),
        vector[4 * model : 5 * model],
        vector[:model],
        vector[model : 2 * model],
        vector[2 * model : 3 * model],
        vector[3 * model : 4 * model],
    )


def solution(mesh):
    in_specs = (
        P(DP, BLK, None),
        P(DP, None),
        P(None, None, HEAD),
        P(HEAD, None),
        P(HEAD),
        P(None, HEAD),
        P(HEAD, None),
        P(),
        P(),
        P(),
        P(),
        P(),
        P(),
        P(DP, BLK, None),
        P(DP, HEAD, BLK),
    )
    out_specs = (
        P(DP, BLK, None),
        P(DP, HEAD, BLK),
        P(DP, BLK, None),
        P(None, (BLK, DP), HEAD),
        P(HEAD, (BLK, DP)),
        P(HEAD),
        P((BLK, DP), HEAD),
        P(HEAD, (BLK, DP)),
        P(None, (BLK, DP), None),
        P(),
        P(),
        P(),
        P(),
        P(),
    )
    return jax.shard_map(shards, mesh=mesh, in_specs=in_specs, out_specs=out_specs, check_vma=False)
```

```python
import functools
import math

import jax
import jax.numpy as jnp
from jax import lax
from jax.experimental import pallas as pl
from jax.experimental.pallas import tpu as pltpu
from jax.sharding import PartitionSpec as P

CSEGS = 3
EPS = 1e-05
FAR = 1e30
LOG2E = math.log2(math.e)
BF = jnp.bfloat16
F32 = jnp.float32
TILE = 256
GROUP = 4
OWN, OTH = 0, 1
BLK, DP, HEAD = "blk", "dp", "head"
SHARE = 1 << 24
TAIL = 1.0


def mib(count):
    return int(count * (1 << 20))


def cost(us):
    return pl.CostEstimate(flops=int(us * SHARE), bytes_accessed=1 << 10, transcendentals=0)

NT = (((1,), (1,)), ((), ()))
GELU_A = math.sqrt(2.0 / math.pi)
GELU_B = 0.044715


def dot(a, b):
    return jnp.dot(a, b, preferred_element_type=F32)


def dot_nt(a, b):
    return lax.dot_general(a, b, NT, preferred_element_type=F32)


def dot_tn(a, b):
    return lax.dot_general(a, b, (((0,), (0,)), ((), ())), preferred_element_type=F32)


def shift(x, axis, by):
    devices = lax.axis_size(axis)
    pairs = [(i, i + by) for i in range(devices) if 0 <= i + by < devices]
    return lax.ppermute(x, axis, pairs)


def trade(x):
    return lax.all_to_all(x, DP, 0, 0)


def swap(x, axis, step=1):
    devices = lax.axis_size(axis)
    return lax.ppermute(x, axis, [(i, i ^ step) for i in range(devices)])


def call(
    kernel, deps=(), gates=(), prefetch=0, in_specs=None, from_hbm=False, to_hbm=False, **rest
):
    def run(*operands):
        count = len(operands)
        if from_hbm:
            operands = operands[:prefetch] + tuple(
                pltpu.with_memory_space_constraint(x, pltpu.HBM)
                if spec.memory_space is None else x
                for x, spec in zip(operands[prefetch:], in_specs)
            )
        passed = len(deps) + len(gates)
        specs = in_specs or [pl.BlockSpec(memory_space=pltpu.VMEM)] * count
        far = pl.BlockSpec(memory_space=pltpu.HBM)
        specs = list(specs) + [far] * passed

        def body(*refs):
            refs = refs[:count] + refs[count + passed :]
            results = count + len(rest_out)
            kernel(*refs[:results], *refs[results + len(gates) :])

        rest_out = list(rest["out_shape"])
        if to_hbm:
            rest_out = [pltpu.HBM(x.shape, x.dtype) for x in rest_out]
        settings = dict(rest)
        settings["out_shape"] = rest_out + [jax.ShapeDtypeStruct(g.shape, g.dtype) for g in gates]
        if gates:
            plain = [pl.BlockSpec(memory_space=pltpu.VMEM)] * len(rest_out)
            settings["out_specs"] = list(rest.get("out_specs", plain)) + [far] * len(gates)
            settings["input_output_aliases"] = {
                count + len(deps) + i: len(rest_out) + i for i in range(len(gates))
            }
        if prefetch:
            grid = {
                key: settings.pop(key)
                for key in ("grid", "out_specs", "scratch_shapes") if key in settings
            }
            settings["grid_spec"] = pltpu.PrefetchScalarGridSpec(
                num_scalar_prefetch=prefetch, in_specs=specs, **grid
            )
        else:
            settings["in_specs"] = specs
        return pl.pallas_call(body, **settings)(*operands, *deps, *gates)

    return run


def by_heads(kernel, count, width):
    def body(*refs):
        for index in range(count):
            columns = slice(index * width, (index + 1) * width)
            views = []
            for ref in refs:
                if len(ref.shape) == 3:
                    views.append(ref.at[index : index + 1])
                elif len(ref.shape) == 2 and ref.dtype == BF:
                    views.append(ref.at[:, columns])
                else:
                    views.append(ref)
            kernel(pl.program_id(0) * count + index, *views)

    return body


def still(shape, index_map):
    return pl.BlockSpec(shape, index_map, pipeline_mode=pl.Buffered(1))


def row_stats(x):
    center = x - jnp.mean(x, axis=-1, keepdims=True)
    inverse = lax.rsqrt(jnp.mean(center * center, axis=-1, keepdims=True) + EPS)
    return center * inverse, inverse


def norm_back(grad, unit, inverse, gain):
    scaled = grad * gain
    mean_one = jnp.mean(scaled, axis=-1, keepdims=True)
    mean_two = jnp.mean(scaled * unit, axis=-1, keepdims=True)
    return inverse * (scaled - mean_one - unit * mean_two)


def front_kernel(me, own, other, gain, bias, normed, tri_own, tri_other, unit, *, slots):
    rows, model = own.shape
    padded = tri_own.shape[0]
    for source, tri in ((own, tri_own), (other, tri_other)):
        for start in range(0, rows, 128):
            part = slice(start, start + 128)
            x, _ = row_stats(source[part, :].astype(F32))
            x = x * gain[...] + bias[...]
            for lane in range(model // 128):
                unit[lane, part, :] = x[:, lane * 128 : (lane + 1) * 128]
            if source is own:
                normed[part, :] = x.astype(BF)
        live = lax.broadcasted_iota(jnp.int32, (padded, 128), 0) < slots
        for lane in range(model // 128):
            unit[lane, rows:, :] = jnp.zeros((unit.shape[1] - rows, 128), F32)
            for tap in range(3):
                at = tap * model + lane * 128
                rows_of = unit[lane, pl.ds(tap, padded, stride=3), :]
                tri[:, at : at + 128] = jnp.where(live, rows_of, 0.0).astype(BF)


def front(me, tokens, gain, bias, slots, padded, deps=(), gates=()):
    _, rows, model = tokens.shape
    tri = jax.ShapeDtypeStruct((padded, 3 * model), BF)
    fixed = lambda shape: still(shape, lambda i, m: (0, 0))
    pick = lambda turn: still((None, rows, model), lambda i, m: ((m[0] + turn) % 2, 0, 0))
    return call(
        functools.partial(front_kernel, slots=slots),
        deps=deps,
        gates=gates,
        **dict(
            prefetch=1,
            grid=(1,),
            in_specs=[pick(0), pick(1), fixed((1, model)), fixed((1, model))],
            out_specs=[fixed((rows, model)), fixed((padded, 3 * model)), fixed((padded, 3 * model))],
            scratch_shapes=[pltpu.VMEM((model // 128, 3 * padded + 8, 128), F32)],
        ),
        out_shape=[jax.ShapeDtypeStruct((rows, model), BF), tri, tri],
        compiler_params=pltpu.CompilerParams(vmem_limit_bytes=mib(14.0)),
        cost_estimate=cost(0.02),
    )(me, tokens, tokens, gain.reshape(1, model), bias.reshape(1, model))


def norm_kernel(rows, gain, bias, normed):
    unit, _ = row_stats(rows[...].astype(F32))
    normed[...] = (unit * gain[...] + bias[...]).astype(BF)


def norm_halo(rows, gain, bias, deps=(), gates=()):
    count, model = rows.shape
    tall = pl.BlockSpec((TILE, model), lambda i: (i, 0))
    fixed = pl.BlockSpec((1, model), lambda i: (0, 0))
    return call(
        norm_kernel,
        deps=deps,
        gates=gates,
        grid=(count // TILE,),
        in_specs=[tall, fixed, fixed],
        out_specs=[tall],
        out_shape=[jax.ShapeDtypeStruct((count, model), BF)],
        compiler_params=pltpu.CompilerParams(vmem_limit_bytes=mib(14.0)),
        cost_estimate=cost(2),
    )(rows, gain.reshape(1, model), bias.reshape(1, model))


def distant_kernel(halo, mem, w, kf, vf):
    rows = halo.shape[0]
    for index, out in ((1, kf), (2, vf)):
        out[:rows, :] = dot(halo[...], w[index]).astype(BF)
        out[rows:, :] = dot(mem[...], w[index]).astype(BF)


def project_distant(halo, mem, w, deps=(), gates=()):
    rows, model = halo.shape
    width = w.shape[2]
    shape = jax.ShapeDtypeStruct((2 * rows, width), BF)
    return call(
        distant_kernel,
        deps=deps,
        gates=gates,
        out_shape=[shape, shape],
        compiler_params=pltpu.CompilerParams(vmem_limit_bytes=mib(14.0)),
        cost_estimate=cost(2.1),
    )(halo, mem, w)


def far_kernel(place, docs, query, out, mem, *, slots, rows):
    position = place[0]
    for seg in range(CSEGS):
        mem[seg * slots : (seg + 1) * slots, :] = docs[pl.ds(seg * rows, slots, stride=3), :]
    mem[CSEGS * slots :, :] = jnp.full((rows - CSEGS * slots, 128), -1, jnp.int32)
    column = lax.broadcasted_iota(jnp.int32, (1, rows), 1)
    step = 64
    for start in range(0, 3 * rows, step):
        local = lax.broadcasted_iota(jnp.int32, (step, 1), 0) + start % rows
        if start < rows:
            doc = docs[CSEGS * rows + start : CSEGS * rows + start + step, :1]
            where, live = local - rows, position > 0
        elif start < 2 * rows:
            doc = mem[start - rows : start - rows + step, :1]
            lead = sum((local >= seg * slots).astype(jnp.int32) for seg in range(1, CSEGS + 1))
            where = (lead - 1 - CSEGS) * rows + 3 * (local - lead * slots) + 1
            live = position - 1 - CSEGS + lead >= 0
        else:
            at = (CSEGS + 1) * rows + start - 2 * rows
            doc = docs[at : at + step, :1]
            where, live = local, position >= 0
        doc = jnp.where(live, doc, -2)
        apart = column - where
        seen = (apart >= 0) & (doc == query[...])
        value = jnp.log((1 + jnp.maximum(apart, 0)).astype(F32))
        out[start : start + step, :] = jnp.where(seen, value, FAR)


def far_log(place, docs, query, slots, deps=(), gates=()):
    rows = query.shape[1]
    return call(
        functools.partial(far_kernel, slots=slots, rows=rows),
        deps=deps,
        gates=gates,
        in_specs=[
            pl.BlockSpec(memory_space=pltpu.SMEM),
            pl.BlockSpec(memory_space=pltpu.VMEM),
            pl.BlockSpec(memory_space=pltpu.VMEM),
        ],
        out_shape=[jax.ShapeDtypeStruct((3 * rows, rows), F32)],
        scratch_shapes=[pltpu.VMEM((rows, 128), jnp.int32)],
        compiler_params=pltpu.CompilerParams(vmem_limit_bytes=mib(14.0)),
        cost_estimate=cost(0.02),
    )(place, docs, query)


def project_kernel(normed, packed, w, q, k, v, kc, vc):
    for index, out in enumerate((q, k, v)):
        out[...] = dot(normed[...], w[index]).astype(BF)
    kc[...] = dot(packed[...], w[1]).astype(BF)
    vc[...] = dot(packed[...], w[2]).astype(BF)


def project(normed, packed, w, deps=(), gates=()):
    rows, model = normed.shape
    padded, width = packed.shape[0], w.shape[2]
    near = jax.ShapeDtypeStruct((rows, width), BF)
    little = jax.ShapeDtypeStruct((padded, width), BF)
    return call(
        project_kernel,
        deps=deps,
        gates=gates,
        out_shape=[near, near, near, little, little],
        compiler_params=pltpu.CompilerParams(vmem_limit_bytes=mib(14.0)),
        cost_estimate=cost(2.0),
    )(normed, packed, w)


def forward_kernel(head, slopes, q, kf, vf, ko, vo, far, out, lse, *, scaling):
    c1 = scaling * LOG2E
    c2 = slopes[head] * LOG2E
    rows, reach = q.shape[0], kf.shape[0]
    vft, vot = vf[...].T, vo[...].T
    for qi in range(rows // TILE):
        qs = slice(qi * TILE, (qi + 1) * TILE)
        until = (qi + 1) * TILE
        qb = q[qs, :]
        near = dot_nt(ko[:until, :], qb) * c1 - c2 * far[reach : reach + until, qs]
        away = dot_nt(kf[...], qb) * c1 - c2 * far[:reach, qs]
        top = jnp.maximum(
            jnp.max(near, axis=0, keepdims=True), jnp.max(away, axis=0, keepdims=True)
        )
        near = jnp.exp2(near - top)
        away = jnp.exp2(away - top)
        total = jnp.sum(near, axis=0, keepdims=True) + jnp.sum(away, axis=0, keepdims=True)
        mixed = dot(vot[:, :until], near.astype(BF)) + dot(vft, away.astype(BF))
        out[qs, :] = (mixed / total).T.astype(BF)
        lse[0, :, qs] = top + jnp.log2(total)


def attend_forward(slopes, q, kf, vf, ko, vo, far, scaling, deps=(), gates=()):
    rows, width = q.shape
    reach = kf.shape[0]
    heads = slopes.shape[0]
    hd = width // heads
    near = pl.BlockSpec((rows, GROUP * hd), lambda h: (0, h))
    wide = pl.BlockSpec((reach, GROUP * hd), lambda h: (0, h))
    return call(
        by_heads(functools.partial(forward_kernel, scaling=scaling), GROUP, hd),
        deps=deps,
        gates=gates,
        grid=(heads // GROUP,),
        in_specs=[
            pl.BlockSpec(memory_space=pltpu.SMEM), near, wide, wide, near, near,
            still((reach + rows, rows), lambda h: (0, 0)),
        ],
        out_specs=[near, pl.BlockSpec((GROUP, 1, rows), lambda h: (h, 0, 0))],
        out_shape=[
            jax.ShapeDtypeStruct((rows, width), BF),
            jax.ShapeDtypeStruct((heads, 1, rows), F32),
        ],
        compiler_params=pltpu.CompilerParams(vmem_limit_bytes=mib(14.0)),
        cost_estimate=cost(3.2),
    )(slopes, q, kf, vf, ko, vo, far)


def backward_kernel(head, slopes, q, do, lse, dot_row, far, k, v, *refs, scaling, own):
    c1 = scaling * LOG2E
    c2 = slopes[head] * LOG2E
    extras = refs[:-4]
    dq, dk_out, dv_out, sums_out = refs[-4:]
    rows, hd = q.shape
    keys = k.shape[0]
    tall = rows
    dqs = [None] * (rows // TILE)
    for ki in range(keys // tall):
        base = ki * tall
        kt = k[base : base + tall, :].T
        dks, dvs = [], []
        for qi in range(rows // TILE):
            qs = slice(qi * TILE, (qi + 1) * TILE)
            until = (qi + 1) * TILE if own else tall
            ks = slice(base, base + until)
            qb, db = q[qs, :], do[qs, :]
            dist = far[ks, qs]
            s = dot_nt(k[ks, :], qb) * c1 - c2 * dist
            p = jnp.exp2(s - lse[0, :, qs])
            dp = dot_nt(v[ks, :], db)
            ds = p * (dp - dot_row[0, :, qs])
            for index, value in enumerate((ds, p * dist, ds * dist)):
                value = jnp.sum(value, axis=0, keepdims=True)
                if ki > 0:
                    value = value + sums_out[0, index : index + 1, qs]
                sums_out[0, index : index + 1, qs] = value
            p = p.astype(BF)
            ds = ds.astype(BF)
            dvs.append(dot(p, db))
            dks.append(dot(ds, qb))
            value = dot(kt[:, :until], ds)
            if ki > 0:
                value = value + dqs[qi]
            dqs[qi] = value
            if ki == keys // tall - 1:
                value = value.T * scaling
                if own:
                    value = value + extras[0][qs, :].astype(F32) + extras[1][qs, :].astype(F32)
                dq[qs, :] = value.astype(BF)
        for start in range(0, tall, TILE):
            ks = slice(base + start, base + start + TILE)
            dk = sum(d[start : start + TILE, :] for d in dks if d.shape[0] > start) * scaling
            dv = sum(d[start : start + TILE, :] for d in dvs if d.shape[0] > start)
            if own:
                dk = dk + extras[2][ks, :].astype(F32)
                dv = dv + extras[3][ks, :].astype(F32)
            dk_out[ks, :] = dk.astype(BF)
            dv_out[ks, :] = dv.astype(BF)


def attend_backward(
    slopes, q, do, lse, dot_row, far, k, v, own, extras, scaling, deps=(), gates=(), late=False
):
    rows, width = q.shape
    keys = k.shape[0]
    heads = slopes.shape[0]
    hd = width // heads
    near = pl.BlockSpec((rows, GROUP * hd), lambda h: (0, h))
    wide = pl.BlockSpec((keys, GROUP * hd), lambda h: (0, h))
    lane = pl.BlockSpec((GROUP, 1, rows), lambda h: (h, 0, 0))
    place = far.shape[0] // keys - 1 if own else 0
    return call(
        by_heads(functools.partial(backward_kernel, scaling=scaling, own=own), GROUP, hd),
        deps=deps,
        gates=gates,
        grid=(heads // GROUP,),
        in_specs=[
            pl.BlockSpec(memory_space=pltpu.SMEM), near, near, lane, lane,
            still((keys, rows), lambda h: (place, 0)), wide, wide,
        ]
        + [near] * len(extras),
        out_specs=[near, wide, wide, pl.BlockSpec((GROUP, 8, rows), lambda h: (h, 0, 0))],
        out_shape=[
            jax.ShapeDtypeStruct((rows, width), BF),
            jax.ShapeDtypeStruct((keys, width), BF),
            jax.ShapeDtypeStruct((keys, width), BF),
            jax.ShapeDtypeStruct((heads, 8, rows), F32),
        ],
        compiler_params=pltpu.CompilerParams(vmem_limit_bytes=mib(14.0)),
        cost_estimate=cost(TAIL * (5 if own else 9)),
        from_hbm=late,
    )(slopes, q, do, lse, dot_row, far, k, v, *extras)


def recon_kernel(head, q, ko, vo, kc, vc, cot, recon, dq, dk, dv, dkc, dvc, *, slots, scaling):
    rows, hd = q.shape
    c1 = scaling * LOG2E
    comp_rows = kc.shape[0]
    live = lax.broadcasted_iota(jnp.int32, (comp_rows, TILE), 0) < slots
    kct, vct, kot, vot = kc[...].T, vc[...].T, ko[...].T, vo[...].T
    for qi in range(rows // TILE):
        qs = slice(qi * TILE, (qi + 1) * TILE)
        qb = q[qs, :]
        full_s = dot_nt(ko[...], qb) * c1
        full_p = jnp.exp2(full_s - jnp.max(full_s, axis=0, keepdims=True))
        full_p = full_p * (1.0 / jnp.sum(full_p, axis=0, keepdims=True))
        full_low = full_p.astype(BF)
        comp_s = jnp.where(live, dot_nt(kc[...], qb) * c1, -FAR)
        comp_p = jnp.exp2(comp_s - jnp.max(comp_s, axis=0, keepdims=True))
        comp_p = comp_p * (1.0 / jnp.sum(comp_p, axis=0, keepdims=True))
        comp_low = comp_p.astype(BF)
        full, comp = dot(vot, full_low), dot(vct, comp_low)
        spread = full - comp
        recon[0, :, qs] = jnp.sum(spread * spread, axis=0, keepdims=True) / hd**0.5
        dfull = spread * (cot[0, :, qs] * (2.0 / hd**0.5))
        dfull_low = dfull.astype(BF)
        dfull_rows = dfull_low.T
        full_dw = dot(vo[...], dfull_low)
        comp_dw = dot(vc[...], dfull_low)
        row = jnp.sum(full_p * full_dw, axis=0, keepdims=True)
        full_ds = (full_p * (full_dw - row)).astype(BF)
        row = jnp.sum(comp_p * comp_dw, axis=0, keepdims=True)
        comp_ds = (comp_p * (row - comp_dw)).astype(BF)
        dq[qs, :] = ((dot(kot, full_ds) + dot(kct, comp_ds)).T * scaling).astype(BF)
        terms = (
            dot(full_ds, qb) * scaling, dot(full_low, dfull_rows),
            dot(comp_ds, qb) * scaling, -dot(comp_low, dfull_rows),
        )
        values = terms if qi == 0 else [a + b for a, b in zip(values, terms)]
    for ref, value in zip((dk, dv, dkc, dvc), values):
        ref[...] = value.astype(ref.dtype)


def recon_both(q, ko, vo, kc, vc, cot, slots, scaling, deps=(), gates=()):
    rows, width = q.shape
    heads = cot.shape[0]
    hd = width // heads
    comp_rows = kc.shape[0]
    near = pl.BlockSpec((rows, GROUP * hd), lambda h: (0, h))
    small = pl.BlockSpec((comp_rows, GROUP * hd), lambda h: (0, h))
    lane = pl.BlockSpec((GROUP, 1, rows), lambda h: (h, 0, 0))
    big = jax.ShapeDtypeStruct((rows, width), BF)
    little = jax.ShapeDtypeStruct((comp_rows, width), BF)
    return call(
        by_heads(functools.partial(recon_kernel, slots=slots, scaling=scaling), GROUP, hd),
        deps=deps,
        gates=gates,
        grid=(heads // GROUP,),
        in_specs=[near, near, near, small, small, lane],
        out_specs=[lane, near, near, near, small, small],
        out_shape=[jax.ShapeDtypeStruct((heads, 1, rows), F32), big, big, big, little, little],
        compiler_params=pltpu.CompilerParams(vmem_limit_bytes=mib(16)),
        cost_estimate=cost(4.3),
        to_hbm=True,
    )(q, ko, vo, kc, vc, cot)


def middle_kernel(me, tokens, a_one, a_two, w_one, w_two, gain, bias, middle, normed):
    value = tokens[...].astype(F32) + (dot(a_one[...], w_one[...]) + dot(a_two[...], w_two[...]))
    middle[...] = value
    unit, _ = row_stats(value)
    normed[...] = (unit * gain[...] + bias[...]).astype(BF)


def middle_norm(me, tokens, a_one, a_two, w_one, w_two, gain, bias, deps=(), gates=()):
    _, rows, model = tokens.shape
    width = a_one.shape[1]
    tall = pl.BlockSpec((TILE, model), lambda i, m: (i, 0))
    part = pl.BlockSpec((TILE, width), lambda i, m: (i, 0))
    fixed = lambda shape: still(shape, lambda i, m: (0, 0))
    return call(
        middle_kernel,
        deps=deps,
        gates=gates,
        **dict(
            prefetch=1,
            grid=(rows // TILE,),
            in_specs=[pl.BlockSpec((None, TILE, model), lambda i, m: (m[0], i, 0)), part, part,
                      fixed((width, model)), fixed((width, model)), fixed((1, model)),
                      fixed((1, model))],
            out_specs=[tall, tall],
        ),
        out_shape=[jax.ShapeDtypeStruct((rows, model), F32), jax.ShapeDtypeStruct((rows, model), BF)],
        compiler_params=pltpu.CompilerParams(vmem_limit_bytes=mib(14.0)),
        cost_estimate=cost(1.1),
    )(me, tokens, a_one, a_two, w_one, w_two, gain.reshape(1, model), bias.reshape(1, model))


def mlp_kernel(which, normed, cot, w_up, w_down, hidden, dinner, dnormed, dn_sum):
    step = pl.program_id(0)
    inner = dot(normed[...], w_up[...])
    dhidden = dot_nt(cot[...], w_down[...])
    square = inner * inner
    inside = jnp.tanh(inner * (GELU_A + (GELU_A * GELU_B) * square))
    bent = 0.5 * (1.0 + inside)
    hidden[...] = (inner * bent).astype(BF)
    slope = bent + inner * (0.5 - 0.5 * inside * inside) * (
        GELU_A + (3.0 * GELU_A * GELU_B) * square
    )
    dlow = (dhidden * slope).astype(BF)
    dinner[...] = dlow
    dn = dot_nt(dlow, w_up[...])

    @pl.when(step == 0)
    def _():
        dn_sum[...] = dn

    @pl.when(step > 0)
    def _():
        dn_sum[...] += dn

    @pl.when(step == pl.num_programs(0) - 1)
    def _():
        dnormed[...] = dn_sum[...].astype(dnormed.dtype)


def mlp(which, normed, cot, w_up, w_down, dtype, deps=(), gates=()):
    rows, model = normed.shape
    units = w_up.shape[1]
    step = 512
    tall = still((rows, model), lambda f, m: (0, 0))
    act = pl.BlockSpec((rows, step), lambda f, m: (0, f))
    return call(
        mlp_kernel,
        deps=deps,
        gates=gates,
        **dict(
            prefetch=1,
            grid=(units // step,),
            in_specs=[tall, still((None, rows, model), lambda f, m: (m[0], 0, 0)),
                      pl.BlockSpec((model, step), lambda f, m: (0, f)),
                      pl.BlockSpec((step, model), lambda f, m: (f, 0))],
            out_specs=[act, act, tall],
            scratch_shapes=[pltpu.VMEM((rows, model), F32)],
        ),
        out_shape=[jax.ShapeDtypeStruct((rows, units), BF)] * 2
        + [jax.ShapeDtypeStruct((rows, model), dtype)],
        compiler_params=pltpu.CompilerParams(vmem_limit_bytes=mib(20.7)),
        cost_estimate=cost(6.4),
    )(which, normed, cot, w_up, w_down)


def branch_kernel(own, oth, w_down, out_own, out_oth, sum_own, sum_oth):
    step = pl.program_id(0)
    for source, total, out in ((own, sum_own, out_own), (oth, sum_oth, out_oth)):
        part = dot(source[...], w_down[...])

        @pl.when(step == 0)
        def _():
            total[...] = part

        @pl.when(step > 0)
        def _():
            total[...] += part

        @pl.when(step == pl.num_programs(0) - 1)
        def _():
            out[...] = total[...].astype(out.dtype)


def branches(own, oth, w_down, deps=(), gates=()):
    rows, units = own.shape
    model = w_down.shape[1]
    step = 512
    tall = still((rows, model), lambda f: (0, 0))
    act = pl.BlockSpec((rows, step), lambda f: (0, f))
    return call(
        branch_kernel,
        deps=deps,
        gates=gates,
        grid=(units // step,),
        in_specs=[act, act, pl.BlockSpec((step, model), lambda f: (f, 0))],
        out_specs=[tall, tall],
        out_shape=[jax.ShapeDtypeStruct((rows, model), BF)] * 2,
        scratch_shapes=[pltpu.VMEM((rows, model), F32)] * 2,
        compiler_params=pltpu.CompilerParams(vmem_limit_bytes=mib(23.3)),
        cost_estimate=cost(TAIL * 6),
        from_hbm=True,
    )(own, oth, w_down)


def turn_kernel(
    me, dn_own, dn_got, middle, cot, a_one, a_two, w_one, w_two, gain,
    dbranch, da_one, da_two, row_one, row_two, sums,
):
    step = pl.program_id(0)
    dn = dn_own[...].astype(F32) + dn_got[...].astype(F32)
    unit, inverse = row_stats(middle[...])
    value = cot[...].astype(F32) + norm_back(dn, unit, inverse, gain[...])
    low = value.astype(BF)
    dbranch[...] = low
    for a, w, da, row in ((a_one, w_one, da_one, row_one), (a_two, w_two, da_two, row_two)):
        grad = dot_nt(low, w[...]).astype(BF)
        da[...] = grad
        product = (grad.astype(F32) * a[...].astype(F32)).T
        heads = row.shape[0]
        row[:, 0, :] = jnp.sum(product.reshape(heads, -1, TILE), axis=1)

    @pl.when(step == 0)
    def _():
        sums[...] = jnp.zeros_like(sums)

    sums[0:1, :] += jnp.sum(dn * unit, axis=0, keepdims=True)
    sums[1:2, :] += jnp.sum(dn, axis=0, keepdims=True)


def turn(me, dn_own, dn_got, middle, cot, a_one, a_two, w_one, w_two, gain, heads, deps=(), gates=()):
    rows, model = middle.shape
    width = a_one.shape[1]
    tall = pl.BlockSpec((TILE, model), lambda i, m: (i, 0))
    part = pl.BlockSpec((TILE, width), lambda i, m: (i, 0))
    lane = pl.BlockSpec((heads, 1, TILE), lambda i, m: (0, 0, i))
    fixed = lambda shape: still(shape, lambda i, m: (0, 0))
    return call(
        turn_kernel,
        deps=deps,
        gates=gates,
        **dict(
            prefetch=1,
            grid=(rows // TILE,),
            in_specs=[tall, tall, tall,
                      pl.BlockSpec((None, TILE, model), lambda i, m: (m[0], i, 0)),
                      part, part, fixed((width, model)), fixed((width, model)), fixed((1, model))],
            out_specs=[tall, part, part, lane, lane, fixed((8, model))],
        ),
        out_shape=[
            jax.ShapeDtypeStruct((rows, model), BF),
            jax.ShapeDtypeStruct((rows, width), BF),
            jax.ShapeDtypeStruct((rows, width), BF),
            jax.ShapeDtypeStruct((heads, 1, rows), F32),
            jax.ShapeDtypeStruct((heads, 1, rows), F32),
            jax.ShapeDtypeStruct((8, model), F32),
        ],
        compiler_params=pltpu.CompilerParams(vmem_limit_bytes=mib(17.4)),
        cost_estimate=cost(TAIL * 5),
    )(me, dn_own, dn_got, middle, cot, a_one, a_two, w_one, w_two, gain.reshape(1, model))


def spread_kernel(ka, va, kb, vb, wka, wva, wkb, wvb, near, four, three, two, held, *, slots):
    step = pl.program_id(0)
    value = dot_nt(ka[...], wka[...]) + dot_nt(va[...], wva[...])
    value = value + dot_nt(kb[...], wkb[...]) + dot_nt(vb[...], wvb[...])

    @pl.when(step == 0)
    def _():
        near[...] = value.astype(BF)

    @pl.when(step == 1)
    def _():
        rows = value.shape[0]
        held[:rows, :] = value
        held[rows:, :] = jnp.zeros((held.shape[0] - rows, value.shape[1]), F32)
        padded = four.shape[0]
        live = lax.broadcasted_iota(jnp.int32, four.shape, 0) < slots
        for index, out in enumerate((four, three, two)):
            part = held[index * slots : index * slots + padded, :]
            out[...] = jnp.where(live, part, 0.0).astype(BF)


def spread(ka, va, kb, vb, wa, wb, slots, padded, deps=(), gates=()):
    rows, width = ka.shape[0] // 2, ka.shape[1]
    model = wa.shape[1]
    part = pl.BlockSpec((rows, width), lambda i: (i, 0))
    weight = lambda t: still((None, model, width), lambda i: (t, 0, 0))
    fixed = lambda *shape: still(shape, lambda i: (0, 0))
    little = jax.ShapeDtypeStruct((padded, model), BF)
    return call(
        functools.partial(spread_kernel, slots=slots),
        deps=deps,
        gates=gates,
        grid=(2,),
        in_specs=[part] * 4 + [weight(1), weight(2)] * 2,
        out_specs=[fixed(rows, model)] + [fixed(padded, model)] * 3,
        out_shape=[jax.ShapeDtypeStruct((rows, model), BF), little, little, little],
        scratch_shapes=[pltpu.VMEM((rows + 16, model), F32)],
        compiler_params=pltpu.CompilerParams(vmem_limit_bytes=mib(17.4)),
        cost_estimate=cost(TAIL * 6),
    )(ka, va, kb, vb, wa, wa, wb, wb)


def base_kernel(q, k, v, kc, vc, w, *refs, more):
    before, slot_before = refs[:2] if more else (None, None)
    base, slot_base, total, slot_total = refs[-4:]
    step = pl.program_id(0)
    for index, part in enumerate((q, k, v)):

        @pl.when(step == index)
        def _():
            value = dot_nt(part[...], w[...])
            if index > 0:
                value = value + total[...]
            elif more:
                value = value + before[...].astype(F32)
            if index == 2:
                base[...] = value.astype(BF)
            else:
                total[...] = value

    for index, part in enumerate((kc, vc)):

        @pl.when(step == index + 1)
        def _():
            value = dot_nt(part[...], w[...])
            if index > 0:
                value = value + slot_total[...]
            elif more:
                value = value + slot_before[...].astype(F32)
            if index == 1:
                slot_base[...] = value.astype(BF)
            else:
                slot_total[...] = value


def base_rows(near, slot, w, before, deps=(), gates=()):
    rows, width = near[0].shape
    padded = slot[0].shape[0]
    model = w.shape[1]
    fixed = lambda *shape: still(shape, lambda i: (0, 0))
    outs = [fixed(rows, model), fixed(padded, model)]
    return call(
        functools.partial(base_kernel, more=bool(before)),
        deps=deps,
        gates=gates,
        grid=(3,),
        in_specs=[fixed(rows, width)] * 3 + [fixed(padded, width)] * 2
        + [pl.BlockSpec((None, model, width), lambda i: (i, 0, 0))]
        + outs[: len(before)],
        out_specs=outs,
        out_shape=[
            jax.ShapeDtypeStruct((rows, model), BF),
            jax.ShapeDtypeStruct((padded, model), BF),
        ],
        scratch_shapes=[pltpu.VMEM((rows, model), F32), pltpu.VMEM((padded, model), F32)],
        compiler_params=pltpu.CompilerParams(vmem_limit_bytes=mib(14.0)),
        cost_estimate=cost(TAIL * 3),
        from_hbm=True,
    )(*near, *slot, w, *before)


def packed_kernel(me, base, *refs):
    gots, (dpacked, mine, away, bias) = refs[:-4], refs[-4:]
    value = sum(part[...].astype(F32) for part in (base, *gots)).astype(BF)
    dpacked[...] = value
    half = mine.shape[1]
    first, second = value[:, :half], value[:, half:]
    low = me[0] == 0
    mine[...] = jnp.where(low, first, second)
    away[...] = jnp.where(low, second, first)
    bias[0:1, :] = jnp.sum(value.astype(F32), axis=0, keepdims=True)


def packed_back(me, base, gots, deps=(), gates=()):
    padded, model = base.shape
    whole = pl.BlockSpec(memory_space=pltpu.VMEM)
    little = jax.ShapeDtypeStruct((padded, model // 2), BF)
    return call(
        packed_kernel,
        deps=deps,
        gates=gates,
        in_specs=[pl.BlockSpec(memory_space=pltpu.SMEM), whole] + [whole] * len(gots),
        out_shape=[jax.ShapeDtypeStruct((padded, model), BF), little, little,
                   jax.ShapeDtypeStruct((8, model), F32)],
        compiler_params=pltpu.CompilerParams(vmem_limit_bytes=mib(14.0)),
        cost_estimate=cost(TAIL * 400),
    )(me, base, *gots)


def finish_kernel(
    me, base, back, dpacked, w_comp, tokens, dmiddle, gain, grad, sums, total, *, rows
):
    model = base.shape[1]
    padded = dpacked.shape[0]
    for lane in range(model // 128):
        wide = slice(lane * 128, (lane + 1) * 128)
        total[lane, :rows, :] = base[:, wide].astype(F32) + back[:, wide].astype(F32)
        total[lane, rows:, :] = jnp.zeros((total.shape[1] - rows, 128), F32)
    for tap in range(3):
        place = pl.ds(tap, padded, stride=3)
        term = dot_nt(dpacked[...], w_comp[tap])
        for lane in range(model // 128):
            value = total[lane, place, :] + term[:, lane * 128 : (lane + 1) * 128]
            total[lane, place, :] = value
    one = jnp.zeros((1, model), F32)
    two = jnp.zeros((1, model), F32)
    for start in range(0, rows, 128):
        part = slice(start, start + 128)
        dn = jnp.concatenate([total[lane, part, :] for lane in range(model // 128)], 1)
        unit, inverse = row_stats(tokens[part, :].astype(F32))
        value = dmiddle[part, :].astype(F32) + norm_back(dn, unit, inverse, gain[...])
        grad[part, :] = value.astype(BF)
        one = one + jnp.sum(dn * unit, axis=0, keepdims=True)
        two = two + jnp.sum(dn, axis=0, keepdims=True)
    sums[0:1, :] = one
    sums[1:2, :] = two


def finish(me, base, back, dpacked, w_comp, tokens, dmiddle, gain, deps=(), gates=()):
    rows, model = base.shape
    padded = dpacked.shape[0]
    fixed = lambda *shape: still(shape, lambda i, m: (0,) * len(shape))
    return call(
        functools.partial(finish_kernel, rows=rows),
        deps=deps,
        gates=gates,
        **dict(
            prefetch=1,
            grid=(1,),
            in_specs=[fixed(rows, model), fixed(rows, model), fixed(padded, model),
                      fixed(*w_comp.shape),
                      still((None, rows, model), lambda i, m: (m[0], 0, 0)),
                      fixed(rows, model), fixed(1, model)],
            out_specs=[fixed(rows, model), fixed(8, model)],
            scratch_shapes=[pltpu.VMEM((model // 128, 3 * padded + 8, 128), F32)],
        ),
        out_shape=[
            jax.ShapeDtypeStruct((rows, model), BF),
            jax.ShapeDtypeStruct((8, model), F32),
        ],
        compiler_params=pltpu.CompilerParams(vmem_limit_bytes=mib(21.1)),
        cost_estimate=cost(TAIL * 4),
    )(me, base, back, dpacked, w_comp, tokens, dmiddle, gain.reshape(1, model))


def weight_kernel(core, *refs, plan, block, share):
    if share:
        operands, (parts, token, held) = refs[:-3], refs[-3:]
    else:
        operands, (held, token) = refs[:-2], refs[-2:]
    token[...] = jnp.zeros_like(token)
    tall = held.shape[0]
    at = 0
    for pairs, columns in plan:
        for start in range(0, columns, block):
            wide = slice(start, min(start + block, columns))
            value = None
            for a, b in pairs:
                term = lax.dot_general(
                    operands[a][...], operands[b][:, wide], (((0,), (0,)), ((), ())),
                    preferred_element_type=F32,
                )
                value = term if value is None else value + term
            held[:, at + start : at + wide.stop] = value.astype(BF)
        at += columns
    if not share:
        return
    for index in range(tall // (2 * share)):
        for side in range(2):
            here = (2 * index + side) * share
            parts[side, index * share : (index + 1) * share, :] = held[here : here + share, :]


def weight_grads(scalars, sections, share, model, limit, tall=512, deps=(), gates=()):
    operands, specs, plan, total = [], [], [], 0
    known = {}

    def place(array, kind, at, columns, depth):
        key = (id(array), kind, at, columns)
        if key not in known:
            known[key] = len(operands)
            operands.append(array)
            if kind == "b":
                col, row = at
                spec = still(
                    (depth, columns), lambda i, c, f=col // columns, r=row // depth: (r, f)
                )
            elif array.ndim == 3:
                spec = pl.BlockSpec((None, depth, tall), lambda i, c, t=at: ((c[1] + t) % 2, 0, i))
            else:
                spec = pl.BlockSpec((depth, tall), lambda i, c, f=at // tall: (0, f + i))
            specs.append(spec)
        return known[key]

    for pairs in sections:
        columns = pairs[0][4]
        plan.append(
            (
                [
                    (
                        place(a, "a", pa, 0, a.shape[-2]),
                        place(b, "b", pb, columns, a.shape[-2]),
                    )
                    for a, pa, b, pb, _ in pairs
                ],
                columns,
            )
        )
        total += columns
    tile = tall // 2 if share else tall
    if share:
        out = [pl.BlockSpec((2, tile, total), lambda i, c: (0, i, 0))]
        shape = [jax.ShapeDtypeStruct((2, tile * (model // tall), total), BF)]
    else:
        out = [pl.BlockSpec((tile, total), lambda i, c: (i, 0))]
        shape = [jax.ShapeDtypeStruct((model, total), BF)]
    out.append(pl.BlockSpec((8, 128), lambda i, c: (0, 0)))
    shape.append(jax.ShapeDtypeStruct((8, 128), F32))
    flops = sum(2 * model * p[4] * p[0].shape[-2] for pairs in sections for p in pairs)
    return call(
        functools.partial(weight_kernel, plan=tuple(plan), block=512, share=share),
        deps=deps,
        gates=gates,
        **dict(
            prefetch=1,
            grid=(model // tall,),
            in_specs=specs,
            out_specs=out,
            scratch_shapes=[pltpu.VMEM((tall, total), BF)] if share else [],
        ),
        out_shape=shape,
        compiler_params=pltpu.CompilerParams(vmem_limit_bytes=mib(limit)),
        cost_estimate=cost(TAIL * flops * 1.4e-9),
        to_hbm=True,
    )(scalars, *operands)


def sum_kernel(*refs, split):
    terms, outs = refs[:-split], refs[-split:]
    total = sum(term[...].astype(F32) for term in terms)
    wide = total.shape[1] // split
    for index, out in enumerate(outs):
        out[...] = total[:, index * wide : (index + 1) * wide].astype(out.dtype)


def add(terms, split, deps=(), gates=()):
    rows, columns = terms[0].shape[-2:]
    wide = columns // split
    tile = TILE if rows % TILE == 0 else rows
    blocks, operands = [], []
    for term in terms:
        if term.ndim == 3:
            for t in range(term.shape[0]):
                blocks.append(pl.BlockSpec((None, tile, columns), lambda i, t=t: (t, i, 0)))
                operands.append(term)
        else:
            blocks.append(pl.BlockSpec((tile, columns), lambda i: (i, 0)))
            operands.append(term)
    return call(
        functools.partial(sum_kernel, split=split),
        deps=deps,
        gates=gates,
        grid=(rows // tile,),
        in_specs=blocks,
        out_specs=[pl.BlockSpec((tile, wide), lambda i: (i, 0))] * split,
        out_shape=[jax.ShapeDtypeStruct((rows, wide), BF)] * split,
        compiler_params=pltpu.CompilerParams(vmem_limit_bytes=mib(14)),
        cost_estimate=cost(TAIL * 2),
    )(*operands)


def halve_kernel(bit, *refs, blocks, stride, terms):
    parts, outs = refs[:terms], refs[terms:]
    rows = parts[0].shape[0] // blocks
    mine = bit[0]
    if len(outs) == 1:
        outs[0][...] = sum(part[...].astype(F32) for part in parts).astype(outs[0].dtype)
        return
    for out, side in zip(outs, (mine, 1 - mine)):
        for j in range(blocks // 2):
            at = (j // stride * 2 * stride + j % stride) * rows + side * (stride * rows)
            place = pl.ds(pl.multiple_of(at, rows), rows)
            total = sum(part[place, :].astype(F32) for part in parts)
            out[j * rows : (j + 1) * rows, :] = total.astype(BF)


def halve(bit, parts, blocks, stride, columns, deps=(), gates=()):
    rows = parts[0][0].shape[-2]
    last = blocks == 1
    shape = jax.ShapeDtypeStruct((rows if last else rows // 2, columns), F32 if last else BF)
    return call(
        functools.partial(halve_kernel, blocks=blocks, stride=stride, terms=len(parts)),
        deps=deps,
        gates=gates,
        **dict(
            prefetch=1,
            grid=(1,),
            in_specs=[
                still((rows, columns), lambda i, m, f=part[1] // columns: (0, f))
                if len(part) == 2
                else still(
                    (None, rows, columns), lambda i, m, f=part[1] // columns, t=part[2]: (t, 0, f)
                )
                for part in parts
            ],
            out_specs=[still(shape.shape, lambda i, m: (0, 0))] * (1 if last else 2),
        ),
        out_shape=[shape] * (1 if last else 2),
        compiler_params=pltpu.CompilerParams(vmem_limit_bytes=mib(14.0)),
        cost_estimate=cost(TAIL * 3),
    )(bit, *[part[0] for part in parts])


class Halving:
    def __init__(self, parts, columns, order, position):
        self.parts, self.columns, self.order = parts, columns, list(order)
        self.position = position
        self.blocks = lax.axis_size(BLK)
        self.left = list(range(self.blocks.bit_length() - 2, -1, -1))

    def step(self, *deps, gates=()):
        bit = self.order.pop(0)
        place = len(self.left) - 1 - self.left.index(bit)
        mine = scalar((self.position >> bit) & 1)
        keep, away, *rest = halve(
            mine, self.parts, self.blocks, 1 << place, self.columns, deps, gates
        )
        self.parts = [(keep, 0), (swap(away, BLK, 1 << bit), 0)]
        self.left.remove(bit)
        self.blocks //= 2
        return (away, *rest) if rest else away

    def last(self, *deps):
        while self.order:
            self.step(*deps)
        return halve(scalar(self.position), self.parts, 1, 1, self.columns, deps)[0]


def scalar(x):
    return x.reshape(1).astype(jnp.int32)


def total_kernel(one, two, out):
    out[...] = one[...] + two[...]


def butterfly_steps():
    blocks = lax.axis_size(BLK)
    return [(DP, 1)] + [(BLK, 1 << i) for i in range(blocks.bit_length() - 1)] + [(HEAD, 1)]


def butterfly_add(x, got, deps=()):
    whole = pl.BlockSpec(memory_space=pltpu.VMEM)
    return call(
        total_kernel,
        deps=deps,
        in_specs=[whole, whole],
        out_shape=[jax.ShapeDtypeStruct(x.shape, F32)],
        cost_estimate=cost(TAIL),
    )(x, got)[0]


def in_order(mine, first, second, axis):
    return jnp.where(
        mine == 0, jnp.concatenate([first, second], axis), jnp.concatenate([second, first], axis)
    )


def pick(x, index, axis=0):
    return lax.dynamic_index_in_dim(x, index, axis, keepdims=False)


def shards(
    tokens, doc_ids, w_qkv, w_out, slopes, w_up, w_down, w_comp, comp_bias,
    norm1_gain, norm1_bias, norm2_gain, norm2_bias, out_cot, recon_cot,
):
    seqs, rows, model = tokens.shape
    heads = slopes.shape[0]
    width = w_qkv.shape[2]
    hd = width // heads
    slots = rows // 3
    used = 3 * slots
    padded = -(-slots // 16) * 16
    memory = CSEGS * slots
    position = lax.axis_index(BLK)
    core = lax.axis_index(DP)
    me = lax.axis_index(HEAD)
    ot = 1 - me
    scaling = hd ** (-0.5)
    half = model // 2
    share = model // (lax.axis_size(BLK) * lax.axis_size(DP))
    bits = lax.axis_size(BLK).bit_length() - 1
    rising = list(range(bits))
    falling = [1, 0] + rising[2:]
    scalars = jnp.stack([core, me]).astype(jnp.int32)
    me_arg, ot_arg = me.reshape(1).astype(jnp.int32), ot.reshape(1).astype(jnp.int32)

    small = jnp.concatenate(
        [pick(recon_cot, ot), jnp.pad(slopes, (0, rows - heads)).reshape(1, rows)], 0
    )
    small_got = swap(small, HEAD)
    half_rows = model // 2
    qkv_part = lax.dynamic_slice_in_dim(w_qkv, core * half_rows, half_rows, 1)
    out_part = lax.dynamic_slice_in_dim(w_out, core * half_rows, half_rows, 1)
    far_part = jnp.concatenate([qkv_part, out_part[None]], 0)
    far_got = swap(far_part, HEAD)
    groups = (OWN, OTH)

    halo_raw = shift(pick(tokens, me), BLK, 1)
    normed, tri_own, tri_oth = front(
        me_arg, tokens, norm1_gain, norm1_bias, slots, padded, deps=(far_part, small)
    )
    packed = dot(tri_own, w_comp.reshape(3 * model, model)) + comp_bias
    packed = packed.astype(BF)
    lag2, lag3 = shift(packed, BLK, 2), shift(packed, BLK, 3)

    docs = pick(doc_ids, me)
    query_doc = lax.dynamic_slice_in_dim(docs, position * rows, rows, 0).reshape(1, rows)
    padded_doc = jnp.concatenate([jnp.full(((CSEGS + 1) * rows,), -1, jnp.int32), docs])
    window = lax.dynamic_slice_in_dim(padded_doc, position * rows, (CSEGS + 2) * rows, 0)
    window = jnp.broadcast_to(window[:, None], ((CSEGS + 2) * rows, 128))
    (far,) = far_log(
        position.reshape(1).astype(jnp.int32), window, query_doc, slots, deps=(packed,)
    )

    weights, outs = {OWN: w_qkv}, {OWN: w_out}
    cots = {OWN: pick(recon_cot, me).reshape(heads, 1, rows)}
    slope = {OWN: slopes}
    q, ko, vo, kc, vc, rec, kf, vf, att, lse = ({} for _ in range(10))
    q[OWN], ko[OWN], vo[OWN], kc[OWN], vc[OWN], lag2 = project(
        normed, packed, w_qkv, deps=(far,), gates=(lag2,)
    )
    lag4 = shift(lag2, BLK, 2)
    cots[OTH] = small_got[:heads].reshape(heads, 1, rows)
    slope[OTH] = small_got[heads, :heads]
    rec[OWN] = recon_both(
        q[OWN], ko[OWN], vo[OWN], kc[OWN], vc[OWN], cots[OWN], slots, scaling,
    )
    mem = jnp.zeros((rows, model), BF)
    for index, lag in enumerate((lag4, lag3, lag2)):
        place = (index * slots, rows - (index + 1) * slots)
        mem = mem + jnp.pad(lag[:slots], (place, (0, 0)))
    halo = norm_halo(halo_raw, norm1_gain, norm1_bias, deps=(rec[OWN][0],))[0]
    kf[OWN], vf[OWN], far_got = project_distant(halo, mem, w_qkv, gates=(far_got,))
    near_got = swap(far_got, DP)
    att[OWN], lse[OWN] = attend_forward(
        slope[OWN], q[OWN], kf[OWN], vf[OWN], ko[OWN], vo[OWN], far, scaling
    )
    weights[OTH] = in_order(core, far_got[:3], near_got[:3], 1)
    outs[OTH] = in_order(core, far_got[3], near_got[3], 1)
    q[OTH], ko[OTH], vo[OTH], kc[OTH], vc[OTH] = project(
        normed, packed, weights[OTH], deps=(att[OWN],)
    )
    kf[OTH], vf[OTH] = project_distant(halo, mem, weights[OTH], deps=(q[OTH],))
    att[OTH], lse[OTH] = attend_forward(
        slope[OTH], q[OTH], kf[OTH], vf[OTH], ko[OTH], vo[OTH], far, scaling
    )

    middle, n2_own = middle_norm(
        me_arg, tokens, att[OWN], att[OTH], w_out, outs[OTH], norm2_gain, norm2_bias
    )
    n2_oth = swap(n2_own, HEAD)
    rec[OTH] = recon_both(
        q[OTH], ko[OTH], vo[OTH], kc[OTH], vc[OTH], cots[OTH], slots, scaling,
        deps=(n2_own,),
    )
    hid_own, din_own, dn_own = mlp(
        me_arg, n2_own, out_cot, w_up, w_down, BF, deps=(rec[OTH][0],)
    )
    hid_oth, din_oth, dn_oth = mlp(
        ot_arg, n2_oth, out_cot, w_up, w_down, BF, deps=(dn_own,)
    )
    dn_got = swap(dn_oth, HEAD)
    units = w_up.shape[1]
    up_down, token = weight_grads(
        scalars,
        [
            [(n2_own, 0, din_own, (0, 0), units), (n2_oth, 0, din_oth, (0, 0), units)],
            [(out_cot, 0, hid_own, (0, 0), units), (out_cot, 1, hid_oth, (0, 0), units)],
        ],
        0, model, 27.7, deps=(dn_oth,),
    )
    ffn_own, ffn_oth = branches(hid_own, hid_oth, w_down, deps=(token,))
    up_down = lax.psum_scatter(up_down, (BLK, DP), scatter_dimension=0, tiled=True)
    (
        dbranch, datt_own, datt_oth, row_own, row_oth, sums2,
        ffn_oth, recon_oth,
    ) = turn(
        me_arg, dn_own, dn_got, middle, out_cot, att[OWN], att[OTH], w_out, outs[OTH],
        norm2_gain, heads, gates=(ffn_oth, rec[OTH][0]),
    )
    ffn_got = swap(ffn_oth, HEAD)
    recon_got = swap(recon_oth.reshape(heads, rows), HEAD)
    datt = {OWN: datt_own, OTH: datt_oth}
    row = {OWN: row_own, OTH: row_oth}
    back, near, grads = {}, {}, {}

    def far_back(g, *deps):
        back[g] = attend_backward(
            slope[g], q[g], datt[g], lse[g], row[g], far, kf[g], vf[g], False, [], scaling,
            deps=deps, late=g == OWN,
        )

    def near_back(g, *deps, gates=()):
        r = rec[g]
        near[g] = attend_backward(
            slope[g], q[g], datt[g], lse[g], row[g], far, ko[g], vo[g], True,
            [back[g][0], r[1], r[2], r[3]], scaling, deps=deps, gates=gates, late=g == OWN,
        )

    def group_grads(g, *deps, gates=()):
        r = rec[g]
        sections = [[(normed, 0, near[g][0], (0, 0), width)]]
        for i in (1, 2):
            sections.append(
                [
                    (normed, 0, near[g][i], (0, 0), width),
                    (packed, 0, r[3 + i], (0, 0), width),
                    (halo, 0, back[g][i], (0, 0), width),
                    (mem, 0, back[g][i], (0, rows), width),
                ]
            )
        sections.append([(dbranch, 0, att[g], (0, 0), width)])
        grads[g] = weight_grads(
            scalars, sections, share, model, 26.4, deps=deps, gates=gates
        )

    far_back(OTH, dbranch)
    near_back(OTH)
    group_grads(OTH)
    cross = trade(grads[OTH][0])
    far_back(OWN, grads[OTH][1])
    (lo_own,) = add((middle, ffn_own, ffn_got), 1, deps=(back[OWN][3],))
    (cross,) = add((cross,), 1, deps=(lo_own,))
    cross_got = swap(cross, HEAD)
    halo_part, back4, back3, back2 = spread(
        back[OTH][1], back[OTH][2], back[OWN][1], back[OWN][2], weights[OTH], w_qkv,
        slots, padded, deps=(cross,),
    )
    slot_gots = [
        shift(part, BLK, -lag)
        for part, lag in zip((back4, back3, back2), range(CSEGS + 1, 1, -1))
    ]
    near_back(OWN, halo_part)
    group_grads(OWN)
    own = trade(grads[OWN][0])
    base_oth = base_rows(
        near[OTH][:3], rec[OTH][4:6], weights[OTH], [], deps=(grads[OWN][1],)
    )
    base, slot_base = base_rows(near[OWN][:3], rec[OWN][4:6], w_qkv, base_oth)
    wide = 2 * width
    late = Halving([(own, 0, 0), (own, 0, 1), (cross_got, 0)], 2 * wide, rising, position)
    moved = late.step(base)
    dpacked, dp_mine, dp_away, bias_sum, halo_part, lo_own = packed_back(
        me_arg, slot_base, slot_gots, deps=(moved,), gates=(halo_part, lo_own)
    )
    dp_got = swap(dp_away, HEAD)
    halo_back = shift(halo_part, BLK, -1)
    lo_got = swap(lo_own, HEAD)
    send, token = weight_grads(
        scalars,
        [
            [
                (tri_own, tap * model, dp_mine, (0, 0), half),
                (tri_oth, tap * model, dp_got, (0, 0), half),
            ]
            for tap in range(3)
        ],
        share, model, 19.1,
    )
    comp = trade(send)
    comp = Halving([(comp, 0, 0), (comp, 0, 1)], 3 * half, falling, position)
    moved = comp.step(token)
    moved = late.step(moved)
    grad_own, sums1 = finish(
        me_arg, base, halo_back, dpacked, w_comp, tokens, dbranch, norm1_gain,
        deps=(recon_got, moved),
    )
    dslopes = {}
    for g in groups:
        total = back[g][3] + near[g][3]
        dslopes[g] = -jnp.sum(total[:, 2] - total[:, 0] * total[:, 1], axis=1)
    both = in_order(me, dslopes[OWN], dslopes[OTH], 0)
    vector = jnp.concatenate(
        [sums1[0], sums1[1], sums2[0], sums2[1], bias_sum[0], jnp.pad(both, (0, 128 - 2 * heads))]
    ).reshape(-1, 128)
    rounds = butterfly_steps()
    vector_got = swap(vector, *rounds.pop(0))
    moved, grad_away = comp.step(sums1, gates=(grad_own,))
    grad_got = swap(grad_away, HEAD)
    vector = butterfly_add(vector, vector_got, deps=(moved,))
    vector_got = swap(vector, *rounds.pop(0))
    moved = vector
    while late.order or comp.order:
        if late.order:
            moved = late.step(moved)
        if comp.order:
            moved = comp.step(moved)
        vector = butterfly_add(vector, vector_got, deps=(moved,))
        vector_got = swap(vector, *rounds.pop(0))
        moved = vector
    up_sum, down_sum = up_down[:, :units].astype(F32), up_down[:, units:].astype(F32).T
    vector = butterfly_add(vector, vector_got, deps=(moved, up_sum, down_sum))
    vector_got = swap(vector, *rounds.pop(0))
    late = late.last(vector)
    while len(rounds) > 1:
        vector = butterfly_add(vector, vector_got, deps=(late,))
        vector_got = swap(vector, *rounds.pop(0))
    if rounds:
        vector = butterfly_add(vector, vector_got, deps=(late,))
        vector_got = swap(vector, *rounds.pop(0))
    grad_tokens = in_order(me, grad_own[None], grad_got[None], 0)
    comp = comp.last(vector, grad_tokens)
    vector = (vector + vector_got).reshape(-1)
    comp = comp.astype(BF)
    comp_got = swap(comp, HEAD)
    comp_all = in_order(
        me, comp.reshape(share, 3, half), comp_got.reshape(share, 3, half), 2
    ).astype(F32)

    slope_sum = lax.dynamic_slice_in_dim(vector, 5 * model + me * heads, heads, 0)

    recon_own = rec[OWN][0].reshape(heads, rows)
    recon = in_order(me, recon_own[None], recon_got[None], 0)
    layer_out = in_order(me, lo_own[None], lo_got[None], 0)
    return (
        layer_out,
        recon,
        grad_tokens,
        jnp.transpose(late[:, : 3 * width].reshape(share, 3, width), (1, 0, 2)),
        late[:, 3 * width :].T,
        slope_sum,
        up_sum,
        down_sum,
        jnp.transpose(comp_all, (1, 0, 2)),
        vector[4 * model : 5 * model],
        vector[:model],
        vector[model : 2 * model],
        vector[2 * model : 3 * model],
        vector[3 * model : 4 * model],
    )


def solution(mesh):
    in_specs = (
        P(DP, BLK, None),
        P(DP, None),
        P(None, None, HEAD),
        P(HEAD, None),
        P(HEAD),
        P(None, HEAD),
        P(HEAD, None),
        P(),
        P(),
        P(),
        P(),
        P(),
        P(),
        P(DP, BLK, None),
        P(DP, HEAD, BLK),
    )
    out_specs = (
        P(DP, BLK, None),
        P(DP, HEAD, BLK),
        P(DP, BLK, None),
        P(None, (BLK, DP), HEAD),
        P(HEAD, (BLK, DP)),
        P(HEAD),
        P((BLK, DP), HEAD),
        P(HEAD, (BLK, DP)),
        P(None, (BLK, DP), None),
        P(),
        P(),
        P(),
        P(),
        P(),
    )
    return jax.shard_map(shards, mesh=mesh, in_specs=in_specs, out_specs=out_specs, check_vma=False)
```
